32 devices in a mesh: groups: 2 (over y), dp: 4 (over z), tensor: 2 (over x), sub: 2 (over core).
Axes of the slice: x: 2, y: 2, z: 4, core: 2. Of those that a mesh axis runs over, the one named last changes fastest.
Arguments:
- tokens: bfloat16 [16384, 4096], P(('groups', 'dp', 'sub'), 'tensor'), parts along dimension 0, may hold values from -6 to 6
- frozen_weight: bfloat16 [4096, 4096], P('tensor', 'sub'), may hold values from -0.09375 to 0.09375
- cotangent: bfloat16 [16384, 4096], P(('groups', 'dp', 'sub'), 'tensor'), parts along dimension 0, may hold values from -6 to 6
- down_adapters: float32 [24, 4096, 64], P(('groups', 'dp'), ('tensor', 'sub')), parts along dimension 0, may hold values from -0.09375 to 0.09375
- up_adapters: float32 [24, 4096, 64], P(('groups', 'dp'), ('tensor', 'sub')), parts along dimension 0, may hold values from -0.75 to 0.75
- down_first_moment: float32 [24, 4096, 64], P(('groups', 'dp'), ('tensor', 'sub')), parts along dimension 0, may hold values from -30 to 30
- up_first_moment: float32 [24, 4096, 64], P(('groups', 'dp'), ('tensor', 'sub')), parts along dimension 0, may hold values from -30 to 30
- down_second_moment: float32 [24, 4096, 64], P(('groups', 'dp'), ('tensor', 'sub')), parts along dimension 0, may hold values from 0.01 to 1
- up_second_moment: float32 [24, 4096, 64], P(('groups', 'dp'), ('tensor', 'sub')), parts along dimension 0, may hold values from 0.01 to 1
- optimizer_steps: int32 [24], P(('groups', 'dp')), parts along dimension 0, may hold values from 1 to 199
- slot_of_tenant: int32 [24], P('groups'), parts along dimension 0, may hold values from 0 to 11, as said below
- tenant_of_block: int32 [128], P('groups'), parts along dimension 0, may hold values from 0 to 11, as said below
Outputs:
- projected: bfloat16 [16384, 4096], P(('groups', 'dp', 'sub'), 'tensor'), parts along dimension 0
- new_lora_a: float32 [24, 4096, 64], P(('groups', 'dp'), ('tensor', 'sub')), parts along dimension 0
- new_lora_b: float32 [24, 4096, 64], P(('groups', 'dp'), ('tensor', 'sub')), parts along dimension 0
- fresh_down_first: float32 [24, 4096, 64], P(('groups', 'dp'), ('tensor', 'sub')), parts along dimension 0
- fresh_up_first: float32 [24, 4096, 64], P(('groups', 'dp'), ('tensor', 'sub')), parts along dimension 0
- fresh_down_second: float32 [24, 4096, 64], P(('groups', 'dp'), ('tensor', 'sub')), parts along dimension 0
- fresh_up_second: float32 [24, 4096, 64], P(('groups', 'dp'), ('tensor', 'sub')), parts along dimension 0
The draws below stay inside these ranges and needn't reach their ends.
There are 2 independent parts, one for each index of `groups`. The reference program is written for one: setup_inputs(seed, part) draws one part's arguments, and reference() takes and returns one part's arrays. A program takes and returns all parts, laid end to end along the dimension named above; an argument that names none is the same for every part. Nothing has to cross between parts.
Inputs may be any that keep to these rules, and one draw needn't show every extreme that they name: `slot_of_tenant`: a permutation of 0 to 11. `tenant_of_block`: among the 8 blocks of one device (aligned blocks of the list), all blocks whose tenants have slots of one owner (slot // 3) have the same tenant.
All inputs are finite; a program needn't handle non-finite values.
Results may differ from the reference program's by a relative error of at most 0.0058.
Values may be sent and summed in bfloat16 or wider, within the bound.
No kernel may reach another device: no remote copies, remote signals or barrier semaphores. Data moves between devices by JAX's collectives and lax.ppermute only.
A program may use at most 192 MiB of HBM per device.

```python
import math
import jax
import jax.numpy as jnp

INPUT_FEATURES = 4096
OUTPUT_FEATURES = 4096
ADAPTER_RANK = 64
BLK_ROWS = 128
BLK_DEV = 8
TEN_DEV = 3
TENANT_COUNT = 12
BLOCKS = 64
TOKENS = 8192
N_DP = 4


def shared_slots(key):
    return jax.random.permutation(jax.random.fold_in(key, 11), TENANT_COUNT).astype(jnp.int32)


def draw_slot_of_tenant(key, part):
    return shared_slots(key)


def draw_tenant_of_block(key, part):
    slots = shared_slots(key)
    key = jax.random.fold_in(key, 5)
    key_owner, key_local = jax.random.split(key)
    device_count = BLOCKS // BLK_DEV
    owner_pick = jax.random.randint(key_owner, (device_count, BLK_DEV), 0, N_DP)
    local_pick = jax.random.randint(key_local, (device_count, N_DP), 0, TEN_DEV)
    chosen = jnp.take_along_axis(local_pick, owner_pick, axis=1)
    slot_pick = owner_pick * TEN_DEV + chosen
    tenant_of_slot = jnp.argsort(slots).astype(jnp.int32)
    return jnp.take(tenant_of_slot, slot_pick.reshape(BLOCKS)).astype(jnp.int32)


def with_ends(drawn, rng, smallest, top_value):
    place = [jax.random.randint(jax.random.fold_in(rng, axis), (), 0, length) for axis, length in enumerate(drawn.shape)]
    widest = drawn.shape.index(max(drawn.shape))
    neighbour = place[:widest] + [(place[widest] + 1) % drawn.shape[widest]] + place[widest + 1:]
    return drawn.at[tuple(place)].set(smallest).at[tuple(neighbour)].set(top_value)


def block_levels(key, shape, cuts, smallest, high):
    def one(axis_at, shards_of):
        draws = jax.random.uniform(jax.random.fold_in(jax.random.fold_in(key, 6), axis_at), (shards_of,), jnp.float32, smallest / len(cuts), high / len(cuts))
        return jnp.repeat(jnp.exp(draws), shape[axis_at] // shards_of).reshape((-1,) + (1,) * (len(shape) - axis_at - 1))

    loudness = one(*cuts[0])
    for cut in cuts[1:]:
        loudness = loudness * one(*cut)
    return loudness


def noise(key, extent, spread, limit, shards=(), held_as=jnp.bfloat16):
    entries = jax.random.normal(key, extent, jnp.float32) * spread
    if len(shards) > 0:
        entries = block_levels(key, extent, shards, -0.22, 0.18) * entries
    return jnp.clip(entries, min=-limit, max=limit).astype(held_as)


def setup_inputs(seed: int = 0, part: int = 0) -> dict:
    arg_keys = jax.random.split(jax.random.key(seed), 13)
    part_splits = jax.random.split(jax.random.fold_in(arg_keys[12], part), 13)
    tokens = noise(part_splits[0], (TOKENS, INPUT_FEATURES), 1.0, 6.0, ((0, 8), (1, 2)))
    frozen_weight = noise(arg_keys[1], (INPUT_FEATURES, OUTPUT_FEATURES), INPUT_FEATURES ** -0.5, 0.09375, ((0, 2), (1, 2)))
    cotangent = noise(part_splits[2], (TOKENS, OUTPUT_FEATURES), 1.0, 6.0, ((0, 8), (1, 2)))
    down_adapters = noise(part_splits[3], (TENANT_COUNT, INPUT_FEATURES, ADAPTER_RANK), INPUT_FEATURES ** -0.5, 0.09375, ((0, 4), (1, 4)), jnp.float32)
    up_adapters = noise(part_splits[4], (TENANT_COUNT, OUTPUT_FEATURES, ADAPTER_RANK), ADAPTER_RANK ** -0.5, 0.75, ((0, 4), (1, 4)), jnp.float32)
    down_first_moment = noise(part_splits[5], (TENANT_COUNT, INPUT_FEATURES, ADAPTER_RANK), 5.0, 30.0, ((0, 4), (1, 4)), jnp.float32)
    up_first_moment = noise(part_splits[6], (TENANT_COUNT, OUTPUT_FEATURES, ADAPTER_RANK), 5.0, 30.0, ((0, 4), (1, 4)), jnp.float32)
    down_second_moment = jnp.clip(jnp.exp(math.log(1.0) - 4.6051702 * jax.random.uniform(part_splits[7], (TENANT_COUNT, INPUT_FEATURES, ADAPTER_RANK), jnp.float32) ** block_levels(part_splits[7], (TENANT_COUNT, INPUT_FEATURES, ADAPTER_RANK), ((0, 4), (1, 4)), -0.2, 0.2)), 0.01, 1.0)
    up_second_moment = jnp.clip(jnp.exp(math.log(1.0) - 4.6051702 * jax.random.uniform(part_splits[8], (TENANT_COUNT, OUTPUT_FEATURES, ADAPTER_RANK), jnp.float32) ** block_levels(part_splits[8], (TENANT_COUNT, OUTPUT_FEATURES, ADAPTER_RANK), ((0, 4), (1, 4)), -0.2, 0.2)), 0.01, 1.0)
    optimizer_steps = with_ends(jax.random.randint(part_splits[9], (TENANT_COUNT,), 1, 200), jax.random.fold_in(part_splits[9], 1), 1, 199).astype(jnp.int32)
    slot_of_tenant = draw_slot_of_tenant(jax.random.fold_in(jax.random.fold_in(arg_keys[12], part), 71), part)
    tenant_of_block = draw_tenant_of_block(jax.random.fold_in(jax.random.fold_in(arg_keys[12], part), 71), part)
    return dict(tokens=tokens, frozen_weight=frozen_weight, cotangent=cotangent, down_adapters=down_adapters, up_adapters=up_adapters, down_first_moment=down_first_moment, up_first_moment=up_first_moment, down_second_moment=down_second_moment, up_second_moment=up_second_moment, optimizer_steps=optimizer_steps, slot_of_tenant=slot_of_tenant, tenant_of_block=tenant_of_block)


ADAPTER_SCALE = 2.0
BETA_ONE = 0.9
BETA_TWO = 0.999
LEARN_RATE = 0.01
ADAM_EPS = 1e-08

def moment_update(param, first, second, grad, count, used_slots):
    steps = (count + 1).astype(jnp.float32)[:, None, None]
    first_new = BETA_ONE * first + (1.0 - BETA_ONE) * grad
    second_new = BETA_TWO * second + (1.0 - BETA_TWO) * grad * grad
    corr_one = 1.0 - jnp.power(jnp.float32(BETA_ONE), steps)
    corr_two = 1.0 - jnp.power(jnp.float32(BETA_TWO), steps)
    update = LEARN_RATE * (first_new / corr_one) / (jnp.sqrt(second_new / corr_two) + ADAM_EPS)
    keep = used_slots[:, None, None]
    return (jnp.where(keep, param - update, param), jnp.where(keep, first_new, first), jnp.where(keep, second_new, second))

def reference(tokens, frozen_weight, cotangent, down_adapters, up_adapters, down_first_moment, up_first_moment, down_second_moment, up_second_moment, optimizer_steps, slot_of_tenant, tenant_of_block):
    slot_of_block = jnp.take(slot_of_tenant, tenant_of_block).astype(jnp.int32)
    down_adapter = jnp.take(down_adapters.astype(jnp.bfloat16), slot_of_block, axis=0).astype(jnp.float32)
    up_adapter = jnp.take(up_adapters.astype(jnp.bfloat16), slot_of_block, axis=0).astype(jnp.float32)
    token_blocks = tokens.reshape(BLOCKS, BLK_ROWS, INPUT_FEATURES).astype(jnp.float32)
    gradient_blocks = cotangent.reshape(BLOCKS, BLK_ROWS, OUTPUT_FEATURES).astype(jnp.float32)
    down_projection = jnp.einsum('bnk,bkr->bnr', token_blocks, down_adapter).astype(jnp.bfloat16).astype(jnp.float32)
    base = jnp.dot(tokens, frozen_weight, preferred_element_type=jnp.float32)
    upper_bound = ADAPTER_SCALE * jnp.einsum('upq,ufq->upf', down_projection, up_adapter)
    projected = (base + upper_bound.reshape(TOKENS, OUTPUT_FEATURES)).astype(jnp.bfloat16)
    backward_pass = (ADAPTER_SCALE * jnp.einsum('psj,pjg->psg', gradient_blocks, up_adapter)).astype(jnp.bfloat16).astype(jnp.float32)
    up_gradient_blocks = ADAPTER_SCALE * jnp.einsum('jtm,jtz->jmz', gradient_blocks, down_projection)
    grad_a_blocks = jnp.einsum('bnk,bnr->bkr', token_blocks, backward_pass)
    down_gradient = jax.ops.segment_sum(grad_a_blocks, slot_of_block, num_segments=TENANT_COUNT)
    up_gradient = jax.ops.segment_sum(up_gradient_blocks, slot_of_block, num_segments=TENANT_COUNT)
    used_slots = jax.ops.segment_sum(jnp.ones((BLOCKS,), jnp.int32), slot_of_block, num_segments=TENANT_COUNT) > 0
    fresh_down, fresh_down_first, fresh_down_second = moment_update(down_adapters, down_first_moment, down_second_moment, down_gradient, optimizer_steps, used_slots)
    fresh_up, fresh_up_first, fresh_up_second = moment_update(up_adapters, up_first_moment, up_second_moment, up_gradient, optimizer_steps, used_slots)
    return (projected, fresh_down, fresh_up, fresh_down_first, fresh_up_first, fresh_down_second, fresh_up_second)
```

```python
import jax
import jax.numpy as jnp
from jax import lax
from jax.sharding import PartitionSpec as P

BLK_ROWS = 128


ADAPTER_SCALE = 2.0
BETA_ONE = 0.9
BETA_TWO = 0.999
LEARN_RATE = 0.01
ADAM_EPS = 1e-08


def moment_update(param, first, second, grad, corr_one, corr_two, used_slots):
    first_new = BETA_ONE * first + (1.0 - BETA_ONE) * grad
    second_new = BETA_TWO * second + (1.0 - BETA_TWO) * grad * grad
    update = LEARN_RATE * (first_new / corr_one) / (jnp.sqrt(second_new / corr_two) + ADAM_EPS)
    keep = used_slots[:, None, None]
    return (
        jnp.where(keep, param - update, param),
        jnp.where(keep, first_new, first),
        jnp.where(keep, second_new, second),
    )


def rotate(value, axis, shift):
    size = lax.axis_size(axis)
    return lax.ppermute(value, axis, [(i, (i + shift) % size) for i in range(size)])


def swap_cores(value):
    return rotate(value, "sub", 1)


def contract(left, right, left_dim, right_dim):
    return lax.dot_general(
        left, right, (((left_dim,), (right_dim,)), ((), ())), preferred_element_type=jnp.float32
    )


def sum_tensor(part):
    total = part
    for shift in range(1, lax.axis_size("tensor")):
        total = total + rotate(part, "tensor", shift)
    return total


def after(value, *deps):
    return lax.optimization_barrier((value,) + deps)[0]


def pick(weights, stacked):
    out = jnp.zeros_like(stacked[0])
    for k in range(stacked.shape[0]):
        out = jnp.where(weights[k], stacked[k], out)
    return out


def on_device(
    tokens,
    frozen_weight,
    cotangent,
    down_adapters,
    up_adapters,
    down_first_moment,
    up_first_moment,
    down_second_moment,
    up_second_moment,
    optimizer_steps,
    slot_of_tenant,
    tenant_of_block,
):
    row_count, din_local = tokens.shape
    dout_local = cotangent.shape[1]
    block_count = row_count // BLK_ROWS
    owners = lax.axis_size("dp")
    cores = lax.axis_size("sub")
    columns = lax.axis_size("tensor")
    z = lax.axis_index("dp")
    s = lax.axis_index("sub")
    x = lax.axis_index("tensor")
    slots, half, rank = down_adapters.shape
    flip = lambda v: jnp.swapaxes(v, 1, 2)
    down_adapters, up_adapters = flip(down_adapters), flip(up_adapters)
    down_first_moment, up_first_moment = flip(down_first_moment), flip(up_first_moment)
    down_second_moment, up_second_moment = flip(down_second_moment), flip(up_second_moment)

    tenants = slot_of_tenant.shape[0]
    hit = tenant_of_block[:, None] == jnp.arange(tenants, dtype=jnp.int32)[None, :]
    slot_table = jnp.sum(jnp.where(hit, slot_of_tenant[None, :], 0), axis=1)
    slot_table = slot_table.reshape(owners, cores, block_count)
    local_ids = z * slots + jnp.arange(slots, dtype=jnp.int32)
    selection = jnp.any(slot_table[:, :, :, None] == local_ids, axis=2)
    used_slots = jnp.any(selection, axis=(0, 1))
    shifted = jnp.roll(selection, -z, axis=0)
    my_slots = lax.dynamic_slice(slot_table, (z, s, 0), (1, 1, block_count))[0, 0]
    my_shift = lax.rem(z - my_slots // slots + owners, owners)
    row_shift = jnp.repeat(my_shift, BLK_ROWS, total_repeat_length=row_count)
    row_mask = row_shift[None, :] == jnp.arange(owners, dtype=jnp.int32)[:, None]

    def outbound(adapters):
        narrow = adapters.astype(jnp.bfloat16)
        return [
            jnp.stack([pick(shifted[d, c], narrow) for c in range(cores)]) for d in range(owners)
        ]

    def inbound(messages):
        got = [rotate(message, "dp", d) if d else message for d, message in enumerate(messages)]
        kept = jnp.stack([lax.dynamic_index_in_dim(g, s, 0, False) for g in got])
        sent = jnp.stack([lax.dynamic_index_in_dim(g, 1 - s, 0, False) for g in got])
        other = swap_cores(sent)
        first = jnp.where(s == 0, kept, other)
        second = jnp.where(s == 0, other, kept)
        return jnp.concatenate([first, second], axis=2).reshape(owners * rank, cores * half)

    def chosen(product):
        grouped = product.reshape(owners, rank, row_count)
        return jnp.sum(jnp.where(row_mask[:, None, :], grouped, 0.0), axis=0)

    def spread(value):
        return jnp.where(row_mask[:, None, :], value[None], jnp.zeros_like(value)[None]).reshape(
            owners * rank, row_count
        )

    def give_back(product, send_type):
        grouped = product.astype(send_type).reshape(owners, rank, cores * half)
        first, second = grouped[:, :, :half], grouped[:, :, half:]
        mine = jnp.where(s == 0, first, second)
        theirs = swap_cores(jnp.where(s == 0, second, first))
        total = 0.0
        for d in range(owners):
            message = jnp.stack([mine[d], theirs[d]])
            if d:
                message = rotate(message, "dp", -d)
            for c in range(cores):
                source_core = s if c == 0 else 1 - s
                weights = lax.dynamic_index_in_dim(shifted[d], source_core, 0, False)
                total = total + jnp.where(
                    weights[:, None, None], message[c].astype(jnp.float32)[None], 0.0
                )
        return total

    per_half = columns // cores
    weight_other = swap_cores(frozen_weight)

    def weight_piece(weight, target):
        return lax.dynamic_slice_in_dim(weight, lax.rem(target, per_half) * dout_local, dout_local, 1)

    def shares(weight):
        return [
            jnp.dot(
                tokens,
                weight_piece(weight, lax.rem(x + shift, columns)),
                preferred_element_type=jnp.float32,
            ).astype(jnp.bfloat16)
            for shift in range(1, columns)
        ]

    def send_stage(products, own):
        got = []
        for shift, share in zip(range(1, columns), products):
            pairs = []
            for t in range(columns):
                for c in range(cores):
                    target = (t + shift) % columns
                    if (target // per_half == c) == own:
                        pairs.append((t * cores + c, target * cores + c))
            got.append(lax.ppermute(share, ("tensor", "sub"), pairs))
        return got

    mine_is_own = (x // per_half) == s
    down_msgs = outbound(down_adapters)
    up_msgs = outbound(up_adapters)
    share_one = shares(after(frozen_weight, *down_msgs, *up_msgs))
    stage_one = send_stage(share_one, True)

    down_cat = inbound(down_msgs)
    down_part = chosen(contract(after(down_cat, *share_one), tokens, 1, 1))
    down_sum = sum_tensor(down_part)
    share_two = shares(after(weight_other, down_part))
    stage_two = send_stage(share_two, False)
    down_wide = spread(after(down_sum, *share_two).astype(jnp.bfloat16))
    up_product = ADAPTER_SCALE * contract(down_wide, cotangent, 1, 0)
    up_cat = inbound(up_msgs)
    back_part = chosen(contract(after(up_cat, up_product), cotangent, 1, 1))
    back_sum = sum_tensor(back_part)
    back_wide = spread((ADAPTER_SCALE * back_sum).astype(jnp.bfloat16))
    down_product = contract(back_wide, tokens, 1, 0)
    up_gradient = give_back(up_product, jnp.bfloat16)
    down_gradient = give_back(down_product, jnp.float32)
    frozen_weight = after(frozen_weight, down_product)

    local_weight = jnp.where(
        mine_is_own, weight_piece(frozen_weight, x), weight_piece(weight_other, x)
    )
    local = jnp.dot(tokens, local_weight, preferred_element_type=jnp.float32)
    local = local + ADAPTER_SCALE * contract(down_wide, up_cat, 0, 0)
    for early, late in zip(stage_one, stage_two):
        local = local + jnp.where(mine_is_own, early, late).astype(jnp.float32)
    projected = local.astype(jnp.bfloat16)

    steps = (optimizer_steps + 1).astype(jnp.float32)[:, None, None]
    corr_one = 1.0 - jnp.power(jnp.float32(BETA_ONE), steps)
    corr_two = 1.0 - jnp.power(jnp.float32(BETA_TWO), steps)
    fresh_down, fresh_down_first, fresh_down_second = moment_update(
        down_adapters,
        down_first_moment,
        down_second_moment,
        down_gradient,
        corr_one,
        corr_two,
        used_slots,
    )
    fresh_up, fresh_up_first, fresh_up_second = moment_update(
        up_adapters,
        up_first_moment,
        up_second_moment,
        up_gradient,
        corr_one,
        corr_two,
        used_slots,
    )
    return (
        projected,
        flip(fresh_down),
        flip(fresh_up),
        flip(fresh_down_first),
        flip(fresh_up_first),
        flip(fresh_down_second),
        flip(fresh_up_second),
    )


def solution(mesh):
    placed = (
        P(("groups", "dp", "sub"), "tensor"),
        P("tensor", "sub"),
        P(("groups", "dp", "sub"), "tensor"),
        P(("groups", "dp"), ("tensor", "sub"), None),
        P(("groups", "dp"), ("tensor", "sub"), None),
        P(("groups", "dp"), ("tensor", "sub"), None),
        P(("groups", "dp"), ("tensor", "sub"), None),
        P(("groups", "dp"), ("tensor", "sub"), None),
        P(("groups", "dp"), ("tensor", "sub"), None),
        P(("groups", "dp")),
        P("groups"),
        P("groups"),
    )
    return jax.shard_map(
        on_device,
        mesh=mesh,
        in_specs=placed,
        out_specs=(
            P(("groups", "dp", "sub"), "tensor"),
            P(("groups", "dp"), ("tensor", "sub"), None),
            P(("groups", "dp"), ("tensor", "sub"), None),
            P(("groups", "dp"), ("tensor", "sub"), None),
            P(("groups", "dp"), ("tensor", "sub"), None),
            P(("groups", "dp"), ("tensor", "sub"), None),
            P(("groups", "dp"), ("tensor", "sub"), None),
        ),
        check_vma=False,
    )
```

```python
import functools

import jax
import jax.numpy as jnp
from jax import lax
from jax.experimental import pallas as pl
from jax.experimental.pallas import tpu as pltpu
from jax.sharding import PartitionSpec as P

BLK_ROWS = 128


ADAPTER_SCALE = 2.0
BETA_ONE = 0.9
BETA_TWO = 0.999
LEARN_RATE = 0.01
ADAM_EPS = 1e-08

SMEM = pl.BlockSpec(memory_space=pltpu.SMEM)
VMEM_BYTES = 44 * 1024 * 1024


def params():
    return pltpu.CompilerParams(vmem_limit_bytes=VMEM_BYTES)


def cost(flops, nbytes):
    return pl.CostEstimate(flops=flops, bytes_accessed=nbytes, transcendentals=0)


def rotate(value, axis, shift):
    size = lax.axis_size(axis)
    return lax.ppermute(value, axis, [(i, (i + shift) % size) for i in range(size)])


def after(value, *deps):
    return lax.optimization_barrier((value,) + deps)[0]


def dims(value):
    return jax.ShapeDtypeStruct(value.shape, value.dtype)


def tables_kernel(owners, cores, slots, block_count, place, slot_of, tenant_of, pick, shift, used):
    z, s = place[0], place[1]
    for k in range(slots):
        used[k] = 0

    def slot_at(device, b):
        return slot_of[tenant_of[device * block_count + b]]

    def per_device(i, carry):
        c, d = lax.div(i, owners), lax.rem(i, owners)
        device = lax.rem(z + d, owners) * cores + lax.rem(s + c, cores)

        def per_block(b, found):
            local = slot_at(device, b) - z * slots
            mine = jnp.logical_and(local >= 0, local < slots)

            @pl.when(mine)
            def _():
                used[local] = 1

            return jnp.where(mine, local, found)

        pick[i] = lax.fori_loop(0, block_count, per_block, 0)
        return carry

    lax.fori_loop(0, owners * cores, per_device, 0)
    for b in range(block_count):
        owner = lax.div(slot_at(z * cores + s, b), slots)
        shift[b] = lax.rem(z - owner + owners, owners)


def pack_kernel(owners, place, pick, own, other, *outs):
    s = place[1]
    half = own.shape[2]
    for d in range(owners):
        k = pick[d]
        near, far = own[k].astype(jnp.bfloat16), other[k].astype(jnp.bfloat16)
        outs[d][:, :half] = jnp.where(s == 0, near, far)
        outs[d][:, half:] = jnp.where(s == 0, far, near)


def product_kernel(owners, rank, tile_rows, shift, *refs):
    parts, rows, out, cat = refs[:owners], refs[owners], refs[owners + 1], refs[owners + 2]
    step = pl.program_id(0)

    @pl.when(step == 0)
    def _():
        for d in range(owners):
            cat[d * rank : (d + 1) * rank, :] = parts[d][...]

    full = lax.dot_general(
        cat[...], rows[...], (((1,), (1,)), ((), ())), preferred_element_type=jnp.float32
    )
    for b in range(tile_rows // BLK_ROWS):
        owner_shift = shift[step * (tile_rows // BLK_ROWS) + b]
        columns = slice(b * BLK_ROWS, (b + 1) * BLK_ROWS)
        value = full[:rank, columns]
        for d in range(1, owners):
            value = jnp.where(owner_shift == d, full[d * rank : (d + 1) * rank, columns], value)
        out[:, columns] = value


def adapter_product(shift, parts, rows, dep):
    owners, (rank, features), row_count = len(parts), parts[0].shape, rows.shape[0]
    tile = min(256, row_count)
    whole = pl.BlockSpec((rank, features), lambda i: (0, 0))
    parts = after(tuple(parts), dep)
    return pl.pallas_call(
        functools.partial(product_kernel, owners, rank, tile),
        grid=(row_count // tile,),
        in_specs=[SMEM] + [whole] * owners + [pl.BlockSpec((tile, features), lambda i: (i, 0))],
        out_specs=pl.BlockSpec((rank, tile), lambda i: (0, i)),
        out_shape=jax.ShapeDtypeStruct((rank, row_count), jnp.float32),
        scratch_shapes=[pltpu.VMEM((owners * rank, features), jnp.bfloat16)],
        compiler_params=params(),
        cost_estimate=cost(2 * owners * rank * features * row_count, 2 * row_count * features),
        name="adapter_product",
    )(shift, *parts, rows)


def outer_kernel(owners, rank, terms, scale_in, scale_out, place, shift, *refs):
    sums, rows, theirs, wide = refs[:terms], refs[terms], refs[terms + 1], refs[terms + 2]

    @pl.when(pl.program_id(0) == 0)
    def _():
        total = sums[0][...]
        for t in range(1, terms):
            total = total + sums[t][...]
        value = (scale_in * total).astype(jnp.bfloat16)
        for b in range(value.shape[1] // BLK_ROWS):
            columns = slice(b * BLK_ROWS, (b + 1) * BLK_ROWS)
            for d in range(owners):
                kept = jnp.where(shift[b] == d, value[:, columns], jnp.zeros_like(value[:, columns]))
                wide[d * rank : (d + 1) * rank, columns] = kept

    product = jnp.dot(wide[...], rows[...], preferred_element_type=jnp.float32)
    theirs[...] = (scale_out * product).astype(theirs.dtype).reshape(theirs.shape)


def gradient_theirs(place, shift, sums, rows, owners, half, scale_in, scale_out, kind, dep):
    rank, row_count = sums[0].shape
    tile = min(512, half)
    tiles = half // tile
    sums = after(tuple(sums), dep)
    whole = pl.BlockSpec((rank, row_count), lambda i, place, shift: (0, 0))
    return pl.pallas_call(
        functools.partial(outer_kernel, owners, rank, len(sums), scale_in, scale_out),
        grid_spec=pltpu.PrefetchScalarGridSpec(
            num_scalar_prefetch=2,
            grid=(tiles,),
            in_specs=[whole] * len(sums)
            + [
                pl.BlockSpec(
                    (row_count, tile), lambda i, place, shift: (0, (1 - place[1]) * tiles + i)
                )
            ],
            out_specs=[
                pl.BlockSpec((owners, rank, tile), lambda i, place, shift: (0, 0, i)),
                pl.BlockSpec((owners * rank, row_count), lambda i, place, shift: (0, 0)),
            ],
        ),
        out_shape=[
            jax.ShapeDtypeStruct((owners, rank, half), kind),
            jax.ShapeDtypeStruct((owners * rank, row_count), jnp.bfloat16),
        ],
        compiler_params=params(),
        cost_estimate=cost(2 * owners * rank * row_count * half, 2 * row_count * half),
        name="gradient_theirs",
    )(place, shift, *sums, rows)


def message_kernel(owners, rank, scale_out, place, wide, rows, theirs, *outs):
    product = scale_out * jnp.dot(wide[...], rows[...], preferred_element_type=jnp.float32)
    for d in range(owners):
        outs[d][0] = product[d * rank : (d + 1) * rank, :].astype(outs[d].dtype)
        outs[d][1] = theirs[d]


def gradient_messages(place, wide, rows, theirs, scale_out, dep):
    owners, rank, half = theirs.shape
    row_count = rows.shape[0]
    tile = min(512, half)
    tiles = half // tile
    wide = after(wide, dep)
    return pl.pallas_call(
        functools.partial(message_kernel, owners, rank, scale_out),
        grid_spec=pltpu.PrefetchScalarGridSpec(
            num_scalar_prefetch=1,
            grid=(tiles,),
            in_specs=[
                pl.BlockSpec(wide.shape, lambda i, place: (0, 0)),
                pl.BlockSpec((row_count, tile), lambda i, place: (0, place[1] * tiles + i)),
                pl.BlockSpec((owners, rank, tile), lambda i, place: (0, 0, i)),
            ],
            out_specs=[pl.BlockSpec((2, rank, tile), lambda i, place: (0, 0, i))] * owners,
        ),
        out_shape=[jax.ShapeDtypeStruct((2, rank, half), theirs.dtype)] * owners,
        compiler_params=params(),
        cost_estimate=cost(2 * owners * rank * row_count * half, 2 * row_count * half),
        name="gradient_messages",
    )(place, wide, rows, theirs)


def share_kernel(piece, rows, weight, out):
    out[...] = jnp.dot(rows[...], weight[...], preferred_element_type=jnp.float32).astype(out.dtype)


def share(tokens, weight, piece, start, count, width, dep):
    features = tokens.shape[1]
    tile = min(512, width)
    tiles = width // tile
    weight = after(weight, dep)
    return pl.pallas_call(
        share_kernel,
        grid_spec=pltpu.PrefetchScalarGridSpec(
            num_scalar_prefetch=1,
            grid=(tiles,),
            in_specs=[
                pl.BlockSpec((count, features), lambda j, piece: (start // count, 0)),
                pl.BlockSpec((features, tile), lambda j, piece: (0, piece[0] * tiles + j)),
            ],
            out_specs=pl.BlockSpec((count, tile), lambda j, piece: (0, j)),
        ),
        out_shape=jax.ShapeDtypeStruct((count, width), jnp.bfloat16),
        compiler_params=params(),
        cost_estimate=cost(2 * count * features * width, 2 * features * (width + count)),
        name="share",
    )(piece, tokens, weight)


def local_kernel(owners, rank, chunks, piece, tokens, own, other, wide, *refs):
    parts, early, out = refs[:owners], refs[owners:-1], refs[-1]

    def run(weight):
        for start, count in chunks:
            rows = slice(start, start + count)
            out[rows, :] = jnp.dot(
                tokens[rows, :], weight[...], preferred_element_type=jnp.float32
            )

    @pl.when(piece[1] == 1)
    def _():
        run(own)

    @pl.when(piece[1] != 1)
    def _():
        run(other)

    for n, (start, count) in enumerate(chunks):
        rows = slice(start, start + count)
        total = out[rows, :]
        for d in range(owners):
            total = total + ADAPTER_SCALE * lax.dot_general(
                wide[d * rank : (d + 1) * rank, rows],
                parts[d][...],
                (((0,), (0,)), ((), ())),
                preferred_element_type=jnp.float32,
            )
        for arrival in early[n :: len(chunks)]:
            total = total + arrival[...].astype(jnp.float32)
        out[rows, :] = total


def local_columns(piece, tokens, own, other, wide, parts, early, chunks, dep):
    row_count, features = tokens.shape
    owners, (rank, width) = len(parts), parts[0].shape
    tile = min(256, width)
    tiles = width // tile
    wide = after(wide, dep)
    arrivals = [a for group in early for a in group]
    pick_own = lambda j, p: (0, jnp.where(p[1] == 1, p[0] * tiles + j, 0))
    pick_other = lambda j, p: (0, jnp.where(p[1] == 1, 0, p[0] * tiles + j))
    return pl.pallas_call(
        functools.partial(local_kernel, owners, rank, chunks),
        grid_spec=pltpu.PrefetchScalarGridSpec(
            num_scalar_prefetch=1,
            grid=(tiles,),
            in_specs=[
                pl.BlockSpec((row_count, features), lambda j, p: (0, 0)),
                pl.BlockSpec((features, tile), pick_own),
                pl.BlockSpec((features, tile), pick_other),
                pl.BlockSpec(wide.shape, lambda j, p: (0, 0)),
            ]
            + [pl.BlockSpec((rank, tile), lambda j, p: (0, j))] * owners
            + [pl.BlockSpec((a.shape[0], tile), lambda j, p: (0, j)) for a in arrivals],
            out_specs=pl.BlockSpec((row_count, tile), lambda j, p: (0, j)),
        ),
        out_shape=jax.ShapeDtypeStruct((row_count, width), jnp.float32),
        compiler_params=params(),
        cost_estimate=cost(2 * row_count * features * width, 4 * row_count * width),
        name="local_columns",
    )(piece, tokens, own, other, wide, *parts, *arrivals)


def finish_kernel(count, *refs):
    local, late, out = refs[0], refs[1 : 1 + count], refs[-1]
    total = local[...]
    for arrival in late:
        total = total + arrival[...].astype(jnp.float32)
    out[...] = total.astype(out.dtype)


def finish(local, late, start, previous):
    row_count, width = local.shape
    count = late[0].shape[0]
    tile = min(256, count)
    first = start // tile
    here = pl.BlockSpec((tile, width), lambda i: (first + i, 0))
    arrived = pl.BlockSpec((tile, width), lambda i: (i, 0))
    operands = [local, *late]
    specs = [here] + [arrived] * len(late)
    aliases = {}
    if previous is not None:
        aliases = {len(operands): 0}
        operands.append(previous)
        specs.append(pl.BlockSpec(memory_space=pl.ANY))
    return pl.pallas_call(
        functools.partial(finish_kernel, len(late)),
        grid=(count // tile,),
        in_specs=specs,
        out_specs=here,
        out_shape=jax.ShapeDtypeStruct((row_count, width), jnp.bfloat16),
        input_output_aliases=aliases,
        compiler_params=params(),
        cost_estimate=cost(count * width, 8 * count * width),
        name="finish",
    )(*operands)


def adam_kernel(owners, slots, pick, used, corr, param, first, second, *refs):
    messages, (new_param, new_first, new_second, grads) = refs[:owners], refs[owners:]
    grads[...] = jnp.zeros_like(grads)
    for d in range(owners):
        for c in range(2):
            k = pick[c * owners + d]
            grads[k] = grads[k] + messages[d][c].astype(jnp.float32)
    for k in range(slots):
        grad = grads[k]
        one = BETA_ONE * first[k] + (1.0 - BETA_ONE) * grad
        two = BETA_TWO * second[k] + (1.0 - BETA_TWO) * grad * grad
        update = LEARN_RATE * (one / corr[k]) / (jnp.sqrt(two / corr[slots + k]) + ADAM_EPS)
        keep = used[k] == 1
        new_param[k] = jnp.where(keep, param[k] - update, param[k])
        new_first[k] = jnp.where(keep, one, first[k])
        new_second[k] = jnp.where(keep, two, second[k])


def adam(pick, used, corr, param, first, second, messages, dep):
    slots, rank, half = param.shape
    tile = min(256, half)
    state = pl.BlockSpec((slots, rank, tile), lambda i: (0, 0, i))
    message = pl.BlockSpec((2, rank, tile), lambda i: (0, 0, i))
    messages = after(tuple(messages), dep)
    return pl.pallas_call(
        functools.partial(adam_kernel, len(messages), slots),
        grid=(half // tile,),
        in_specs=[SMEM] * 3 + [state] * 3 + [message] * len(messages),
        out_specs=[state] * 3,
        out_shape=[dims(param)] * 3,
        scratch_shapes=[pltpu.VMEM((slots, rank, tile), jnp.float32)],
        compiler_params=params(),
        cost_estimate=cost(20 * param.size, 40 * param.size),
        name="adam",
    )(pick, used, corr, param, first, second, *messages)


def on_device(
    tokens,
    frozen_weight,
    cotangent,
    down_adapters,
    up_adapters,
    down_first_moment,
    up_first_moment,
    down_second_moment,
    up_second_moment,
    optimizer_steps,
    slot_of_tenant,
    tenant_of_block,
):
    row_count, din_local = tokens.shape
    width = cotangent.shape[1]
    block_count = row_count // BLK_ROWS
    owners = lax.axis_size("dp")
    cores = lax.axis_size("sub")
    columns = lax.axis_size("tensor")
    z = lax.axis_index("dp")
    s = lax.axis_index("sub")
    x = lax.axis_index("tensor")
    slots, half, rank = down_adapters.shape
    flip = lambda v: jnp.swapaxes(v, 1, 2)
    down_adapters, up_adapters = flip(down_adapters), flip(up_adapters)
    down_first_moment, up_first_moment = flip(down_first_moment), flip(up_first_moment)
    down_second_moment, up_second_moment = flip(down_second_moment), flip(up_second_moment)
    per_half = columns // cores
    place = jnp.stack([z, s]).astype(jnp.int32)

    down_other = rotate(down_adapters, "sub", 1)
    up_other = rotate(up_adapters, "sub", 1)

    pick, shift, used = pl.pallas_call(
        functools.partial(tables_kernel, owners, cores, slots, block_count),
        in_specs=[SMEM] * 3,
        out_specs=[SMEM] * 3,
        out_shape=[
            jax.ShapeDtypeStruct((cores * owners,), jnp.int32),
            jax.ShapeDtypeStruct((block_count,), jnp.int32),
            jax.ShapeDtypeStruct((slots,), jnp.int32),
        ],
        name="tables",
    )(place, slot_of_tenant, tenant_of_block)
    steps = (optimizer_steps + 1).astype(jnp.float32)
    corr = jnp.concatenate(
        [
            1.0 - jnp.power(jnp.float32(BETA_ONE), steps),
            1.0 - jnp.power(jnp.float32(BETA_TWO), steps),
        ]
    )

    def pack(own, other, dep):
        return pl.pallas_call(
            functools.partial(pack_kernel, owners),
            in_specs=[SMEM] * 2 + [pl.BlockSpec(memory_space=pltpu.VMEM)] * 2,
            out_specs=[pl.BlockSpec(memory_space=pltpu.VMEM)] * owners,
            out_shape=[jax.ShapeDtypeStruct((rank, cores * half), jnp.bfloat16)] * owners,
            compiler_params=params(),
            cost_estimate=cost(own.size, 12 * own.size),
            name="pack",
        )(place, pick, own, after(other, dep))

    def spread_out(messages, sign):
        return [m if d == 0 else rotate(m, "dp", sign * d) for d, m in enumerate(messages)]

    def shares(weight, start, count, dep):
        out = []
        for step in range(1, columns):
            piece = lax.rem(lax.rem(x + step, columns), per_half).astype(jnp.int32).reshape(1)
            out.append(share(tokens, weight, piece, start, count, width, dep))
            dep = out[-1]
        return out

    def send(products, own, dep):
        got = []
        for step, product in zip(range(1, columns), products):
            pairs = []
            for t in range(columns):
                for c in range(cores):
                    target = (t + step) % columns
                    if (target // per_half == c) == own:
                        pairs.append((t * cores + c, target * cores + c))
            got.append(lax.ppermute(after(product, dep), ("tensor", "sub"), pairs))
        return got

    def exchange(part):
        return [part] + [rotate(part, "tensor", step) for step in range(1, columns)]

    quarter = row_count // 4
    early_chunks = ((0, 2 * quarter), (2 * quarter, quarter), (3 * quarter, quarter))
    late_chunks = ((0, 2 * quarter), (2 * quarter, 2 * quarter))

    down_packed = pack(down_adapters, down_other, used)
    down_parts = spread_out(down_packed, 1)
    up_packed = pack(up_adapters, up_other, down_packed[0])
    other_weight = rotate(after(frozen_weight, up_packed[0]), "sub", 1)

    own_a = shares(frozen_weight, *early_chunks[0], up_packed[0])
    early_a = send(own_a, True, used)
    own_c = shares(frozen_weight, *early_chunks[2], own_a[-1])

    down_part = adapter_product(shift, down_parts, tokens, own_c[-1])
    down_sums = exchange(down_part)
    up_parts = spread_out(after(tuple(up_packed), down_part), 1)
    own_b = shares(frozen_weight, *early_chunks[1], down_part)
    early_b = send(own_b, True, used)
    late_a_share = shares(other_weight, *late_chunks[0], own_b[-1])

    up_theirs, down_wide = gradient_theirs(
        place, shift, down_sums, cotangent, owners, half, 1.0, ADAPTER_SCALE, jnp.bfloat16,
        late_a_share[-1],
    )
    up_swapped = rotate(up_theirs, "sub", 1)
    late_b_share = shares(other_weight, *late_chunks[1], up_theirs)
    up_messages = gradient_messages(
        place, down_wide, cotangent, up_swapped, ADAPTER_SCALE, late_b_share[-1]
    )
    back_part = adapter_product(shift, up_parts, cotangent, up_messages[0])
    back_sums = exchange(back_part)
    up_returned = spread_out(after(tuple(up_messages), back_part), -1)
    early_c = send(own_c, True, back_part)

    down_theirs, back_wide = gradient_theirs(
        place, shift, back_sums, tokens, owners, half, ADAPTER_SCALE, 1.0, jnp.float32,
        back_part,
    )
    down_swapped = rotate(down_theirs, "sub", 1)
    late_a = send(late_a_share, False, down_theirs)
    down_messages = gradient_messages(place, back_wide, tokens, down_swapped, 1.0, back_part)
    down_returned = spread_out(down_messages, -1)
    late_b = send(late_b_share, False, down_messages[0])

    piece = jnp.stack([lax.rem(x, per_half), (lax.div(x, per_half) == s).astype(jnp.int32)])
    local = local_columns(
        piece.astype(jnp.int32), tokens, frozen_weight, other_weight, down_wide, up_parts,
        list(zip(early_a, early_b, early_c)), early_chunks, down_messages[0],
    )
    fresh_up, fresh_up_first, fresh_up_second = adam(
        pick, used, corr, up_adapters, up_first_moment, up_second_moment, up_returned, local
    )
    projected = finish(after(local, fresh_up), late_a, late_chunks[0][0], None)
    projected = finish(local, late_b, late_chunks[1][0], projected)
    fresh_down, fresh_down_first, fresh_down_second = adam(
        pick, used, corr, down_adapters, down_first_moment, down_second_moment, down_returned,
        fresh_up,
    )
    return (
        projected,
        flip(fresh_down),
        flip(fresh_up),
        flip(fresh_down_first),
        flip(fresh_up_first),
        flip(fresh_down_second),
        flip(fresh_up_second),
    )


def solution(mesh):
    placed = (
        P(("groups", "dp", "sub"), "tensor"),
        P("tensor", "sub"),
        P(("groups", "dp", "sub"), "tensor"),
        P(("groups", "dp"), ("tensor", "sub"), None),
        P(("groups", "dp"), ("tensor", "sub"), None),
        P(("groups", "dp"), ("tensor", "sub"), None),
        P(("groups", "dp"), ("tensor", "sub"), None),
        P(("groups", "dp"), ("tensor", "sub"), None),
        P(("groups", "dp"), ("tensor", "sub"), None),
        P(("groups", "dp")),
        P("groups"),
        P("groups"),
    )
    return jax.shard_map(
        on_device,
        mesh=mesh,
        in_specs=placed,
        out_specs=(
            P(("groups", "dp", "sub"), "tensor"),
            P(("groups", "dp"), ("tensor", "sub"), None),
            P(("groups", "dp"), ("tensor", "sub"), None),
            P(("groups", "dp"), ("tensor", "sub"), None),
            P(("groups", "dp"), ("tensor", "sub"), None),
            P(("groups", "dp"), ("tensor", "sub"), None),
            P(("groups", "dp"), ("tensor", "sub"), None),
        ),
        check_vma=False,
    )
```

```python
import functools

import jax
import jax.numpy as jnp
from jax import lax
from jax.experimental import pallas as pl
from jax.experimental.pallas import tpu as pltpu
from jax.sharding import PartitionSpec as P

BLK_ROWS = 128


ADAPTER_SCALE = 2.0
BETA_ONE = 0.9
BETA_TWO = 0.999
LEARN_RATE = 0.01
ADAM_EPS = 1e-08

SMEM = pl.BlockSpec(memory_space=pltpu.SMEM)
VMEM_BYTES = 63_000_000
TOP_CODE = 32767.0
LEVELS = 64.0
LEVEL_LANES = 128
COST = 20.0


def params():
    return pltpu.CompilerParams(vmem_limit_bytes=VMEM_BYTES)


def cost(micros):
    flops = int(micros * 1_000_000_000 * COST)
    return pl.CostEstimate(flops=flops, bytes_accessed=1000, transcendentals=0)


def rotate(value, axis, shift):
    size = lax.axis_size(axis)
    return lax.ppermute(value, axis, [(i, (i + shift) % size) for i in range(size)])


ANY = pl.BlockSpec(memory_space=pl.ANY)


def behind(kernel, deps, scalars=0):
    return lambda *refs: kernel(*refs[:scalars], *refs[scalars + len(deps) :])


def tie_kernel(*refs):
    pass


def tie(values, deps):
    return pl.pallas_call(
        tie_kernel,
        in_specs=[ANY] * (len(values) + len(deps)),
        out_specs=[ANY] * len(values),
        out_shape=[dims(v) for v in values],
        input_output_aliases={k: k for k in range(len(values))},
        cost_estimate=cost(100),
        name="tie",
    )(*values, *deps)


def dims(value):
    return jax.ShapeDtypeStruct(value.shape, value.dtype)


def tables_kernel(owners, cores, slots, block_count, place, slot_of, tenant_of, pick, shift, used):
    z, s = place[0], place[1]
    for k in range(slots):
        used[k] = 0

    def slot_at(device, b):
        return slot_of[tenant_of[device * block_count + b]]

    def per_device(i, carry):
        c, d = lax.div(i, owners), lax.rem(i, owners)
        device = lax.rem(z + d, owners) * cores + lax.rem(s + c, cores)

        def per_block(b, found):
            local = slot_at(device, b) - z * slots
            mine = jnp.logical_and(local >= 0, local < slots)

            @pl.when(mine)
            def _():
                used[local] = 1

            return jnp.where(mine, local, found)

        pick[i] = lax.fori_loop(0, block_count, per_block, 0)
        return carry

    lax.fori_loop(0, owners * cores, per_device, 0)
    for b in range(block_count):
        owner = lax.div(slot_at(z * cores + s, b), slots)
        shift[b] = lax.rem(z - owner + owners, owners)


def pack_kernel(owners, place, pick, own, other, *outs):
    s = place[1]
    half = own.shape[2]
    for d in range(owners):
        k = pick[d]
        near, far = own[k].astype(jnp.bfloat16), other[k].astype(jnp.bfloat16)
        outs[d][:, :half] = jnp.where(s == 0, near, far)
        outs[d][:, half:] = jnp.where(s == 0, far, near)


def product_kernel(owners, rank, tile_rows, shift, *refs):
    parts, rows, out, cat = refs[:owners], refs[owners], refs[owners + 1], refs[owners + 2]
    step = pl.program_id(0)

    @pl.when(step == 0)
    def _():
        for d in range(owners):
            cat[d * rank : (d + 1) * rank, :] = parts[d][...]

    full = lax.dot_general(
        cat[...], rows[...], (((1,), (1,)), ((), ())), preferred_element_type=jnp.float32
    )
    for b in range(tile_rows // BLK_ROWS):
        owner_shift = shift[step * (tile_rows // BLK_ROWS) + b]
        columns = slice(b * BLK_ROWS, (b + 1) * BLK_ROWS)
        value = full[:rank, columns]
        for d in range(1, owners):
            value = jnp.where(owner_shift == d, full[d * rank : (d + 1) * rank, columns], value)
        out[:, columns] = value


def adapter_product(shift, parts, rows, deps):
    owners, (rank, features), row_count = len(parts), parts[0].shape, rows.shape[0]
    tile = min(256, row_count)
    whole = pl.BlockSpec((rank, features), lambda i: (0, 0))
    return pl.pallas_call(
        behind(functools.partial(product_kernel, owners, rank, tile), deps),
        grid=(row_count // tile,),
        in_specs=[ANY] * len(deps) + [SMEM] + [whole] * owners + [pl.BlockSpec((tile, features), lambda i: (i, 0))],
        out_specs=pl.BlockSpec((rank, tile), lambda i: (0, i)),
        out_shape=jax.ShapeDtypeStruct((rank, row_count), jnp.float32),
        scratch_shapes=[pltpu.VMEM((owners * rank, features), jnp.bfloat16)],
        compiler_params=params(),
        cost_estimate=cost(2.6),
        name="adapter_product",
    )(*deps, shift, *parts, rows)


def encode(product, kind):
    if kind != jnp.int16:
        return product.astype(kind)
    top = jnp.maximum(jnp.max(jnp.abs(product), axis=1, keepdims=True), 1e-30)
    level = jnp.floor(jnp.log2(top) * LEVELS) + 2.0
    coded = jnp.round(product * (TOP_CODE * jnp.exp2(level * (-1.0 / LEVELS))))
    coded = jnp.clip(coded, -TOP_CODE, TOP_CODE).astype(jnp.int32).astype(jnp.int16)
    lanes = jnp.broadcast_to(level, (product.shape[0], LEVEL_LANES))
    return jnp.concatenate([coded, lanes.astype(jnp.int32).astype(jnp.int16)], axis=1)


def message_lanes(half, kind):
    return half + (LEVEL_LANES if kind == jnp.int16 else 0)


def outer_kernel(owners, rank, terms, scale_in, scale_out, place, shift, *refs):
    sums, rows, theirs, wide = refs[:terms], refs[terms], refs[terms + 1], refs[terms + 2]
    total = sums[0][...]
    for t in range(1, terms):
        total = total + sums[t][...]
    value = (scale_in * total).astype(jnp.bfloat16)
    for b in range(value.shape[1] // BLK_ROWS):
        columns = slice(b * BLK_ROWS, (b + 1) * BLK_ROWS)
        for d in range(owners):
            kept = jnp.where(shift[b] == d, value[:, columns], jnp.zeros_like(value[:, columns]))
            wide[d * rank : (d + 1) * rank, columns] = kept
    product = scale_out * jnp.dot(wide[...], rows[...], preferred_element_type=jnp.float32)
    theirs[...] = encode(product, theirs.dtype).reshape(theirs.shape)


def gradient_theirs(place, shift, sums, rows, owners, half, scale_in, scale_out, kind, deps):
    rank, row_count = sums[0].shape
    lanes = message_lanes(half, kind)
    whole = pl.BlockSpec((rank, row_count), lambda i, place, shift: (0, 0))
    return pl.pallas_call(
        behind(
            functools.partial(outer_kernel, owners, rank, len(sums), scale_in, scale_out), deps, 2
        ),
        grid_spec=pltpu.PrefetchScalarGridSpec(
            num_scalar_prefetch=2,
            grid=(1,),
            in_specs=[ANY] * len(deps)
            + [whole] * len(sums)
            + [pl.BlockSpec((row_count, half), lambda i, place, shift: (0, 1 - place[1]))],
            out_specs=[
                pl.BlockSpec((owners, rank, lanes), lambda i, place, shift: (0, 0, 0)),
                pl.BlockSpec((owners * rank, row_count), lambda i, place, shift: (0, 0)),
            ],
        ),
        out_shape=[
            jax.ShapeDtypeStruct((owners, rank, lanes), kind),
            jax.ShapeDtypeStruct((owners * rank, row_count), jnp.bfloat16),
        ],
        compiler_params=params(),
        cost_estimate=cost(2),
        name="gradient_theirs",
    )(place, shift, *deps, *sums, rows)


def message_kernel(owners, rank, scale_out, place, wide, rows, theirs, *outs):
    product = scale_out * jnp.dot(wide[...], rows[...], preferred_element_type=jnp.float32)
    coded = encode(product, theirs.dtype)
    for d in range(owners):
        outs[d][0] = coded[d * rank : (d + 1) * rank, :]
        outs[d][1] = theirs[d]


def gradient_messages(place, wide, rows, theirs, half, scale_out, deps):
    owners, rank, lanes = theirs.shape
    row_count = rows.shape[0]
    return pl.pallas_call(
        behind(functools.partial(message_kernel, owners, rank, scale_out), deps, 1),
        grid_spec=pltpu.PrefetchScalarGridSpec(
            num_scalar_prefetch=1,
            grid=(1,),
            in_specs=[ANY] * len(deps)
            + [
                pl.BlockSpec(wide.shape, lambda i, place: (0, 0)),
                pl.BlockSpec((row_count, half), lambda i, place: (0, place[1])),
                pl.BlockSpec((owners, rank, lanes), lambda i, place: (0, 0, 0)),
            ],
            out_specs=[pl.BlockSpec((2, rank, lanes), lambda i, place: (0, 0, 0))] * owners,
        ),
        out_shape=[jax.ShapeDtypeStruct((2, rank, lanes), theirs.dtype)] * owners,
        compiler_params=params(),
        cost_estimate=cost(2.4),
        name="gradient_messages",
    )(place, *deps, wide, rows, theirs)


def share_kernel(spans, keep, rows, weight, *outs):
    if keep:

        @pl.when(pl.program_id(0) == 0)
        def _():
            outs[-1][...] = rows[...]

    product = jnp.dot(rows[...], weight[...], preferred_element_type=jnp.float32)
    for out, (start, count) in zip(outs, spans):
        out[...] = product[start : start + count, :].astype(out.dtype)


def share(tokens, weight, piece, start, total, spans, width, keep, deps):
    features = tokens.shape[1]
    tile = min(512, width)
    tiles = width // tile
    return pl.pallas_call(
        behind(functools.partial(share_kernel, spans, keep), deps),
        grid=(tiles,),
        in_specs=[ANY] * len(deps)
        + [
            pl.BlockSpec((total, features), lambda j: (start // total, 0)),
            pl.BlockSpec((features, tile), lambda j: (0, piece * tiles + j)),
        ],
        out_specs=[pl.BlockSpec((count, tile), lambda j: (0, j)) for _, count in spans]
        + [pl.BlockSpec((total, features), lambda j: (0, 0))] * keep,
        out_shape=[jax.ShapeDtypeStruct((count, width), jnp.bfloat16) for _, count in spans]
        + [jax.ShapeDtypeStruct((total, features), jnp.bfloat16)] * keep,
        compiler_params=params(),
        cost_estimate=cost(4.0 * total / 256),
        name="share",
    )(*deps, tokens, weight)


def finish_kernel(owners, rank, tile, flags, spans, mine_is_own, wide, *refs):
    parts, arrays = refs[:owners], refs[owners : owners + len(flags)]
    out, cat = refs[-2], refs[-1]
    step = pl.program_id(0)

    @pl.when(step == 0)
    def _():
        for d in range(owners):
            cat[d * rank : (d + 1) * rank, :] = parts[d][...]

    total = ADAPTER_SCALE * lax.dot_general(
        wide[...], cat[...], (((0,), (0,)), ((), ())), preferred_element_type=jnp.float32
    )
    for array, flag, (first, last) in zip(arrays, flags, spans):
        active = jnp.logical_and(step >= first, step < last)
        if flag >= 0:
            active = jnp.logical_and(active, mine_is_own[0] == flag)
        value = array[...].astype(jnp.float32)
        total = total + jnp.where(active, value, 0.0)
    out[...] = total.astype(out.dtype)


def finish(mine_is_own, wide, parts, row_count, start, count, terms, previous, deps):
    owners, (rank, width) = len(parts), parts[0].shape
    tile = BLK_ROWS
    for size in (256, 512):
        if all(v % size == 0 for v in [start, count] + [t[0].shape[0] for t in terms]):
            tile = size
    first = start // tile
    specs, spans = [], []
    for array, row, _ in terms:
        low, many = (row - start) // tile, array.shape[0] // tile
        place_of = lambda i, low=low, many=many: (jnp.clip(i - low, 0, many - 1), 0)
        specs.append(pl.BlockSpec((tile, width), place_of))
        spans.append((low, low + many))
    operands = [*deps, mine_is_own, wide, *parts] + [t[0] for t in terms]
    in_specs = (
        [ANY] * len(deps)
        + [SMEM, pl.BlockSpec((owners * rank, tile), lambda i: (0, first + i))]
        + [pl.BlockSpec((rank, width), lambda i: (0, 0))] * owners
        + specs
    )
    aliases = {}
    if previous is not None:
        aliases = {len(operands): 0}
        operands.append(previous)
        in_specs.append(ANY)
    return pl.pallas_call(
        behind(
            functools.partial(finish_kernel, owners, rank, tile, [t[2] for t in terms], spans),
            deps,
        ),
        grid=(count // tile,),
        in_specs=in_specs,
        out_specs=pl.BlockSpec((tile, width), lambda i: (first + i, 0)),
        out_shape=jax.ShapeDtypeStruct((row_count, width), jnp.bfloat16),
        scratch_shapes=[pltpu.VMEM((owners * rank, width), jnp.bfloat16)],
        input_output_aliases=aliases,
        compiler_params=params(),
        cost_estimate=cost(4),
        name="finish",
    )(*operands)


def adam_kernel(owners, slots, coded, pick, used, corr, param, first, second, *refs):
    messages, levels = refs[:owners], refs[owners:-4]
    new_param, new_first, new_second, grads = refs[-4:]
    grads[...] = jnp.zeros_like(grads)
    for d in range(owners):
        for c in range(2):
            k = pick[c * owners + d]
            value = messages[d][c].astype(jnp.float32)
            if coded:
                level = levels[d][c].astype(jnp.float32)[:, :1]
                value = value * (jnp.exp2(level * (1.0 / LEVELS)) * (1.0 / TOP_CODE))
            grads[k] = grads[k] + value
    for k in range(slots):
        grad = grads[k]
        one = BETA_ONE * first[k] + (1.0 - BETA_ONE) * grad
        two = BETA_TWO * second[k] + (1.0 - BETA_TWO) * grad * grad
        update = LEARN_RATE * (one / corr[k]) / (jnp.sqrt(two / corr[slots + k]) + ADAM_EPS)
        keep = used[k] == 1
        new_param[k] = jnp.where(keep, param[k] - update, param[k])
        new_first[k] = jnp.where(keep, one, first[k])
        new_second[k] = jnp.where(keep, two, second[k])


def adam(pick, used, corr, param, first, second, messages, deps):
    slots, rank, half = param.shape
    tile = min(256, half)
    state = pl.BlockSpec((slots, rank, tile), lambda i: (0, 0, i))
    message = pl.BlockSpec((2, rank, tile), lambda i: (0, 0, i))
    coded = messages[0].dtype == jnp.int16
    levels = messages if coded else ()
    level = pl.BlockSpec((2, rank, LEVEL_LANES), lambda i: (0, 0, half // LEVEL_LANES))
    return pl.pallas_call(
        behind(functools.partial(adam_kernel, len(messages), slots, coded), deps),
        grid=(half // tile,),
        in_specs=[ANY] * len(deps)
        + [SMEM] * 3
        + [state] * 3
        + [message] * len(messages)
        + [level] * len(levels),
        out_specs=[state] * 3,
        out_shape=[dims(param)] * 3,
        scratch_shapes=[pltpu.VMEM((slots, rank, tile), jnp.float32)],
        compiler_params=params(),
        cost_estimate=cost(4),
        name="adam",
    )(*deps, pick, used, corr, param, first, second, *messages, *levels)


def on_device(
    tokens,
    frozen_weight,
    cotangent,
    down_adapters,
    up_adapters,
    down_first_moment,
    up_first_moment,
    down_second_moment,
    up_second_moment,
    optimizer_steps,
    slot_of_tenant,
    tenant_of_block,
):
    row_count, din_local = tokens.shape
    width = cotangent.shape[1]
    block_count = row_count // BLK_ROWS
    owners = lax.axis_size("dp")
    cores = lax.axis_size("sub")
    columns = lax.axis_size("tensor")
    z = lax.axis_index("dp")
    s = lax.axis_index("sub")
    x = lax.axis_index("tensor")
    slots, half, rank = down_adapters.shape
    flip = lambda v: jnp.swapaxes(v, 1, 2)
    down_adapters, up_adapters = flip(down_adapters), flip(up_adapters)
    down_first_moment, up_first_moment = flip(down_first_moment), flip(up_first_moment)
    down_second_moment, up_second_moment = flip(down_second_moment), flip(up_second_moment)
    per_half = columns // cores
    place = jnp.stack([z, s]).astype(jnp.int32)

    down_other = rotate(down_adapters, "sub", 1)
    up_other = rotate(up_adapters, "sub", 1)

    def tables(deps):
        return pl.pallas_call(
            behind(functools.partial(tables_kernel, owners, cores, slots, block_count), deps),
            in_specs=[ANY] * len(deps) + [SMEM] * 3,
            out_specs=[SMEM] * 3,
            out_shape=[
                jax.ShapeDtypeStruct((cores * owners,), jnp.int32),
                jax.ShapeDtypeStruct((block_count,), jnp.int32),
                jax.ShapeDtypeStruct((slots,), jnp.int32),
            ],
            cost_estimate=cost(2),
            name="tables",
        )(*deps, place, slot_of_tenant, tenant_of_block)

    steps = (optimizer_steps + 1).astype(jnp.float32)
    corr = jnp.concatenate(
        [
            1.0 - jnp.power(jnp.float32(BETA_ONE), steps),
            1.0 - jnp.power(jnp.float32(BETA_TWO), steps),
        ]
    )

    def pack(own, other, deps):
        return pl.pallas_call(
            behind(functools.partial(pack_kernel, owners), deps),
            in_specs=[ANY] * len(deps) + [SMEM] * 2 + [pl.BlockSpec(memory_space=pltpu.VMEM)] * 2,
            out_specs=[pl.BlockSpec(memory_space=pltpu.VMEM)] * owners,
            out_shape=[jax.ShapeDtypeStruct((rank, cores * half), jnp.bfloat16)] * owners,
            compiler_params=params(),
        cost_estimate=cost(1),
            name="pack",
        )(*deps, place, pick, own, other)

    def spread_out(messages, sign):
        return [m if d == 0 else rotate(m, "dp", sign * d) for d, m in enumerate(messages)]

    def shares(rows, start, total, spans, keep, deps):
        pieces = []
        for piece in range(per_half):
            kept = int(keep and piece == 0)
            out = share(rows, frozen_weight, piece, start, total, spans, width, kept, deps)
            pieces.append(out[: len(spans)])
            copy = out[-1] if kept else copy if piece else None
            deps = [pieces[-1][0]]
        chunks = [list(chunk) for chunk in zip(*pieces)]
        return chunks + [copy] if keep else chunks

    def piece_for(chunk, target):
        if per_half == 1:
            return chunk[0]
        out = chunk[0]
        for piece in range(1, per_half):
            out = jnp.where(lax.rem(target, per_half) == piece, chunk[piece], out)
        return out

    def send(chunk, cross):
        got = []
        for step in range(1, columns):
            pairs = []
            for t in range(columns):
                for c in range(cores):
                    target = (t + step) % columns
                    if target // per_half == c:
                        pairs.append((t * cores + c, target * cores + (c + cross) % cores))
            operand = piece_for(chunk, lax.rem(x + step, columns))
            got.append(lax.ppermute(operand, ("tensor", "sub"), pairs))
        return got

    def send_local(chunk):
        pairs = []
        for t in range(columns):
            c = t // per_half
            pairs.append((t * cores + c, t * cores + (c + 1) % cores))
        return lax.ppermute(piece_for(chunk, x), ("tensor", "sub"), pairs)

    def exchange(part):
        return [part] + [rotate(part, "tensor", step) for step in range(1, columns)]

    half_rows, quarter = row_count // 2, row_count // 4
    all_half = (0, half_rows)
    two_quarters = [(0, quarter), (quarter, quarter)]
    own_a, low_rows = shares(tokens, 0, half_rows, [all_half], True, [])
    got_a = send(own_a, 0)
    other_low = rotate(low_rows, "sub", 1)

    pick, shift, used = tables([own_a[-1]])
    down_packed = pack(down_adapters, down_other, [])
    down_parts = spread_out(down_packed, 1)
    up_packed = pack(up_adapters, up_other, [down_packed[0]])
    own_b, own_c, high_rows = shares(
        tokens, half_rows, half_rows, two_quarters, True, [up_packed[0]]
    )
    high_rows, = tie([high_rows], [other_low])
    other_high = rotate(high_rows, "sub", 1)
    own_b = tie(own_b, got_a + [high_rows])
    got_b = send(own_b, 0)
    up_packed = tie(up_packed, down_parts + [own_b[-1]])
    up_parts = spread_out(up_packed, 1)

    down_part = adapter_product(shift, down_parts, tokens, [up_packed[0], other_high])
    down_sums = exchange(down_part)
    cross_a, cross_a_near = shares(other_low, 0, half_rows, [all_half] * 2, False, [down_part])
    up_theirs, down_wide = gradient_theirs(
        place, shift, down_sums, cotangent, owners, half, 1.0, ADAPTER_SCALE, jnp.bfloat16,
        [cross_a[-1]] + got_b,
    )
    own_c = tie(own_c, [up_theirs])
    got_c = send(own_c, 0)
    up_swapped = rotate(up_theirs, "sub", 1)
    cross_b, cross_b_near = shares(
        other_high, 0, half_rows, [all_half] * 2, False, [own_c[-1]]
    )
    up_messages = gradient_messages(
        place, down_wide, cotangent, up_swapped, half, ADAPTER_SCALE, [cross_b[-1]] + up_parts
    )
    up_returned = spread_out(up_messages, -1)
    back_part = adapter_product(shift, up_parts, cotangent, [up_messages[0]] + got_c)
    back_sums = exchange(back_part)
    cross_a = tie(cross_a, [back_sums[-1]])
    late_a = send(cross_a, 1)
    down_theirs, back_wide = gradient_theirs(
        place, shift, back_sums, tokens, owners, half, ADAPTER_SCALE, 1.0, jnp.int16,
        [cross_a[-1]],
    )
    down_swapped = rotate(down_theirs, "sub", 1)
    back_wide, = tie([back_wide], [down_theirs])
    down_messages = gradient_messages(
        place, back_wide, tokens, down_swapped, half, 1.0, up_returned
    )
    down_returned = spread_out(down_messages, -1)
    cross_a_near = tie(cross_a_near, [down_messages[0]])
    local_a = send_local(cross_a_near)
    cross_b_near = tie(cross_b_near, [local_a])
    local_b = send_local(cross_b_near)

    fresh_up, fresh_up_first, fresh_up_second = adam(
        pick, used, corr, up_adapters, up_first_moment, up_second_moment, up_returned,
        [down_messages[0]],
    )
    cross_b = tie(cross_b, late_a)
    late_b = send(cross_b, 1)
    mine_is_own = (lax.div(x, per_half) == s).astype(jnp.int32).reshape(1)
    kept = [(piece_for(own_a, x), 0, 1), (piece_for(own_b, x), half_rows, 1)]
    kept.append((piece_for(own_c, x), half_rows + quarter, 1))
    terms_a = [kept[0], (local_a, 0, 0)] + [(g, 0, -1) for g in got_a + late_a]
    terms_b = kept[1:] + [(local_b, half_rows, 0)]
    terms_b += [(g, half_rows, -1) for g in got_b + late_b]
    terms_b += [(g, half_rows + quarter, -1) for g in got_c]
    projected = finish(
        mine_is_own, down_wide, up_parts, row_count, 0, half_rows, terms_a, None,
        [fresh_up],
    )
    fresh_down, fresh_down_first, fresh_down_second = adam(
        pick, used, corr, down_adapters, down_first_moment, down_second_moment, down_returned,
        [projected],
    )
    projected = finish(
        mine_is_own, down_wide, up_parts, row_count, half_rows, half_rows, terms_b, projected,
        [fresh_down],
    )
    return (
        projected,
        flip(fresh_down),
        flip(fresh_up),
        flip(fresh_down_first),
        flip(fresh_up_first),
        flip(fresh_down_second),
        flip(fresh_up_second),
    )


def solution(mesh):
    placed = (
        P(("groups", "dp", "sub"), "tensor"),
        P("tensor", "sub"),
        P(("groups", "dp", "sub"), "tensor"),
        P(("groups", "dp"), ("tensor", "sub"), None),
        P(("groups", "dp"), ("tensor", "sub"), None),
        P(("groups", "dp"), ("tensor", "sub"), None),
        P(("groups", "dp"), ("tensor", "sub"), None),
        P(("groups", "dp"), ("tensor", "sub"), None),
        P(("groups", "dp"), ("tensor", "sub"), None),
        P(("groups", "dp")),
        P("groups"),
        P("groups"),
    )
    return jax.shard_map(
        on_device,
        mesh=mesh,
        in_specs=placed,
        out_specs=(
            P(("groups", "dp", "sub"), "tensor"),
            P(("groups", "dp"), ("tensor", "sub"), None),
            P(("groups", "dp"), ("tensor", "sub"), None),
            P(("groups", "dp"), ("tensor", "sub"), None),
            P(("groups", "dp"), ("tensor", "sub"), None),
            P(("groups", "dp"), ("tensor", "sub"), None),
            P(("groups", "dp"), ("tensor", "sub"), None),
        ),
        check_vma=False,
    )
```

```python
import functools

import jax
import jax.numpy as jnp
from jax import lax
from jax.experimental import pallas as pl
from jax.experimental.pallas import tpu as pltpu
from jax.sharding import PartitionSpec as P

BLK_ROWS = 128


ADAPTER_SCALE = 2.0
BETA_ONE = 0.9
BETA_TWO = 0.999
LEARN_RATE = 0.01
ADAM_EPS = 1e-08

SMEM = pl.BlockSpec(memory_space=pltpu.SMEM)
VMEM_BYTES = 63_000_000
TOP_CODE = 32767.0
LEVELS = 64.0
LEVEL_LANES = 128
COST = 20.0


def params():
    return pltpu.CompilerParams(vmem_limit_bytes=VMEM_BYTES)


def cost(micros):
    flops = int(micros * 1_000_000_000 * COST)
    return pl.CostEstimate(flops=flops, bytes_accessed=1000, transcendentals=0)


def rotate(value, axis, shift):
    size = lax.axis_size(axis)
    return lax.ppermute(value, axis, [(i, (i + shift) % size) for i in range(size)])


ANY = pl.BlockSpec(memory_space=pl.ANY)


def behind(kernel, deps, scalars=0):
    return lambda *refs: kernel(*refs[:scalars], *refs[scalars + len(deps) :])


def tie_kernel(*refs):
    pass


def tie(values, deps):
    return pl.pallas_call(
        tie_kernel,
        in_specs=[ANY] * (len(values) + len(deps)),
        out_specs=[ANY] * len(values),
        out_shape=[dims(v) for v in values],
        input_output_aliases={k: k for k in range(len(values))},
        cost_estimate=cost(100),
        name="tie",
    )(*values, *deps)


def dims(value):
    return jax.ShapeDtypeStruct(value.shape, value.dtype)


def tables_kernel(owners, cores, slots, block_count, place, slot_of, tenant_of, pick, owner_of, used):
    z, s = place[0], place[1]
    for k in range(slots):
        used[k] = 0

    def slot_at(device, b):
        return slot_of[tenant_of[device * block_count + b]]

    def per_device(i, carry):
        c, d = lax.div(i, owners), lax.rem(i, owners)
        device = d * cores + lax.rem(s + c, cores)

        def per_block(b, found):
            local = slot_at(device, b) - z * slots
            mine = jnp.logical_and(local >= 0, local < slots)

            @pl.when(mine)
            def _():
                used[local] = 1

            return jnp.where(mine, local, found)

        pick[i] = lax.fori_loop(0, block_count, per_block, 0)
        return carry

    lax.fori_loop(0, owners * cores, per_device, 0)
    for b in range(block_count):
        owner_of[b] = lax.div(slot_at(z * cores + s, b), slots)


def pack_kernel(owners, place, pick, own, other, out):
    s = place[1]
    half = own.shape[2]
    for d in range(owners):
        k = pick[d]
        near, far = own[k].astype(jnp.bfloat16), other[k].astype(jnp.bfloat16)
        out[d, :, :half] = jnp.where(s == 0, near, far)
        out[d, :, half:] = jnp.where(s == 0, far, near)


def product_kernel(owners, rank, tile_rows, owner_of, adapters, rows, out):
    step = pl.program_id(0)
    full = lax.dot_general(
        adapters[...], rows[...], (((1,), (1,)), ((), ())), preferred_element_type=jnp.float32
    )
    for b in range(tile_rows // BLK_ROWS):
        owner = owner_of[step * (tile_rows // BLK_ROWS) + b]
        columns = slice(b * BLK_ROWS, (b + 1) * BLK_ROWS)
        value = full[:rank, columns]
        for d in range(1, owners):
            value = jnp.where(owner == d, full[d * rank : (d + 1) * rank, columns], value)
        out[:, columns] = value


def adapter_product(owner_of, adapters, rows, deps):
    (owners, rank, features), row_count = adapters.shape, rows.shape[0]
    tile = min(256, row_count)
    return pl.pallas_call(
        behind(functools.partial(product_kernel, owners, rank, tile), deps),
        grid=(row_count // tile,),
        in_specs=[ANY] * len(deps)
        + [
            SMEM,
            pl.BlockSpec((owners * rank, features), lambda i: (0, 0)),
            pl.BlockSpec((tile, features), lambda i: (i, 0)),
        ],
        out_specs=pl.BlockSpec((rank, tile), lambda i: (0, i)),
        out_shape=jax.ShapeDtypeStruct((rank, row_count), jnp.float32),
        compiler_params=params(),
        cost_estimate=cost(5),
        name="adapter_product",
    )(*deps, owner_of, adapters.reshape(owners * rank, features), rows)


def encode(product, kind):
    if kind != jnp.int16:
        return product.astype(kind)
    top = jnp.maximum(jnp.max(jnp.abs(product), axis=1, keepdims=True), 1e-30)
    level = jnp.floor(jnp.log2(top) * LEVELS) + 2.0
    coded = jnp.round(product * (TOP_CODE * jnp.exp2(level * (-1.0 / LEVELS))))
    coded = jnp.clip(coded, -TOP_CODE, TOP_CODE).astype(jnp.int32).astype(jnp.int16)
    lanes = jnp.broadcast_to(level, (product.shape[0], LEVEL_LANES))
    return jnp.concatenate([coded, lanes.astype(jnp.int32).astype(jnp.int16)], axis=1)


def message_lanes(half, kind):
    return half + (LEVEL_LANES if kind == jnp.int16 else 0)


def outer_kernel(owners, rank, terms, scale_in, scale_out, place, owner_of, *refs):
    sums, rows, theirs, wide = refs[:terms], refs[terms], refs[terms + 1], refs[terms + 2]
    total = sums[0][...]
    for t in range(1, terms):
        total = total + sums[t][...]
    value = (scale_in * total).astype(jnp.bfloat16)
    for b in range(value.shape[1] // BLK_ROWS):
        columns = slice(b * BLK_ROWS, (b + 1) * BLK_ROWS)
        for d in range(owners):
            kept = jnp.where(owner_of[b] == d, value[:, columns], jnp.zeros_like(value[:, columns]))
            wide[d * rank : (d + 1) * rank, columns] = kept
    product = scale_out * jnp.dot(wide[...], rows[...], preferred_element_type=jnp.float32)
    theirs[...] = encode(product, theirs.dtype).reshape(theirs.shape)


def gradient_theirs(place, owner_of, sums, rows, owners, half, scale_in, scale_out, kind, deps):
    rank, row_count = sums[0].shape
    lanes = message_lanes(half, kind)
    whole = pl.BlockSpec((rank, row_count), lambda i, place, owner_of: (0, 0))
    return pl.pallas_call(
        behind(
            functools.partial(outer_kernel, owners, rank, len(sums), scale_in, scale_out), deps, 2
        ),
        grid_spec=pltpu.PrefetchScalarGridSpec(
            num_scalar_prefetch=2,
            grid=(1,),
            in_specs=[ANY] * len(deps)
            + [whole] * len(sums)
            + [pl.BlockSpec((row_count, half), lambda i, place, owner_of: (0, 1 - place[1]))],
            out_specs=[
                pl.BlockSpec((owners, rank, lanes), lambda i, place, owner_of: (0, 0, 0)),
                pl.BlockSpec((owners * rank, row_count), lambda i, place, owner_of: (0, 0)),
            ],
        ),
        out_shape=[
            jax.ShapeDtypeStruct((owners, rank, lanes), kind),
            jax.ShapeDtypeStruct((owners * rank, row_count), jnp.bfloat16),
        ],
        compiler_params=params(),
        cost_estimate=cost(2),
        name="gradient_theirs",
    )(place, owner_of, *deps, *sums, rows)


def message_kernel(owners, rank, scale_out, place, wide, rows, theirs, out):
    product = scale_out * jnp.dot(wide[...], rows[...], preferred_element_type=jnp.float32)
    coded = encode(product, theirs.dtype)
    for d in range(owners):
        out[d, 0] = coded[d * rank : (d + 1) * rank, :]
        out[d, 1] = theirs[d]


def gradient_messages(place, wide, rows, theirs, half, scale_out, deps):
    owners, rank, lanes = theirs.shape
    row_count = rows.shape[0]
    return pl.pallas_call(
        behind(functools.partial(message_kernel, owners, rank, scale_out), deps, 1),
        grid_spec=pltpu.PrefetchScalarGridSpec(
            num_scalar_prefetch=1,
            grid=(1,),
            in_specs=[ANY] * len(deps)
            + [
                pl.BlockSpec(wide.shape, lambda i, place: (0, 0)),
                pl.BlockSpec((row_count, half), lambda i, place: (0, place[1])),
                pl.BlockSpec((owners, rank, lanes), lambda i, place: (0, 0, 0)),
            ],
            out_specs=pl.BlockSpec((owners, 2, rank, lanes), lambda i, place: (0, 0, 0, 0)),
        ),
        out_shape=jax.ShapeDtypeStruct((owners, 2, rank, lanes), theirs.dtype),
        compiler_params=params(),
        cost_estimate=cost(2.4),
        name="gradient_messages",
    )(place, *deps, wide, rows, theirs)


def share_kernel(spans, keep, rows, weight, *outs):
    if keep:

        @pl.when(pl.program_id(0) == 0)
        def _():
            outs[-1][...] = rows[...]

    product = jnp.dot(rows[...], weight[...], preferred_element_type=jnp.float32)
    for out, (start, count) in zip(outs, spans):
        out[...] = product[start : start + count, :].astype(out.dtype)


def share(tokens, weight, piece, start, total, spans, width, keep, deps):
    features = tokens.shape[1]
    tile = min(512, width)
    tiles = width // tile
    return pl.pallas_call(
        behind(functools.partial(share_kernel, spans, keep), deps),
        grid=(tiles,),
        in_specs=[ANY] * len(deps)
        + [
            pl.BlockSpec((total, features), lambda j: (start // total, 0)),
            pl.BlockSpec((features, tile), lambda j: (0, piece * tiles + j)),
        ],
        out_specs=[pl.BlockSpec((count, tile), lambda j: (0, j)) for _, count in spans]
        + [pl.BlockSpec((total, features), lambda j: (0, 0))] * keep,
        out_shape=[jax.ShapeDtypeStruct((count, width), jnp.bfloat16) for _, count in spans]
        + [jax.ShapeDtypeStruct((total, features), jnp.bfloat16)] * keep,
        compiler_params=params(),
        cost_estimate=cost(4.0 * total / 256),
        name="share",
    )(*deps, tokens, weight)


def finish_kernel(flags, spans, mine_is_own, wide, adapters, *refs):
    arrays, out = refs[: len(flags)], refs[-1]
    step = pl.program_id(0)
    total = ADAPTER_SCALE * lax.dot_general(
        wide[...], adapters[...], (((0,), (0,)), ((), ())), preferred_element_type=jnp.float32
    )
    for array, flag, (first, last) in zip(arrays, flags, spans):
        active = jnp.logical_and(step >= first, step < last)
        active = jnp.logical_and(active, mine_is_own[0] == flag)
        total = total + jnp.where(active, array[...].astype(jnp.float32), 0.0)
    out[...] = total.astype(out.dtype)


def finish(mine_is_own, wide, adapters, row_count, start, count, terms, previous, deps):
    (owners, rank, width) = adapters.shape
    tile = min(256, count)
    first = start // tile
    specs, spans = [], []
    for array, row, flag in terms:
        low, many = (row - start) // tile, array.shape[0] // tile

        def block_of(i, mine, low=low, many=many, flag=flag):
            return (jnp.where(mine[0] == flag, jnp.clip(i - low, 0, many - 1), 0), 0)

        specs.append(pl.BlockSpec((tile, width), block_of))
        spans.append((low, low + many))
    operands = [mine_is_own, *deps, wide, adapters.reshape(owners * rank, width)]
    operands += [t[0] for t in terms]
    in_specs = (
        [ANY] * len(deps)
        + [
            pl.BlockSpec((owners * rank, tile), lambda i, mine: (0, first + i)),
            pl.BlockSpec((owners * rank, width), lambda i, mine: (0, 0)),
        ]
        + specs
    )
    aliases = {}
    if previous is not None:
        aliases = {len(operands): 0}
        operands.append(previous)
        in_specs.append(ANY)
    return pl.pallas_call(
        behind(functools.partial(finish_kernel, [t[2] for t in terms], spans), deps, 1),
        grid_spec=pltpu.PrefetchScalarGridSpec(
            num_scalar_prefetch=1,
            grid=(count // tile,),
            in_specs=in_specs,
            out_specs=pl.BlockSpec((tile, width), lambda i, mine: (first + i, 0)),
        ),
        out_shape=jax.ShapeDtypeStruct((row_count, width), jnp.bfloat16),
        input_output_aliases=aliases,
        compiler_params=params(),
        cost_estimate=cost(4),
        name="finish",
    )(*operands)


def adam_kernel(owners, slots, coded, pick, used, corr, param, first, second, messages, *refs):
    levels = refs[0]
    new_param, new_first, new_second, grads = refs[-4:]
    grads[...] = jnp.zeros_like(grads)
    for d in range(owners):
        for c in range(2):
            k = pick[c * owners + d]
            value = messages[d, c].astype(jnp.float32)
            if coded:
                level = levels[d, c].astype(jnp.float32)[:, :1]
                value = value * (jnp.exp2(level * (1.0 / LEVELS)) * (1.0 / TOP_CODE))
            grads[k] = grads[k] + value
    for k in range(slots):
        grad = grads[k]
        one = BETA_ONE * first[k] + (1.0 - BETA_ONE) * grad
        two = BETA_TWO * second[k] + (1.0 - BETA_TWO) * grad * grad
        update = LEARN_RATE * (one / corr[k]) / (jnp.sqrt(two / corr[slots + k]) + ADAM_EPS)
        keep = used[k] == 1
        new_param[k] = jnp.where(keep, param[k] - update, param[k])
        new_first[k] = jnp.where(keep, one, first[k])
        new_second[k] = jnp.where(keep, two, second[k])


def adam(pick, used, corr, param, first, second, messages, deps):
    slots, rank, half = param.shape
    owners = messages.shape[0]
    tile = min(256, half)
    state = pl.BlockSpec((slots, rank, tile), lambda i: (0, 0, i))
    message = pl.BlockSpec((owners, 2, rank, tile), lambda i: (0, 0, 0, i))
    coded = messages.dtype == jnp.int16
    levels = [messages] * coded
    level = pl.BlockSpec(
        (owners, 2, rank, LEVEL_LANES), lambda i: (0, 0, 0, half // LEVEL_LANES)
    )
    return pl.pallas_call(
        behind(functools.partial(adam_kernel, owners, slots, coded), deps),
        grid=(half // tile,),
        in_specs=[ANY] * len(deps) + [SMEM] * 3 + [state] * 3 + [message] + [level] * coded,
        out_specs=[state] * 3,
        out_shape=[dims(param)] * 3,
        scratch_shapes=[pltpu.VMEM((slots, rank, tile), jnp.float32)],
        compiler_params=params(),
        cost_estimate=cost(4),
        name="adam",
    )(*deps, pick, used, corr, param, first, second, messages, *levels)


def on_device(
    tokens,
    frozen_weight,
    cotangent,
    down_adapters,
    up_adapters,
    down_first_moment,
    up_first_moment,
    down_second_moment,
    up_second_moment,
    optimizer_steps,
    slot_of_tenant,
    tenant_of_block,
):
    row_count, din_local = tokens.shape
    width = cotangent.shape[1]
    block_count = row_count // BLK_ROWS
    owners = lax.axis_size("dp")
    cores = lax.axis_size("sub")
    columns = lax.axis_size("tensor")
    z = lax.axis_index("dp")
    s = lax.axis_index("sub")
    x = lax.axis_index("tensor")
    slots, half, rank = down_adapters.shape
    flip = lambda v: jnp.swapaxes(v, 1, 2)
    down_adapters, up_adapters = flip(down_adapters), flip(up_adapters)
    down_first_moment, up_first_moment = flip(down_first_moment), flip(up_first_moment)
    down_second_moment, up_second_moment = flip(down_second_moment), flip(up_second_moment)
    per_half = columns // cores
    place = jnp.stack([z, s]).astype(jnp.int32)

    down_other = rotate(down_adapters, "sub", 1)
    up_other = rotate(up_adapters, "sub", 1)

    def tables(deps):
        return pl.pallas_call(
            behind(functools.partial(tables_kernel, owners, cores, slots, block_count), deps),
            in_specs=[ANY] * len(deps) + [SMEM] * 3,
            out_specs=[SMEM] * 3,
            out_shape=[
                jax.ShapeDtypeStruct((cores * owners,), jnp.int32),
                jax.ShapeDtypeStruct((block_count,), jnp.int32),
                jax.ShapeDtypeStruct((slots,), jnp.int32),
            ],
            cost_estimate=cost(2),
            name="tables",
        )(*deps, place, slot_of_tenant, tenant_of_block)

    steps = (optimizer_steps + 1).astype(jnp.float32)
    corr = jnp.concatenate(
        [
            1.0 - jnp.power(jnp.float32(BETA_ONE), steps),
            1.0 - jnp.power(jnp.float32(BETA_TWO), steps),
        ]
    )

    def pack(own, other, deps):
        return pl.pallas_call(
            behind(functools.partial(pack_kernel, owners), deps),
            in_specs=[ANY] * len(deps) + [SMEM] * 2 + [pl.BlockSpec(memory_space=pltpu.VMEM)] * 2,
            out_specs=pl.BlockSpec(memory_space=pltpu.VMEM),
            out_shape=jax.ShapeDtypeStruct((owners, rank, cores * half), jnp.bfloat16),
            compiler_params=params(),
        cost_estimate=cost(1),
            name="pack",
        )(*deps, place, pick, own, other)

    def spread_out(messages):
        return lax.all_to_all(messages, "dp", split_axis=0, concat_axis=0, tiled=True)

    def shares(rows, start, total, spans, keep, deps):
        pieces = []
        for piece in range(per_half):
            kept = int(keep and piece == 0)
            out = share(rows, frozen_weight, piece, start, total, spans, width, kept, deps)
            pieces.append(out[: len(spans)])
            copy = out[-1] if kept else copy if piece else None
            deps = [pieces[-1][0]]
        chunks = [list(chunk) for chunk in zip(*pieces)]
        return chunks + [copy] if keep else chunks

    def piece_for(chunk, target):
        if per_half == 1:
            return chunk[0]
        out = chunk[0]
        for piece in range(1, per_half):
            out = jnp.where(lax.rem(target, per_half) == piece, chunk[piece], out)
        return out

    def send(chunk, cross):
        got = []
        for step in range(1, columns):
            pairs = []
            for t in range(columns):
                for c in range(cores):
                    target = (t + step) % columns
                    if target // per_half == c:
                        pairs.append((t * cores + c, target * cores + (c + cross) % cores))
            operand = piece_for(chunk, lax.rem(x + step, columns))
            got.append(lax.ppermute(operand, ("tensor", "sub"), pairs))
        return got

    def send_local(chunk):
        pairs = []
        for t in range(columns):
            c = t // per_half
            pairs.append((t * cores + c, t * cores + (c + 1) % cores))
        return lax.ppermute(piece_for(chunk, x), ("tensor", "sub"), pairs)

    def exchange(part):
        return [part] + [rotate(part, "tensor", step) for step in range(1, columns)]

    half_rows = row_count // 2
    one_half = [(0, half_rows)]
    both = one_half * 2
    pick, owner_of, used = tables([])
    down_packed = pack(down_adapters, down_other, [])
    down_arrived = spread_out(down_packed)
    own_a, low_rows = shares(tokens, 0, half_rows, one_half, True, [down_packed])
    got_a = send(own_a, 0)
    other_low = rotate(low_rows, "sub", 1)
    up_packed = pack(up_adapters, up_other, [own_a[-1]])
    own_b, high_rows = shares(tokens, half_rows, half_rows, one_half, True, [up_packed])
    other_high = rotate(high_rows, "sub", 1)
    up_packed, = tie([up_packed], [down_arrived, own_b[-1]])
    up_arrived = spread_out(up_packed)

    down_part = adapter_product(owner_of, down_arrived, tokens, [up_packed])
    down_sums = exchange(down_part)
    own_b = tie(own_b, [down_part])
    got_b = send(own_b, 0)
    cross_a, cross_a_near = shares(other_low, 0, half_rows, both, False, [own_b[-1]])
    local_a = send_local(cross_a_near)
    up_theirs, down_wide = gradient_theirs(
        place, owner_of, down_sums, cotangent, owners, half, 1.0, ADAPTER_SCALE, jnp.bfloat16,
        [cross_a[-1]] + got_a,
    )
    up_swapped = rotate(up_theirs, "sub", 1)
    down_wide, = tie([down_wide], [up_theirs])
    up_messages = gradient_messages(
        place, down_wide, cotangent, up_swapped, half, ADAPTER_SCALE, [up_arrived]
    )
    up_returned = spread_out(up_messages)
    back_part = adapter_product(owner_of, up_arrived, cotangent, [up_messages])
    back_sums = exchange(back_part)
    cross_a = tie(cross_a, [back_part])
    late_a = send(cross_a, 1)
    cross_b, cross_b_near = shares(other_high, 0, half_rows, both, False, [cross_a[-1]])
    down_theirs, back_wide = gradient_theirs(
        place, owner_of, back_sums, tokens, owners, half, ADAPTER_SCALE, 1.0, jnp.int16,
        [cross_b[-1]] + got_b,
    )
    down_swapped = rotate(down_theirs, "sub", 1)
    cross_b = tie(cross_b, [down_theirs])
    late_b = send(cross_b, 1)
    back_wide, = tie([back_wide], [cross_b[-1]])
    down_messages = gradient_messages(
        place, back_wide, tokens, down_swapped, half, 1.0, [up_returned]
    )
    down_returned = spread_out(down_messages)
    cross_b_near = tie(cross_b_near, [down_messages])
    local_b = send_local(cross_b_near)

    fresh_up, fresh_up_first, fresh_up_second = adam(
        pick, used, corr, up_adapters, up_first_moment, up_second_moment, up_returned,
        [cross_b_near[-1]],
    )
    mine_is_own = (lax.div(x, per_half) == s).astype(jnp.int32).reshape(1)
    terms_a = [(piece_for(own_a, x), 0, 1), (local_a, 0, 0)]
    terms_a += [(g, 0, 1) for g in got_a] + [(g, 0, 0) for g in late_a]
    terms_b = [(piece_for(own_b, x), half_rows, 1), (local_b, half_rows, 0)]
    terms_b += [(g, half_rows, 1) for g in got_b] + [(g, half_rows, 0) for g in late_b]
    projected = finish(
        mine_is_own, down_wide, up_arrived, row_count, 0, half_rows, terms_a, None, [fresh_up]
    )
    projected = finish(
        mine_is_own, down_wide, up_arrived, row_count, half_rows, half_rows, terms_b, projected,
        [],
    )
    fresh_down, fresh_down_first, fresh_down_second = adam(
        pick, used, corr, down_adapters, down_first_moment, down_second_moment, down_returned,
        [projected],
    )
    return (
        projected,
        flip(fresh_down),
        flip(fresh_up),
        flip(fresh_down_first),
        flip(fresh_up_first),
        flip(fresh_down_second),
        flip(fresh_up_second),
    )


def solution(mesh):
    placed = (
        P(("groups", "dp", "sub"), "tensor"),
        P("tensor", "sub"),
        P(("groups", "dp", "sub"), "tensor"),
        P(("groups", "dp"), ("tensor", "sub"), None),
        P(("groups", "dp"), ("tensor", "sub"), None),
        P(("groups", "dp"), ("tensor", "sub"), None),
        P(("groups", "dp"), ("tensor", "sub"), None),
        P(("groups", "dp"), ("tensor", "sub"), None),
        P(("groups", "dp"), ("tensor", "sub"), None),
        P(("groups", "dp")),
        P("groups"),
        P("groups"),
    )
    return jax.shard_map(
        on_device,
        mesh=mesh,
        in_specs=placed,
        out_specs=(
            P(("groups", "dp", "sub"), "tensor"),
            P(("groups", "dp"), ("tensor", "sub"), None),
            P(("groups", "dp"), ("tensor", "sub"), None),
            P(("groups", "dp"), ("tensor", "sub"), None),
            P(("groups", "dp"), ("tensor", "sub"), None),
            P(("groups", "dp"), ("tensor", "sub"), None),
            P(("groups", "dp"), ("tensor", "sub"), None),
        ),
        check_vma=False,
    )
```

```python
import functools

import jax
import jax.numpy as jnp
from jax import lax
from jax.experimental import pallas as pl
from jax.experimental.pallas import tpu as pltpu
from jax.sharding import PartitionSpec as P

BLK_ROWS = 128


ADAPTER_SCALE = 2.0
BETA_ONE = 0.9
BETA_TWO = 0.999
LEARN_RATE = 0.01
ADAM_EPS = 1e-08

SMEM = pl.BlockSpec(memory_space=pltpu.SMEM)
VMEM_BYTES = 24 * 1024 * 1024
TOP_CODE = 32767.0
LEVELS = 64.0
LEVEL_LANES = 128
COST = 20.0


def params():
    return pltpu.CompilerParams(vmem_limit_bytes=VMEM_BYTES)


def cost(micros):
    flops = int(micros * 1_000_000_000 * COST)
    return pl.CostEstimate(flops=flops, bytes_accessed=1000, transcendentals=0)


def rotate(value, axis, shift):
    size = lax.axis_size(axis)
    return lax.ppermute(value, axis, [(i, (i + shift) % size) for i in range(size)])


ANY = pl.BlockSpec(memory_space=pl.ANY)


def behind(kernel, deps, scalars=0):
    return lambda *refs: kernel(*refs[:scalars], *refs[scalars + len(deps) :])


def tie_kernel(*refs):
    pass


def tie(values, deps):
    return pl.pallas_call(
        tie_kernel,
        in_specs=[ANY] * (len(values) + len(deps)),
        out_specs=[ANY] * len(values),
        out_shape=[dims(v) for v in values],
        input_output_aliases={k: k for k in range(len(values))},
        cost_estimate=cost(100),
        name="tie",
    )(*values, *deps)


def dims(value):
    return jax.ShapeDtypeStruct(value.shape, value.dtype)


def tables_kernel(owners, cores, slots, block_count, place, slot_of, tenant_of, pick, owner_of, used):
    z, s = place[0], place[1]
    for k in range(slots):
        used[k] = 0

    def slot_at(device, b):
        return slot_of[tenant_of[device * block_count + b]]

    def per_device(i, carry):
        c, d = lax.div(i, owners), lax.rem(i, owners)
        device = d * cores + lax.rem(s + c, cores)

        def per_block(b, found):
            local = slot_at(device, b) - z * slots
            mine = jnp.logical_and(local >= 0, local < slots)

            @pl.when(mine)
            def _():
                used[local] = 1

            return jnp.where(mine, local, found)

        pick[i] = lax.fori_loop(0, block_count, per_block, 0)
        return carry

    lax.fori_loop(0, owners * cores, per_device, 0)
    for b in range(block_count):
        owner_of[b] = lax.div(slot_at(z * cores + s, b), slots)


def pack_kernel(owners, place, pick, own, other, out):
    s = place[1]
    half = own.shape[2]
    for d in range(owners):
        k = pick[d]
        near, far = own[k].astype(jnp.bfloat16), other[k].astype(jnp.bfloat16)
        out[d, :, :half] = jnp.where(s == 0, near, far)
        out[d, :, half:] = jnp.where(s == 0, far, near)


def product_kernel(owners, rank, tile_rows, owner_of, adapters, rows, out):
    step = pl.program_id(0)
    full = lax.dot_general(
        adapters[...], rows[...], (((1,), (1,)), ((), ())), preferred_element_type=jnp.float32
    )
    for b in range(tile_rows // BLK_ROWS):
        owner = owner_of[step * (tile_rows // BLK_ROWS) + b]
        columns = slice(b * BLK_ROWS, (b + 1) * BLK_ROWS)
        value = full[:rank, columns]
        for d in range(1, owners):
            value = jnp.where(owner == d, full[d * rank : (d + 1) * rank, columns], value)
        out[:, columns] = value


def adapter_product(owner_of, adapters, rows, deps):
    (owners, rank, features), row_count = adapters.shape, rows.shape[0]
    tile = min(256, row_count)
    return pl.pallas_call(
        behind(functools.partial(product_kernel, owners, rank, tile), deps),
        grid=(row_count // tile,),
        in_specs=[ANY] * len(deps)
        + [
            SMEM,
            pl.BlockSpec((owners * rank, features), lambda i: (0, 0)),
            pl.BlockSpec((tile, features), lambda i: (i, 0)),
        ],
        out_specs=pl.BlockSpec((rank, tile), lambda i: (0, i)),
        out_shape=jax.ShapeDtypeStruct((rank, row_count), jnp.float32),
        compiler_params=params(),
        cost_estimate=cost(5),
        name="adapter_product",
    )(*deps, owner_of, adapters.reshape(owners * rank, features), rows)


def encode(product, kind):
    if kind != jnp.int16:
        return product.astype(kind)
    top = jnp.maximum(jnp.max(jnp.abs(product), axis=1, keepdims=True), 1e-30)
    level = jnp.floor(jnp.log2(top) * LEVELS) + 2.0
    coded = jnp.round(product * (TOP_CODE * jnp.exp2(level * (-1.0 / LEVELS))))
    coded = jnp.clip(coded, -TOP_CODE, TOP_CODE).astype(jnp.int32).astype(jnp.int16)
    lanes = jnp.broadcast_to(level, (product.shape[0], LEVEL_LANES))
    return jnp.concatenate([coded, lanes.astype(jnp.int32).astype(jnp.int16)], axis=1)


def message_lanes(half, kind):
    return half + (LEVEL_LANES if kind == jnp.int16 else 0)


def outer_kernel(owners, rank, terms, scale_in, scale_out, place, owner_of, *refs):
    sums, rows, theirs, wide = refs[:terms], refs[terms], refs[terms + 1], refs[terms + 2]
    total = sums[0][...]
    for t in range(1, terms):
        total = total + sums[t][...]
    value = (scale_in * total).astype(jnp.bfloat16)
    for b in range(value.shape[1] // BLK_ROWS):
        columns = slice(b * BLK_ROWS, (b + 1) * BLK_ROWS)
        for d in range(owners):
            kept = jnp.where(owner_of[b] == d, value[:, columns], jnp.zeros_like(value[:, columns]))
            wide[d * rank : (d + 1) * rank, columns] = kept
    product = scale_out * jnp.dot(wide[...], rows[...], preferred_element_type=jnp.float32)
    theirs[...] = encode(product, theirs.dtype).reshape(theirs.shape)


def gradient_theirs(place, owner_of, sums, rows, owners, half, scale_in, scale_out, kind, deps):
    rank, row_count = sums[0].shape
    lanes = message_lanes(half, kind)
    whole = pl.BlockSpec((rank, row_count), lambda i, place, owner_of: (0, 0))
    return pl.pallas_call(
        behind(
            functools.partial(outer_kernel, owners, rank, len(sums), scale_in, scale_out), deps, 2
        ),
        grid_spec=pltpu.PrefetchScalarGridSpec(
            num_scalar_prefetch=2,
            grid=(1,),
            in_specs=[ANY] * len(deps)
            + [whole] * len(sums)
            + [pl.BlockSpec((row_count, half), lambda i, place, owner_of: (0, 1 - place[1]))],
            out_specs=[
                pl.BlockSpec((owners, rank, lanes), lambda i, place, owner_of: (0, 0, 0)),
                pl.BlockSpec((owners * rank, row_count), lambda i, place, owner_of: (0, 0)),
            ],
        ),
        out_shape=[
            jax.ShapeDtypeStruct((owners, rank, lanes), kind),
            jax.ShapeDtypeStruct((owners * rank, row_count), jnp.bfloat16),
        ],
        compiler_params=params(),
        cost_estimate=cost(2),
        name="gradient_theirs",
    )(place, owner_of, *deps, *sums, rows)


def message_kernel(owners, rank, scale_out, place, wide, rows, theirs, out):
    product = scale_out * jnp.dot(wide[...], rows[...], preferred_element_type=jnp.float32)
    coded = encode(product, theirs.dtype)
    for d in range(owners):
        out[d, 0] = coded[d * rank : (d + 1) * rank, :]
        out[d, 1] = theirs[d]


def gradient_messages(place, wide, rows, theirs, half, scale_out, deps):
    owners, rank, lanes = theirs.shape
    row_count = rows.shape[0]
    return pl.pallas_call(
        behind(functools.partial(message_kernel, owners, rank, scale_out), deps, 1),
        grid_spec=pltpu.PrefetchScalarGridSpec(
            num_scalar_prefetch=1,
            grid=(1,),
            in_specs=[ANY] * len(deps)
            + [
                pl.BlockSpec(wide.shape, lambda i, place: (0, 0)),
                pl.BlockSpec((row_count, half), lambda i, place: (0, place[1])),
                pl.BlockSpec((owners, rank, lanes), lambda i, place: (0, 0, 0)),
            ],
            out_specs=pl.BlockSpec((owners, 2, rank, lanes), lambda i, place: (0, 0, 0, 0)),
        ),
        out_shape=jax.ShapeDtypeStruct((owners, 2, rank, lanes), theirs.dtype),
        compiler_params=params(),
        cost_estimate=cost(2.4),
        name="gradient_messages",
    )(place, *deps, wide, rows, theirs)


def share_kernel(spans, keep, rows, weight, *outs):
    if keep:

        @pl.when(pl.program_id(0) == 0)
        def _():
            outs[-1][...] = rows[...]

    product = jnp.dot(rows[...], weight[...], preferred_element_type=jnp.float32)
    for out, (start, count) in zip(outs, spans):
        out[...] = product[start : start + count, :].astype(out.dtype)


def share(tokens, weight, piece, start, total, spans, width, keep, deps):
    features = tokens.shape[1]
    tile = min(512, width)
    tiles = width // tile
    return pl.pallas_call(
        behind(functools.partial(share_kernel, spans, keep), deps),
        grid=(tiles,),
        in_specs=[ANY] * len(deps)
        + [
            pl.BlockSpec((total, features), lambda j: (start // total, 0)),
            pl.BlockSpec((features, tile), lambda j: (0, piece * tiles + j)),
        ],
        out_specs=[pl.BlockSpec((count, tile), lambda j: (0, j)) for _, count in spans]
        + [pl.BlockSpec((total, features), lambda j: (0, 0))] * keep,
        out_shape=[jax.ShapeDtypeStruct((count, width), jnp.bfloat16) for _, count in spans]
        + [jax.ShapeDtypeStruct((total, features), jnp.bfloat16)] * keep,
        compiler_params=params(),
        cost_estimate=cost(4.0 * total / 256),
        name="share",
    )(*deps, tokens, weight)


def finish_kernel(flags, spans, mine_is_own, wide, adapters, *refs):
    arrays, out = refs[: len(flags)], refs[-1]
    step = pl.program_id(0)
    total = ADAPTER_SCALE * lax.dot_general(
        wide[...], adapters[...], (((0,), (0,)), ((), ())), preferred_element_type=jnp.float32
    )
    for array, flag, (first, last) in zip(arrays, flags, spans):
        active = jnp.logical_and(step >= first, step < last)
        active = jnp.logical_and(active, mine_is_own[0] == flag)
        total = total + jnp.where(active, array[...].astype(jnp.float32), 0.0)
    out[...] = total.astype(out.dtype)


def finish(mine_is_own, wide, adapters, row_count, start, count, terms, previous, deps):
    (owners, rank, width) = adapters.shape
    tile = min(256, count)
    first = start // tile
    specs, spans = [], []
    for array, row, flag in terms:
        low, many = (row - start) // tile, array.shape[0] // tile

        def block_of(i, mine, low=low, many=many, flag=flag):
            return (jnp.where(mine[0] == flag, jnp.clip(i - low, 0, many - 1), 0), 0)

        specs.append(pl.BlockSpec((tile, width), block_of))
        spans.append((low, low + many))
    operands = [mine_is_own, *deps, wide, adapters.reshape(owners * rank, width)]
    operands += [t[0] for t in terms]
    in_specs = (
        [ANY] * len(deps)
        + [
            pl.BlockSpec((owners * rank, tile), lambda i, mine: (0, first + i)),
            pl.BlockSpec((owners * rank, width), lambda i, mine: (0, 0)),
        ]
        + specs
    )
    aliases = {}
    if previous is not None:
        aliases = {len(operands): 0}
        operands.append(previous)
        in_specs.append(ANY)
    return pl.pallas_call(
        behind(functools.partial(finish_kernel, [t[2] for t in terms], spans), deps, 1),
        grid_spec=pltpu.PrefetchScalarGridSpec(
            num_scalar_prefetch=1,
            grid=(count // tile,),
            in_specs=in_specs,
            out_specs=pl.BlockSpec((tile, width), lambda i, mine: (first + i, 0)),
        ),
        out_shape=jax.ShapeDtypeStruct((row_count, width), jnp.bfloat16),
        input_output_aliases=aliases,
        compiler_params=params(),
        cost_estimate=cost(4),
        name="finish",
    )(*operands)


def adam_kernel(owners, slots, coded, pick, used, corr, param, first, second, messages, *refs):
    levels = refs[0]
    new_param, new_first, new_second, grads = refs[-4:]
    grads[...] = jnp.zeros_like(grads)
    for d in range(owners):
        for c in range(2):
            k = pick[c * owners + d]
            value = messages[d, c].astype(jnp.float32)
            if coded:
                level = levels[d, c].astype(jnp.float32)[:, :1]
                value = value * (jnp.exp2(level * (1.0 / LEVELS)) * (1.0 / TOP_CODE))
            grads[k] = grads[k] + value
    for k in range(slots):
        grad = grads[k]
        one = BETA_ONE * first[k] + (1.0 - BETA_ONE) * grad
        two = BETA_TWO * second[k] + (1.0 - BETA_TWO) * grad * grad
        update = LEARN_RATE * (one / corr[k]) / (jnp.sqrt(two / corr[slots + k]) + ADAM_EPS)
        keep = used[k] == 1
        new_param[k] = jnp.where(keep, param[k] - update, param[k])
        new_first[k] = jnp.where(keep, one, first[k])
        new_second[k] = jnp.where(keep, two, second[k])


def adam(pick, used, corr, param, first, second, messages, deps):
    slots, rank, half = param.shape
    owners = messages.shape[0]
    tile = min(256, half)
    state = pl.BlockSpec((slots, rank, tile), lambda i: (0, 0, i))
    message = pl.BlockSpec((owners, 2, rank, tile), lambda i: (0, 0, 0, i))
    coded = messages.dtype == jnp.int16
    levels = [messages] * coded
    level = pl.BlockSpec(
        (owners, 2, rank, LEVEL_LANES), lambda i: (0, 0, 0, half // LEVEL_LANES)
    )
    return pl.pallas_call(
        behind(functools.partial(adam_kernel, owners, slots, coded), deps),
        grid=(half // tile,),
        in_specs=[ANY] * len(deps) + [SMEM] * 3 + [state] * 3 + [message] + [level] * coded,
        out_specs=[state] * 3,
        out_shape=[dims(param)] * 3,
        scratch_shapes=[pltpu.VMEM((slots, rank, tile), jnp.float32)],
        compiler_params=params(),
        cost_estimate=cost(4),
        name="adam",
    )(*deps, pick, used, corr, param, first, second, messages, *levels)


def on_device(
    tokens,
    frozen_weight,
    cotangent,
    down_adapters,
    up_adapters,
    down_first_moment,
    up_first_moment,
    down_second_moment,
    up_second_moment,
    optimizer_steps,
    slot_of_tenant,
    tenant_of_block,
):
    row_count, din_local = tokens.shape
    width = cotangent.shape[1]
    block_count = row_count // BLK_ROWS
    owners = lax.axis_size("dp")
    cores = lax.axis_size("sub")
    columns = lax.axis_size("tensor")
    z = lax.axis_index("dp")
    s = lax.axis_index("sub")
    x = lax.axis_index("tensor")
    slots, half, rank = down_adapters.shape
    flip = lambda v: jnp.swapaxes(v, 1, 2)
    down_adapters, up_adapters = flip(down_adapters), flip(up_adapters)
    down_first_moment, up_first_moment = flip(down_first_moment), flip(up_first_moment)
    down_second_moment, up_second_moment = flip(down_second_moment), flip(up_second_moment)
    per_half = columns // cores
    place = jnp.stack([z, s]).astype(jnp.int32)

    down_other = rotate(down_adapters, "sub", 1)
    up_other = rotate(up_adapters, "sub", 1)

    def tables(deps):
        return pl.pallas_call(
            behind(functools.partial(tables_kernel, owners, cores, slots, block_count), deps),
            in_specs=[ANY] * len(deps) + [SMEM] * 3,
            out_specs=[SMEM] * 3,
            out_shape=[
                jax.ShapeDtypeStruct((cores * owners,), jnp.int32),
                jax.ShapeDtypeStruct((block_count,), jnp.int32),
                jax.ShapeDtypeStruct((slots,), jnp.int32),
            ],
            cost_estimate=cost(2),
            name="tables",
        )(*deps, place, slot_of_tenant, tenant_of_block)

    steps = (optimizer_steps + 1).astype(jnp.float32)
    corr = jnp.concatenate(
        [
            1.0 - jnp.power(jnp.float32(BETA_ONE), steps),
            1.0 - jnp.power(jnp.float32(BETA_TWO), steps),
        ]
    )

    def pack(own, other, deps):
        return pl.pallas_call(
            behind(functools.partial(pack_kernel, owners), deps),
            in_specs=[ANY] * len(deps) + [SMEM] * 2 + [pl.BlockSpec(memory_space=pltpu.VMEM)] * 2,
            out_specs=pl.BlockSpec(memory_space=pltpu.VMEM),
            out_shape=jax.ShapeDtypeStruct((owners, rank, cores * half), jnp.bfloat16),
            compiler_params=params(),
        cost_estimate=cost(1),
            name="pack",
        )(*deps, place, pick, own, other)

    def spread_out(messages):
        return lax.all_to_all(messages, "dp", split_axis=0, concat_axis=0, tiled=True)

    def shares(rows, start, total, spans, keep, deps):
        pieces = []
        for piece in range(per_half):
            kept = int(keep and piece == 0)
            out = share(rows, frozen_weight, piece, start, total, spans, width, kept, deps)
            pieces.append(out[: len(spans)])
            copy = out[-1] if kept else copy if piece else None
            deps = [pieces[-1][0]]
        chunks = [list(chunk) for chunk in zip(*pieces)]
        return chunks + [copy] if keep else chunks

    def piece_for(chunk, target):
        if per_half == 1:
            return chunk[0]
        out = chunk[0]
        for piece in range(1, per_half):
            out = jnp.where(lax.rem(target, per_half) == piece, chunk[piece], out)
        return out

    def send(chunk, cross):
        got = []
        for step in range(1, columns):
            pairs = []
            for t in range(columns):
                for c in range(cores):
                    target = (t + step) % columns
                    if target // per_half == c:
                        pairs.append((t * cores + c, target * cores + (c + cross) % cores))
            operand = piece_for(chunk, lax.rem(x + step, columns))
            got.append(lax.ppermute(operand, ("tensor", "sub"), pairs))
        return got

    def send_local(chunk):
        pairs = []
        for t in range(columns):
            c = t // per_half
            pairs.append((t * cores + c, t * cores + (c + 1) % cores))
        return lax.ppermute(piece_for(chunk, x), ("tensor", "sub"), pairs)

    def exchange(part):
        return [part] + [rotate(part, "tensor", step) for step in range(1, columns)]

    half_rows = row_count // 2
    one_half = [(0, half_rows)]
    both = one_half * 2
    pick, owner_of, used = tables([])
    down_packed = pack(down_adapters, down_other, [])
    down_arrived = spread_out(down_packed)
    own_a, low_rows = shares(tokens, 0, half_rows, one_half, True, [down_packed])
    got_a = send(own_a, 0)
    other_low = rotate(low_rows, "sub", 1)
    up_packed = pack(up_adapters, up_other, [own_a[-1]])
    own_b, high_rows = shares(tokens, half_rows, half_rows, one_half, True, [up_packed])
    other_high = rotate(high_rows, "sub", 1)
    up_packed, = tie([up_packed], [down_arrived, own_b[-1]])
    up_arrived = spread_out(up_packed)

    down_part = adapter_product(owner_of, down_arrived, tokens, [up_packed])
    down_sums = exchange(down_part)
    own_b = tie(own_b, [down_part])
    got_b = send(own_b, 0)
    cross_a, cross_a_near = shares(other_low, 0, half_rows, both, False, [own_b[-1]])
    local_a = send_local(cross_a_near)
    up_theirs, down_wide = gradient_theirs(
        place, owner_of, down_sums, cotangent, owners, half, 1.0, ADAPTER_SCALE, jnp.bfloat16,
        [cross_a[-1]] + got_a,
    )
    up_swapped = rotate(up_theirs, "sub", 1)
    down_wide, = tie([down_wide], [up_theirs])
    up_messages = gradient_messages(
        place, down_wide, cotangent, up_swapped, half, ADAPTER_SCALE, [up_arrived]
    )
    up_returned = spread_out(up_messages)
    back_part = adapter_product(owner_of, up_arrived, cotangent, [up_messages])
    back_sums = exchange(back_part)
    cross_a = tie(cross_a, [back_part])
    late_a = send(cross_a, 1)
    cross_b, cross_b_near = shares(other_high, 0, half_rows, both, False, [cross_a[-1]])
    down_theirs, back_wide = gradient_theirs(
        place, owner_of, back_sums, tokens, owners, half, ADAPTER_SCALE, 1.0, jnp.int16,
        [cross_b[-1]] + got_b,
    )
    down_swapped = rotate(down_theirs, "sub", 1)
    cross_b = tie(cross_b, [down_theirs])
    late_b = send(cross_b, 1)
    back_wide, = tie([back_wide], [cross_b[-1]])
    down_messages = gradient_messages(
        place, back_wide, tokens, down_swapped, half, 1.0, [up_returned]
    )
    down_returned = spread_out(down_messages)
    cross_b_near = tie(cross_b_near, [down_messages])
    local_b = send_local(cross_b_near)

    fresh_up, fresh_up_first, fresh_up_second = adam(
        pick, used, corr, up_adapters, up_first_moment, up_second_moment, up_returned,
        [cross_b_near[-1]],
    )
    mine_is_own = (lax.div(x, per_half) == s).astype(jnp.int32).reshape(1)
    terms_a = [(piece_for(own_a, x), 0, 1), (local_a, 0, 0)]
    terms_a += [(g, 0, 1) for g in got_a] + [(g, 0, 0) for g in late_a]
    terms_b = [(piece_for(own_b, x), half_rows, 1), (local_b, half_rows, 0)]
    terms_b += [(g, half_rows, 1) for g in got_b] + [(g, half_rows, 0) for g in late_b]
    projected = finish(
        mine_is_own, down_wide, up_arrived, row_count, 0, half_rows, terms_a, None, [fresh_up]
    )
    projected = finish(
        mine_is_own, down_wide, up_arrived, row_count, half_rows, half_rows, terms_b, projected,
        [],
    )
    fresh_down, fresh_down_first, fresh_down_second = adam(
        pick, used, corr, down_adapters, down_first_moment, down_second_moment, down_returned,
        [projected],
    )
    return (
        projected,
        flip(fresh_down),
        flip(fresh_up),
        flip(fresh_down_first),
        flip(fresh_up_first),
        flip(fresh_down_second),
        flip(fresh_up_second),
    )


def solution(mesh):
    placed = (
        P(("groups", "dp", "sub"), "tensor"),
        P("tensor", "sub"),
        P(("groups", "dp", "sub"), "tensor"),
        P(("groups", "dp"), ("tensor", "sub"), None),
        P(("groups", "dp"), ("tensor", "sub"), None),
        P(("groups", "dp"), ("tensor", "sub"), None),
        P(("groups", "dp"), ("tensor", "sub"), None),
        P(("groups", "dp"), ("tensor", "sub"), None),
        P(("groups", "dp"), ("tensor", "sub"), None),
        P(("groups", "dp")),
        P("groups"),
        P("groups"),
    )
    return jax.shard_map(
        on_device,
        mesh=mesh,
        in_specs=placed,
        out_specs=(
            P(("groups", "dp", "sub"), "tensor"),
            P(("groups", "dp"), ("tensor", "sub"), None),
            P(("groups", "dp"), ("tensor", "sub"), None),
            P(("groups", "dp"), ("tensor", "sub"), None),
            P(("groups", "dp"), ("tensor", "sub"), None),
            P(("groups", "dp"), ("tensor", "sub"), None),
            P(("groups", "dp"), ("tensor", "sub"), None),
        ),
        check_vma=False,
    )
```

```python
import functools

import jax
import jax.numpy as jnp
from jax import lax
from jax.experimental import pallas as pl
from jax.experimental.pallas import tpu as pltpu
from jax.sharding import PartitionSpec as P

BLK_ROWS = 128


ADAPTER_SCALE = 2.0
BETA_ONE = 0.9
BETA_TWO = 0.999
LEARN_RATE = 0.01
ADAM_EPS = 1e-08

SMEM = pl.BlockSpec(memory_space=pltpu.SMEM)
VMEM_BYTES = 63_000_000
TOP_CODE = 32767.0
LEVELS = 64.0
LEVEL_LANES = 128
COST = 20.0


def params():
    return pltpu.CompilerParams(vmem_limit_bytes=VMEM_BYTES)


def cost(micros):
    flops = int(micros * 1_000_000_000 * COST)
    return pl.CostEstimate(flops=flops, bytes_accessed=1000, transcendentals=0)


def rotate(value, axis, shift):
    size = lax.axis_size(axis)
    return lax.ppermute(value, axis, [(i, (i + shift) % size) for i in range(size)])


ANY = pl.BlockSpec(memory_space=pl.ANY)


def behind(kernel, deps, scalars=0):
    return lambda *refs: kernel(*refs[:scalars], *refs[scalars + len(deps) :])


def tie_kernel(*refs):
    pass


def tie(values, deps):
    return pl.pallas_call(
        tie_kernel,
        in_specs=[ANY] * (len(values) + len(deps)),
        out_specs=[ANY] * len(values),
        out_shape=[dims(v) for v in values],
        input_output_aliases={k: k for k in range(len(values))},
        cost_estimate=cost(100),
        name="tie",
    )(*values, *deps)


def dims(value):
    return jax.ShapeDtypeStruct(value.shape, value.dtype)


def tables_kernel(devices, cores, slots, block_count, place, slot_of, tenant_of, pick, owner_of, used):
    z, s = place[0], place[1]
    for k in range(slots):
        used[k] = 0

    def slot_at(device, b):
        return slot_of[tenant_of[device * block_count + b]]

    def per_device(device, carry):
        def per_block(b, found):
            local = slot_at(device, b) - z * slots
            mine = jnp.logical_and(local >= 0, local < slots)

            @pl.when(mine)
            def _():
                used[local] = 1

            return jnp.where(mine, local, found)

        pick[device] = lax.fori_loop(0, block_count, per_block, 0)
        return carry

    lax.fori_loop(0, devices, per_device, 0)
    for b in range(block_count):
        owner_of[b] = lax.div(slot_at(z * cores + s, b), slots)


def pack_kernel(devices, pick, own, out):
    for device in range(devices):
        out[device] = own[pick[device]].astype(jnp.bfloat16)


def product_kernel(owners, cores, rank, tile_rows, owner_of, *refs):
    halves, (rows, out, turned) = refs[:cores], refs[cores:]
    step = pl.program_id(0)
    half = turned.shape[0] // cores

    @pl.when(step == 0)
    def _():
        for h in range(cores):
            flat = halves[h][...].reshape(owners * rank, half)
            turned[h * half : (h + 1) * half, :] = flat.T

    full = jnp.dot(rows[...], turned[...], preferred_element_type=jnp.float32)
    for b in range(tile_rows // BLK_ROWS):
        owner = owner_of[step * (tile_rows // BLK_ROWS) + b]
        span = slice(b * BLK_ROWS, (b + 1) * BLK_ROWS)
        value = full[span, :rank]
        for d in range(1, owners):
            value = jnp.where(owner == d, full[span, d * rank : (d + 1) * rank], value)
        out[:, span] = value.T


def halves_specs(owners, cores, rank, half):
    return [
        pl.BlockSpec((owners, None, rank, half), lambda *ids, h=h: (0, h, 0, 0))
        for h in range(cores)
    ]


def adapter_product(owner_of, adapters, rows, deps):
    (owners, cores, rank, half), (row_count, features) = adapters.shape, rows.shape
    tile = min(256, row_count)
    return pl.pallas_call(
        behind(functools.partial(product_kernel, owners, cores, rank, tile), deps),
        grid=(row_count // tile,),
        in_specs=[ANY] * len(deps)
        + [SMEM]
        + halves_specs(owners, cores, rank, half)
        + [pl.BlockSpec((tile, features), lambda i: (i, 0))],
        out_specs=pl.BlockSpec((rank, tile), lambda i: (0, i)),
        out_shape=jax.ShapeDtypeStruct((rank, row_count), jnp.float32),
        scratch_shapes=[pltpu.VMEM((features, owners * rank), jnp.bfloat16)],
        compiler_params=params(),
        cost_estimate=cost(5),
        name="adapter_product",
    )(*deps, owner_of, *[adapters] * cores, rows)


def encode(product, kind):
    if kind != jnp.int16:
        return product.astype(kind)
    top = jnp.maximum(jnp.max(jnp.abs(product), axis=1, keepdims=True), 1e-30)
    level = jnp.floor(jnp.log2(top) * LEVELS) + 2.0
    coded = jnp.round(product * (TOP_CODE * jnp.exp2(level * (-1.0 / LEVELS))))
    coded = jnp.clip(coded, -TOP_CODE, TOP_CODE).astype(jnp.int32).astype(jnp.int16)
    lanes = jnp.broadcast_to(level, (product.shape[0], LEVEL_LANES))
    return jnp.concatenate([coded, lanes.astype(jnp.int32).astype(jnp.int16)], axis=1)


def gradient_kernel(owners, rank, terms, scale_in, scale_out, owner_of, *refs):
    sums, (rows, out, wide) = refs[:terms], refs[terms:]

    @pl.when(pl.program_id(0) == 0)
    def _():
        total = sums[0][...]
        for t in range(1, terms):
            total = total + sums[t][...]
        value = (scale_in * total).astype(jnp.bfloat16)
        for b in range(value.shape[1] // BLK_ROWS):
            span = slice(b * BLK_ROWS, (b + 1) * BLK_ROWS)
            for d in range(owners):
                kept = jnp.where(owner_of[b] == d, value[:, span], jnp.zeros_like(value[:, span]))
                wide[d * rank : (d + 1) * rank, span] = kept

    product = scale_out * jnp.dot(wide[...], rows[...], preferred_element_type=jnp.float32)
    out[...] = encode(product, out.dtype).reshape(out.shape)


def gradients(owner_of, sums, rows, owners, half, scale_in, scale_out, kind, deps):
    rank, row_count = sums[0].shape
    cores = rows.shape[1] // half
    lanes = half + (LEVEL_LANES if kind == jnp.int16 else 0)
    whole = pl.BlockSpec((rank, row_count), lambda h: (0, 0))
    return pl.pallas_call(
        behind(
            functools.partial(gradient_kernel, owners, rank, len(sums), scale_in, scale_out), deps
        ),
        grid=(cores,),
        in_specs=[ANY] * len(deps)
        + [SMEM]
        + [whole] * len(sums)
        + [pl.BlockSpec((row_count, half), lambda h: (0, h))],
        out_specs=[
            pl.BlockSpec((owners, None, rank, lanes), lambda h: (0, h, 0, 0)),
            pl.BlockSpec((owners * rank, row_count), lambda h: (0, 0)),
        ],
        out_shape=[
            jax.ShapeDtypeStruct((owners, cores, rank, lanes), kind),
            jax.ShapeDtypeStruct((owners * rank, row_count), jnp.bfloat16),
        ],
        compiler_params=params(),
        cost_estimate=cost(4),
        name="gradients",
    )(*deps, owner_of, *sums, rows)


def share_kernel(spans, keep, rows, weight, *outs):
    if keep:

        @pl.when(pl.program_id(0) == 0)
        def _():
            outs[-1][...] = rows[...]

    product = jnp.dot(rows[...], weight[...], preferred_element_type=jnp.float32)
    for out, (start, count) in zip(outs, spans):
        out[...] = product[start : start + count, :].astype(out.dtype)


def share(tokens, weight, piece, start, total, spans, width, keep, deps):
    features = tokens.shape[1]
    tile = min(512, width)
    tiles = width // tile
    return pl.pallas_call(
        behind(functools.partial(share_kernel, spans, keep), deps),
        grid=(tiles,),
        in_specs=[ANY] * len(deps)
        + [
            pl.BlockSpec((total, features), lambda j: (start // total, 0)),
            pl.BlockSpec((features, tile), lambda j: (0, piece * tiles + j)),
        ],
        out_specs=[pl.BlockSpec((count, tile), lambda j: (0, j)) for _, count in spans]
        + [pl.BlockSpec((total, features), lambda j: (0, 0))] * keep,
        out_shape=[jax.ShapeDtypeStruct((count, width), jnp.bfloat16) for _, count in spans]
        + [jax.ShapeDtypeStruct((total, features), jnp.bfloat16)] * keep,
        compiler_params=params(),
        cost_estimate=cost(4.0 * total / 256),
        name="share",
    )(*deps, tokens, weight)


def finish_kernel(cores, flags, spans, mine_is_own, wide, *refs):
    halves, arrays, out = refs[:cores], refs[cores : cores + len(flags)], refs[-1]
    step = pl.program_id(0)
    turned = wide[...].T
    half = halves[0].shape[-1]
    for h in range(cores):
        span = slice(h * half, (h + 1) * half)
        flat = halves[h][...].reshape(turned.shape[1], half)
        total = ADAPTER_SCALE * jnp.dot(turned, flat, preferred_element_type=jnp.float32)
        for array, flag, (first, last) in zip(arrays, flags, spans):
            active = jnp.logical_and(step >= first, step < last)
            active = jnp.logical_and(active, mine_is_own[0] == flag)
            total = total + jnp.where(active, array[:, span].astype(jnp.float32), 0.0)
        out[:, span] = total.astype(out.dtype)


def finish(mine_is_own, wide, adapters, row_count, start, count, terms, previous, deps):
    owners, cores, rank, half = adapters.shape
    width = cores * half
    tile = min(256, count)
    first = start // tile
    specs, spans = [], []
    for array, row, flag in terms:
        low, many = (row - start) // tile, array.shape[0] // tile

        def block_of(i, mine, low=low, many=many, flag=flag):
            return (jnp.where(mine[0] == flag, jnp.clip(i - low, 0, many - 1), 0), 0)

        specs.append(pl.BlockSpec((tile, width), block_of))
        spans.append((low, low + many))
    operands = [mine_is_own, *deps, wide, *[adapters] * cores]
    operands += [t[0] for t in terms]
    in_specs = (
        [ANY] * len(deps)
        + [pl.BlockSpec((owners * rank, tile), lambda i, mine: (0, first + i))]
        + halves_specs(owners, cores, rank, half)
        + specs
    )
    aliases = {}
    if previous is not None:
        aliases = {len(operands): 0}
        operands.append(previous)
        in_specs.append(ANY)
    return pl.pallas_call(
        behind(functools.partial(finish_kernel, cores, [t[2] for t in terms], spans), deps, 1),
        grid_spec=pltpu.PrefetchScalarGridSpec(
            num_scalar_prefetch=1,
            grid=(count // tile,),
            in_specs=in_specs,
            out_specs=pl.BlockSpec((tile, width), lambda i, mine: (first + i, 0)),
        ),
        out_shape=jax.ShapeDtypeStruct((row_count, width), jnp.bfloat16),
        input_output_aliases=aliases,
        compiler_params=params(),
        cost_estimate=cost(4),
        name="finish",
    )(*operands)


def adam_kernel(devices, slots, coded, pick, used, corr, param, first, second, messages, *refs):
    levels = refs[0]
    new_param, new_first, new_second, grads = refs[-4:]
    grads[...] = jnp.zeros_like(grads)
    for device in range(devices):
        k = pick[device]
        value = messages[device].astype(jnp.float32)
        if coded:
            level = levels[device].astype(jnp.float32)[:, :1]
            value = value * (jnp.exp2(level * (1.0 / LEVELS)) * (1.0 / TOP_CODE))
        grads[k] = grads[k] + value
    for k in range(slots):
        grad = grads[k]
        one = BETA_ONE * first[k] + (1.0 - BETA_ONE) * grad
        two = BETA_TWO * second[k] + (1.0 - BETA_TWO) * grad * grad
        update = LEARN_RATE * (one / corr[k]) / (jnp.sqrt(two / corr[slots + k]) + ADAM_EPS)
        keep = used[k] == 1
        new_param[k] = jnp.where(keep, param[k] - update, param[k])
        new_first[k] = jnp.where(keep, one, first[k])
        new_second[k] = jnp.where(keep, two, second[k])


def adam(pick, used, corr, param, first, second, messages, deps):
    slots, rank, half = param.shape
    devices = messages.shape[0]
    tile = min(256, half)
    state = pl.BlockSpec((slots, rank, tile), lambda i: (0, 0, i))
    message = pl.BlockSpec((devices, rank, tile), lambda i: (0, 0, i))
    coded = messages.dtype == jnp.int16
    levels = [messages] * coded
    level = pl.BlockSpec((devices, rank, LEVEL_LANES), lambda i: (0, 0, half // LEVEL_LANES))
    return pl.pallas_call(
        behind(functools.partial(adam_kernel, devices, slots, coded), deps),
        grid=(half // tile,),
        in_specs=[ANY] * len(deps) + [SMEM] * 3 + [state] * 3 + [message] + [level] * coded,
        out_specs=[state] * 3,
        out_shape=[dims(param)] * 3,
        scratch_shapes=[pltpu.VMEM((slots, rank, tile), jnp.float32)],
        compiler_params=params(),
        cost_estimate=cost(4),
        name="adam",
    )(*deps, pick, used, corr, param, first, second, messages, *levels)


def on_device(
    tokens,
    frozen_weight,
    cotangent,
    down_adapters,
    up_adapters,
    down_first_moment,
    up_first_moment,
    down_second_moment,
    up_second_moment,
    optimizer_steps,
    slot_of_tenant,
    tenant_of_block,
):
    row_count, din_local = tokens.shape
    width = cotangent.shape[1]
    block_count = row_count // BLK_ROWS
    owners = lax.axis_size("dp")
    cores = lax.axis_size("sub")
    columns = lax.axis_size("tensor")
    z = lax.axis_index("dp")
    s = lax.axis_index("sub")
    x = lax.axis_index("tensor")
    slots, half, rank = down_adapters.shape
    flip = lambda v: jnp.swapaxes(v, 1, 2)
    down_adapters, up_adapters = flip(down_adapters), flip(up_adapters)
    down_first_moment, up_first_moment = flip(down_first_moment), flip(up_first_moment)
    down_second_moment, up_second_moment = flip(down_second_moment), flip(up_second_moment)
    per_half = columns // cores
    place = jnp.stack([z, s]).astype(jnp.int32)

    devices = owners * cores

    def tables(deps):
        return pl.pallas_call(
            behind(functools.partial(tables_kernel, devices, cores, slots, block_count), deps),
            in_specs=[ANY] * len(deps) + [SMEM] * 3,
            out_specs=[SMEM] * 3,
            out_shape=[
                jax.ShapeDtypeStruct((devices,), jnp.int32),
                jax.ShapeDtypeStruct((block_count,), jnp.int32),
                jax.ShapeDtypeStruct((slots,), jnp.int32),
            ],
            cost_estimate=cost(2),
            name="tables",
        )(*deps, place, slot_of_tenant, tenant_of_block)

    steps = (optimizer_steps + 1).astype(jnp.float32)
    corr = jnp.concatenate(
        [
            1.0 - jnp.power(jnp.float32(BETA_ONE), steps),
            1.0 - jnp.power(jnp.float32(BETA_TWO), steps),
        ]
    )

    def pack(own, deps):
        return pl.pallas_call(
            behind(functools.partial(pack_kernel, devices), deps),
            in_specs=[ANY] * len(deps) + [SMEM, pl.BlockSpec(memory_space=pltpu.VMEM)],
            out_specs=pl.BlockSpec(memory_space=pltpu.VMEM),
            out_shape=jax.ShapeDtypeStruct((devices, rank, half), jnp.bfloat16),
            compiler_params=params(),
            cost_estimate=cost(1),
            name="pack",
        )(*deps, pick, own)

    def spread_out(messages):
        flat = messages.reshape((devices,) + messages.shape[-2:])
        return lax.all_to_all(flat, ("dp", "sub"), split_axis=0, concat_axis=0, tiled=True)

    def by_owner(arrived):
        return arrived.reshape(owners, cores, rank, half)

    def shares(rows, start, total, spans, keep, deps):
        pieces = []
        for piece in range(per_half):
            kept = int(keep and piece == 0)
            out = share(rows, frozen_weight, piece, start, total, spans, width, kept, deps)
            pieces.append(out[: len(spans)])
            copy = out[-1] if kept else copy if piece else None
            deps = [pieces[-1][0]]
        chunks = [list(chunk) for chunk in zip(*pieces)]
        return chunks + [copy] if keep else chunks

    def piece_for(chunk, target):
        if per_half == 1:
            return chunk[0]
        out = chunk[0]
        for piece in range(1, per_half):
            out = jnp.where(lax.rem(target, per_half) == piece, chunk[piece], out)
        return out

    def send(chunk, cross):
        got = []
        for step in range(1, columns):
            pairs = []
            for t in range(columns):
                for c in range(cores):
                    target = (t + step) % columns
                    if target // per_half == c:
                        pairs.append((t * cores + c, target * cores + (c + cross) % cores))
            operand = piece_for(chunk, lax.rem(x + step, columns))
            got.append(lax.ppermute(operand, ("tensor", "sub"), pairs))
        return got

    def send_local(chunk):
        pairs = []
        for t in range(columns):
            c = t // per_half
            pairs.append((t * cores + c, t * cores + (c + 1) % cores))
        return lax.ppermute(piece_for(chunk, x), ("tensor", "sub"), pairs)

    def exchange(part):
        return [part] + [rotate(part, "tensor", step) for step in range(1, columns)]

    half_rows = row_count // 2
    one_half = [(0, half_rows)]
    both = one_half * 2
    pick, owner_of, used = tables([])
    down_packed = pack(down_adapters, [])
    down_arrived = by_owner(spread_out(down_packed))
    own_a, low_rows = shares(tokens, 0, half_rows, one_half, True, [down_packed])
    got_a = send(own_a, 0)
    other_low = rotate(low_rows, "sub", 1)
    up_packed = pack(up_adapters, [own_a[-1]])
    own_b, high_rows = shares(tokens, half_rows, half_rows, one_half, True, [up_packed])
    other_high = rotate(high_rows, "sub", 1)
    up_packed, = tie([up_packed], [down_arrived, own_b[-1]])
    up_arrived = by_owner(spread_out(up_packed))

    down_part = adapter_product(owner_of, down_arrived, tokens, [up_packed])
    down_sums = exchange(down_part)
    own_b = tie(own_b, [down_part])
    got_b = send(own_b, 0)
    cross_a, cross_a_near = shares(other_low, 0, half_rows, both, False, [own_b[-1]])
    local_a = send_local(cross_a_near)
    up_messages, down_wide = gradients(
        owner_of, down_sums, cotangent, owners, half, 1.0, ADAPTER_SCALE, jnp.bfloat16,
        [cross_a[-1]] + got_a,
    )
    up_messages, = tie([up_messages], [up_arrived])
    up_returned = spread_out(up_messages)
    back_part = adapter_product(owner_of, up_arrived, cotangent, [up_messages])
    back_sums = exchange(back_part)
    cross_a = tie(cross_a, [back_part])
    late_a = send(cross_a, 1)
    cross_b, cross_b_near = shares(other_high, 0, half_rows, both, False, [cross_a[-1]])
    down_messages, back_wide = gradients(
        owner_of, back_sums, tokens, owners, half, ADAPTER_SCALE, 1.0, jnp.int16,
        [cross_b[-1]] + got_b,
    )
    cross_b = tie(cross_b, [down_messages])
    late_b = send(cross_b, 1)
    down_messages, = tie([down_messages], [up_returned])
    down_returned = spread_out(down_messages)
    cross_b_near = tie(cross_b_near, [down_messages])
    local_b = send_local(cross_b_near)

    fresh_up, fresh_up_first, fresh_up_second = adam(
        pick, used, corr, up_adapters, up_first_moment, up_second_moment, up_returned,
        [cross_b_near[-1]],
    )
    mine_is_own = (lax.div(x, per_half) == s).astype(jnp.int32).reshape(1)
    terms_a = [(piece_for(own_a, x), 0, 1), (local_a, 0, 0)]
    terms_a += [(g, 0, 1) for g in got_a] + [(g, 0, 0) for g in late_a]
    terms_b = [(piece_for(own_b, x), half_rows, 1), (local_b, half_rows, 0)]
    terms_b += [(g, half_rows, 1) for g in got_b] + [(g, half_rows, 0) for g in late_b]
    projected = finish(
        mine_is_own, down_wide, up_arrived, row_count, 0, half_rows, terms_a, None, [fresh_up]
    )
    projected = finish(
        mine_is_own, down_wide, up_arrived, row_count, half_rows, half_rows, terms_b, projected,
        [],
    )
    fresh_down, fresh_down_first, fresh_down_second = adam(
        pick, used, corr, down_adapters, down_first_moment, down_second_moment, down_returned,
        [projected],
    )
    return (
        projected,
        flip(fresh_down),
        flip(fresh_up),
        flip(fresh_down_first),
        flip(fresh_up_first),
        flip(fresh_down_second),
        flip(fresh_up_second),
    )


def solution(mesh):
    placed = (
        P(("groups", "dp", "sub"), "tensor"),
        P("tensor", "sub"),
        P(("groups", "dp", "sub"), "tensor"),
        P(("groups", "dp"), ("tensor", "sub"), None),
        P(("groups", "dp"), ("tensor", "sub"), None),
        P(("groups", "dp"), ("tensor", "sub"), None),
        P(("groups", "dp"), ("tensor", "sub"), None),
        P(("groups", "dp"), ("tensor", "sub"), None),
        P(("groups", "dp"), ("tensor", "sub"), None),
        P(("groups", "dp")),
        P("groups"),
        P("groups"),
    )
    return jax.shard_map(
        on_device,
        mesh=mesh,
        in_specs=placed,
        out_specs=(
            P(("groups", "dp", "sub"), "tensor"),
            P(("groups", "dp"), ("tensor", "sub"), None),
            P(("groups", "dp"), ("tensor", "sub"), None),
            P(("groups", "dp"), ("tensor", "sub"), None),
            P(("groups", "dp"), ("tensor", "sub"), None),
            P(("groups", "dp"), ("tensor", "sub"), None),
            P(("groups", "dp"), ("tensor", "sub"), None),
        ),
        check_vma=False,
    )
```

```python
import functools

import jax
import jax.numpy as jnp
from jax import lax
from jax.experimental import pallas as pl
from jax.experimental.pallas import tpu as pltpu
from jax.sharding import PartitionSpec as P

BLK_ROWS = 128


ADAPTER_SCALE = 2.0
BETA_ONE = 0.9
BETA_TWO = 0.999
LEARN_RATE = 0.01
ADAM_EPS = 1e-08

SMEM = pl.BlockSpec(memory_space=pltpu.SMEM)
VMEM_BYTES = 63_000_000
TOP_CODE = 32767.0
LEVELS = 64.0
LEVEL_LANES = 128
COST = 20.0


def params():
    return pltpu.CompilerParams(vmem_limit_bytes=VMEM_BYTES)


def cost(micros):
    flops = int(micros * 1_000_000_000 * COST)
    return pl.CostEstimate(flops=flops, bytes_accessed=1000, transcendentals=0)


def rotate(value, axis, shift):
    size = lax.axis_size(axis)
    return lax.ppermute(value, axis, [(i, (i + shift) % size) for i in range(size)])


ANY = pl.BlockSpec(memory_space=pl.ANY)


def behind(kernel, deps, scalars=0):
    return lambda *refs: kernel(*refs[:scalars], *refs[scalars + len(deps) :])


def tie_kernel(*refs):
    pass


def tie(values, deps):
    return pl.pallas_call(
        tie_kernel,
        in_specs=[ANY] * (len(values) + len(deps)),
        out_specs=[ANY] * len(values),
        out_shape=[dims(v) for v in values],
        input_output_aliases={k: k for k in range(len(values))},
        cost_estimate=cost(100),
        name="tie",
    )(*values, *deps)


def dims(value):
    return jax.ShapeDtypeStruct(value.shape, value.dtype)


def tables_kernel(devices, cores, slots, block_count, place, slot_of, tenant_of, pick, owner_of, used):
    z, s = place[0], place[1]
    for k in range(slots):
        used[k] = 0

    def slot_at(device, b):
        return slot_of[tenant_of[device * block_count + b]]

    def per_device(device, carry):
        def per_block(b, found):
            local = slot_at(device, b) - z * slots
            mine = jnp.logical_and(local >= 0, local < slots)

            @pl.when(mine)
            def _():
                used[local] = 1

            return jnp.where(mine, local, found)

        pick[device] = lax.fori_loop(0, block_count, per_block, 0)
        return carry

    lax.fori_loop(0, devices, per_device, 0)
    for b in range(block_count):
        owner_of[b] = lax.div(slot_at(z * cores + s, b), slots)


def pack_kernel(devices, pick, own, out):
    for device in range(devices):
        out[device] = own[pick[device]].astype(jnp.bfloat16)


def product_kernel(owners, cores, rank, tile_rows, owner_of, *refs):
    halves, (rows, out) = refs[:cores], refs[cores:]
    step = pl.program_id(0)
    half = halves[0].shape[-1]
    full = 0.0
    for h in range(cores):
        full = full + lax.dot_general(
            halves[h][...].reshape(owners * rank, half),
            rows[:, h * half : (h + 1) * half],
            (((1,), (1,)), ((), ())),
            preferred_element_type=jnp.float32,
        )
    for b in range(tile_rows // BLK_ROWS):
        owner = owner_of[step * (tile_rows // BLK_ROWS) + b]
        span = slice(b * BLK_ROWS, (b + 1) * BLK_ROWS)
        value = full[:rank, span]
        for d in range(1, owners):
            value = jnp.where(owner == d, full[d * rank : (d + 1) * rank, span], value)
        out[:, span] = value


def halves_specs(owners, cores, rank, half):
    return [
        pl.BlockSpec((owners, None, rank, half), lambda *ids, h=h: (0, h, 0, 0))
        for h in range(cores)
    ]


def adapter_product(owner_of, adapters, rows, deps):
    (owners, cores, rank, half), (row_count, features) = adapters.shape, rows.shape
    tile = min(256, row_count)
    return pl.pallas_call(
        behind(functools.partial(product_kernel, owners, cores, rank, tile), deps),
        grid=(row_count // tile,),
        in_specs=[ANY] * len(deps)
        + [SMEM]
        + halves_specs(owners, cores, rank, half)
        + [pl.BlockSpec((tile, features), lambda i: (i, 0))],
        out_specs=pl.BlockSpec((rank, tile), lambda i: (0, i)),
        out_shape=jax.ShapeDtypeStruct((rank, row_count), jnp.float32),
        compiler_params=params(),
        cost_estimate=cost(5),
        name="adapter_product",
    )(*deps, owner_of, *[adapters] * cores, rows)


def encode(product, kind):
    if kind != jnp.int16:
        return product.astype(kind)
    top = jnp.maximum(jnp.max(jnp.abs(product), axis=1, keepdims=True), 1e-30)
    level = jnp.floor(jnp.log2(top) * LEVELS) + 2.0
    coded = jnp.round(product * (TOP_CODE * jnp.exp2(level * (-1.0 / LEVELS))))
    coded = jnp.clip(coded, -TOP_CODE, TOP_CODE).astype(jnp.int32).astype(jnp.int16)
    lanes = jnp.broadcast_to(level, (product.shape[0], LEVEL_LANES))
    return jnp.concatenate([coded, lanes.astype(jnp.int32).astype(jnp.int16)], axis=1)


def gradient_kernel(owners, rank, terms, scale_in, scale_out, owner_of, *refs):
    sums, (rows, out, wide) = refs[:terms], refs[terms:]

    @pl.when(pl.program_id(0) == 0)
    def _():
        total = sums[0][...]
        for t in range(1, terms):
            total = total + sums[t][...]
        value = (scale_in * total).astype(jnp.bfloat16)
        for b in range(value.shape[1] // BLK_ROWS):
            span = slice(b * BLK_ROWS, (b + 1) * BLK_ROWS)
            for d in range(owners):
                kept = jnp.where(owner_of[b] == d, value[:, span], jnp.zeros_like(value[:, span]))
                wide[d * rank : (d + 1) * rank, span] = kept

    product = scale_out * jnp.dot(wide[...], rows[...], preferred_element_type=jnp.float32)
    out[...] = encode(product, out.dtype).reshape(out.shape)


def gradients(owner_of, sums, rows, owners, half, scale_in, scale_out, kind, deps):
    rank, row_count = sums[0].shape
    cores = rows.shape[1] // half
    lanes = half + (LEVEL_LANES if kind == jnp.int16 else 0)
    whole = pl.BlockSpec((rank, row_count), lambda h: (0, 0))
    return pl.pallas_call(
        behind(
            functools.partial(gradient_kernel, owners, rank, len(sums), scale_in, scale_out), deps
        ),
        grid=(cores,),
        in_specs=[ANY] * len(deps)
        + [SMEM]
        + [whole] * len(sums)
        + [pl.BlockSpec((row_count, half), lambda h: (0, h))],
        out_specs=[
            pl.BlockSpec((owners, None, rank, lanes), lambda h: (0, h, 0, 0)),
            pl.BlockSpec((owners * rank, row_count), lambda h: (0, 0)),
        ],
        out_shape=[
            jax.ShapeDtypeStruct((owners, cores, rank, lanes), kind),
            jax.ShapeDtypeStruct((owners * rank, row_count), jnp.bfloat16),
        ],
        compiler_params=params(),
        cost_estimate=cost(4),
        name="gradients",
    )(*deps, owner_of, *sums, rows)


def share_kernel(spans, keep, rows, weight, *outs):
    if keep:

        @pl.when(pl.program_id(0) == 0)
        def _():
            outs[-1][...] = rows[...]

    product = jnp.dot(rows[...], weight[...], preferred_element_type=jnp.float32)
    for out, (start, count) in zip(outs, spans):
        out[...] = product[start : start + count, :].astype(out.dtype)


def share(tokens, weight, piece, start, total, spans, width, keep, deps):
    features = tokens.shape[1]
    tile = min(512, width)
    tiles = width // tile
    return pl.pallas_call(
        behind(functools.partial(share_kernel, spans, keep), deps),
        grid=(tiles,),
        in_specs=[ANY] * len(deps)
        + [
            pl.BlockSpec((total, features), lambda j: (start // total, 0)),
            pl.BlockSpec((features, tile), lambda j: (0, piece * tiles + j)),
        ],
        out_specs=[pl.BlockSpec((count, tile), lambda j: (0, j)) for _, count in spans]
        + [pl.BlockSpec((total, features), lambda j: (0, 0))] * keep,
        out_shape=[jax.ShapeDtypeStruct((count, width), jnp.bfloat16) for _, count in spans]
        + [jax.ShapeDtypeStruct((total, features), jnp.bfloat16)] * keep,
        compiler_params=params(),
        cost_estimate=cost(4.0 * total / 256),
        name="share",
    )(*deps, tokens, weight)


def finish_kernel(cores, flags, spans, mine_is_own, wide, *refs):
    halves, arrays, out = refs[:cores], refs[cores : cores + len(flags)], refs[-1]
    step = pl.program_id(0)
    turned = wide[...].T
    half = halves[0].shape[-1]
    for h in range(cores):
        span = slice(h * half, (h + 1) * half)
        flat = halves[h][...].reshape(turned.shape[1], half)
        total = ADAPTER_SCALE * jnp.dot(turned, flat, preferred_element_type=jnp.float32)
        for array, flag, (first, last) in zip(arrays, flags, spans):
            active = jnp.logical_and(step >= first, step < last)
            active = jnp.logical_and(active, mine_is_own[0] == flag)
            total = total + jnp.where(active, array[:, span].astype(jnp.float32), 0.0)
        out[:, span] = total.astype(out.dtype)


def finish(mine_is_own, wide, adapters, row_count, start, count, terms, previous, deps):
    owners, cores, rank, half = adapters.shape
    width = cores * half
    tile = min(256, count)
    first = start // tile
    specs, spans = [], []
    for array, row, flag in terms:
        low, many = (row - start) // tile, array.shape[0] // tile

        def block_of(i, mine, low=low, many=many, flag=flag):
            return (jnp.where(mine[0] == flag, jnp.clip(i - low, 0, many - 1), 0), 0)

        specs.append(pl.BlockSpec((tile, width), block_of))
        spans.append((low, low + many))
    operands = [mine_is_own, *deps, wide, *[adapters] * cores]
    operands += [t[0] for t in terms]
    in_specs = (
        [ANY] * len(deps)
        + [pl.BlockSpec((owners * rank, tile), lambda i, mine: (0, first + i))]
        + halves_specs(owners, cores, rank, half)
        + specs
    )
    aliases = {}
    if previous is not None:
        aliases = {len(operands): 0}
        operands.append(previous)
        in_specs.append(ANY)
    return pl.pallas_call(
        behind(functools.partial(finish_kernel, cores, [t[2] for t in terms], spans), deps, 1),
        grid_spec=pltpu.PrefetchScalarGridSpec(
            num_scalar_prefetch=1,
            grid=(count // tile,),
            in_specs=in_specs,
            out_specs=pl.BlockSpec((tile, width), lambda i, mine: (first + i, 0)),
        ),
        out_shape=jax.ShapeDtypeStruct((row_count, width), jnp.bfloat16),
        input_output_aliases=aliases,
        compiler_params=params(),
        cost_estimate=cost(4),
        name="finish",
    )(*operands)


def adam_kernel(devices, slots, coded, pick, used, corr, param, first, second, messages, *refs):
    levels = refs[0]
    new_param, new_first, new_second, grads = refs[-4:]
    grads[...] = jnp.zeros_like(grads)
    for device in range(devices):
        k = pick[device]
        value = messages[device].astype(jnp.float32)
        if coded:
            level = levels[device].astype(jnp.float32)[:, :1]
            value = value * (jnp.exp2(level * (1.0 / LEVELS)) * (1.0 / TOP_CODE))
        grads[k] = grads[k] + value
    for k in range(slots):
        grad = grads[k]
        one = BETA_ONE * first[k] + (1.0 - BETA_ONE) * grad
        two = BETA_TWO * second[k] + (1.0 - BETA_TWO) * grad * grad
        update = LEARN_RATE * (one / corr[k]) / (jnp.sqrt(two / corr[slots + k]) + ADAM_EPS)
        keep = used[k] == 1
        new_param[k] = jnp.where(keep, param[k] - update, param[k])
        new_first[k] = jnp.where(keep, one, first[k])
        new_second[k] = jnp.where(keep, two, second[k])


def adam(pick, used, corr, param, first, second, messages, deps):
    slots, rank, half = param.shape
    devices = messages.shape[0]
    tile = min(256, half)
    state = pl.BlockSpec((slots, rank, tile), lambda i: (0, 0, i))
    message = pl.BlockSpec((devices, rank, tile), lambda i: (0, 0, i))
    coded = messages.dtype == jnp.int16
    levels = [messages] * coded
    level = pl.BlockSpec((devices, rank, LEVEL_LANES), lambda i: (0, 0, half // LEVEL_LANES))
    return pl.pallas_call(
        behind(functools.partial(adam_kernel, devices, slots, coded), deps),
        grid=(half // tile,),
        in_specs=[ANY] * len(deps) + [SMEM] * 3 + [state] * 3 + [message] + [level] * coded,
        out_specs=[state] * 3,
        out_shape=[dims(param)] * 3,
        scratch_shapes=[pltpu.VMEM((slots, rank, tile), jnp.float32)],
        compiler_params=params(),
        cost_estimate=cost(4),
        name="adam",
    )(*deps, pick, used, corr, param, first, second, messages, *levels)


def on_device(
    tokens,
    frozen_weight,
    cotangent,
    down_adapters,
    up_adapters,
    down_first_moment,
    up_first_moment,
    down_second_moment,
    up_second_moment,
    optimizer_steps,
    slot_of_tenant,
    tenant_of_block,
):
    row_count, din_local = tokens.shape
    width = cotangent.shape[1]
    block_count = row_count // BLK_ROWS
    owners = lax.axis_size("dp")
    cores = lax.axis_size("sub")
    columns = lax.axis_size("tensor")
    z = lax.axis_index("dp")
    s = lax.axis_index("sub")
    x = lax.axis_index("tensor")
    slots, half, rank = down_adapters.shape
    flip = lambda v: jnp.swapaxes(v, 1, 2)
    down_adapters, up_adapters = flip(down_adapters), flip(up_adapters)
    down_first_moment, up_first_moment = flip(down_first_moment), flip(up_first_moment)
    down_second_moment, up_second_moment = flip(down_second_moment), flip(up_second_moment)
    per_half = columns // cores
    place = jnp.stack([z, s]).astype(jnp.int32)

    devices = owners * cores

    def tables(deps):
        return pl.pallas_call(
            behind(functools.partial(tables_kernel, devices, cores, slots, block_count), deps),
            in_specs=[ANY] * len(deps) + [SMEM] * 3,
            out_specs=[SMEM] * 3,
            out_shape=[
                jax.ShapeDtypeStruct((devices,), jnp.int32),
                jax.ShapeDtypeStruct((block_count,), jnp.int32),
                jax.ShapeDtypeStruct((slots,), jnp.int32),
            ],
            cost_estimate=cost(2),
            name="tables",
        )(*deps, place, slot_of_tenant, tenant_of_block)

    steps = (optimizer_steps + 1).astype(jnp.float32)
    corr = jnp.concatenate(
        [
            1.0 - jnp.power(jnp.float32(BETA_ONE), steps),
            1.0 - jnp.power(jnp.float32(BETA_TWO), steps),
        ]
    )

    def pack(own, deps):
        return pl.pallas_call(
            behind(functools.partial(pack_kernel, devices), deps),
            in_specs=[ANY] * len(deps) + [SMEM, pl.BlockSpec(memory_space=pltpu.VMEM)],
            out_specs=pl.BlockSpec(memory_space=pltpu.VMEM),
            out_shape=jax.ShapeDtypeStruct((devices, rank, half), jnp.bfloat16),
            compiler_params=params(),
            cost_estimate=cost(1),
            name="pack",
        )(*deps, pick, own)

    def spread_out(messages):
        flat = messages.reshape((devices,) + messages.shape[-2:])
        return lax.all_to_all(flat, ("dp", "sub"), split_axis=0, concat_axis=0, tiled=True)

    def by_owner(arrived):
        return arrived.reshape(owners, cores, rank, half)

    def shares(rows, start, total, spans, keep, deps):
        pieces = []
        for piece in range(per_half):
            kept = int(keep and piece == 0)
            out = share(rows, frozen_weight, piece, start, total, spans, width, kept, deps)
            pieces.append(out[: len(spans)])
            copy = out[-1] if kept else copy if piece else None
            deps = [pieces[-1][0]]
        chunks = [list(chunk) for chunk in zip(*pieces)]
        return chunks + [copy] if keep else chunks

    def piece_for(chunk, target):
        if per_half == 1:
            return chunk[0]
        out = chunk[0]
        for piece in range(1, per_half):
            out = jnp.where(lax.rem(target, per_half) == piece, chunk[piece], out)
        return out

    def send(chunk, cross):
        got = []
        for step in range(1, columns):
            pairs = []
            for t in range(columns):
                for c in range(cores):
                    target = (t + step) % columns
                    if target // per_half == c:
                        pairs.append((t * cores + c, target * cores + (c + cross) % cores))
            operand = piece_for(chunk, lax.rem(x + step, columns))
            got.append(lax.ppermute(operand, ("tensor", "sub"), pairs))
        return got

    def send_local(chunk):
        pairs = []
        for t in range(columns):
            c = t // per_half
            pairs.append((t * cores + c, t * cores + (c + 1) % cores))
        return lax.ppermute(piece_for(chunk, x), ("tensor", "sub"), pairs)

    def exchange(part):
        return [part] + [rotate(part, "tensor", step) for step in range(1, columns)]

    half_rows = row_count // 2
    one_half = [(0, half_rows)]
    both = one_half * 2
    pick, owner_of, used = tables([])
    down_packed = pack(down_adapters, [])
    down_arrived = by_owner(spread_out(down_packed))
    own_a, low_rows = shares(tokens, 0, half_rows, one_half, True, [down_packed])
    got_a = send(own_a, 0)
    other_low = rotate(low_rows, "sub", 1)
    up_packed = pack(up_adapters, [own_a[-1]])
    own_b, high_rows = shares(tokens, half_rows, half_rows, one_half, True, [up_packed])
    other_high = rotate(high_rows, "sub", 1)
    up_arrived = by_owner(spread_out(up_packed))

    down_part = adapter_product(owner_of, down_arrived, tokens, [own_b[-1]])
    down_sums = exchange(down_part)
    own_b = tie(own_b, [down_part])
    got_b = send(own_b, 0)
    cross_a, cross_a_near = shares(other_low, 0, half_rows, both, False, [own_b[-1]])
    local_a = send_local(cross_a_near)
    back_part = adapter_product(owner_of, up_arrived, cotangent, [cross_a[-1]])
    back_sums = exchange(back_part)
    cross_a = tie(cross_a, [back_part])
    late_a = send(cross_a, 1)
    up_messages, down_wide = gradients(
        owner_of, down_sums, cotangent, owners, half, 1.0, ADAPTER_SCALE, jnp.bfloat16,
        [cross_a[-1]] + got_a,
    )
    up_returned = spread_out(up_messages)
    cross_b, cross_b_near = shares(other_high, 0, half_rows, both, False, [up_messages])
    down_messages, back_wide = gradients(
        owner_of, back_sums, tokens, owners, half, ADAPTER_SCALE, 1.0, jnp.int16,
        [cross_b[-1]] + got_b,
    )
    cross_b = tie(cross_b, [down_messages])
    late_b = send(cross_b, 1)
    down_returned = spread_out(down_messages)
    cross_b_near = tie(cross_b_near, [down_messages])
    local_b = send_local(cross_b_near)

    fresh_up, fresh_up_first, fresh_up_second = adam(
        pick, used, corr, up_adapters, up_first_moment, up_second_moment, up_returned,
        [cross_b_near[-1]],
    )
    mine_is_own = (lax.div(x, per_half) == s).astype(jnp.int32).reshape(1)
    terms_a = [(piece_for(own_a, x), 0, 1), (local_a, 0, 0)]
    terms_a += [(g, 0, 1) for g in got_a] + [(g, 0, 0) for g in late_a]
    terms_b = [(piece_for(own_b, x), half_rows, 1), (local_b, half_rows, 0)]
    terms_b += [(g, half_rows, 1) for g in got_b] + [(g, half_rows, 0) for g in late_b]
    projected = finish(
        mine_is_own, down_wide, up_arrived, row_count, 0, half_rows, terms_a, None, [fresh_up]
    )
    projected = finish(
        mine_is_own, down_wide, up_arrived, row_count, half_rows, half_rows, terms_b, projected,
        [],
    )
    fresh_down, fresh_down_first, fresh_down_second = adam(
        pick, used, corr, down_adapters, down_first_moment, down_second_moment, down_returned,
        [projected],
    )
    return (
        projected,
        flip(fresh_down),
        flip(fresh_up),
        flip(fresh_down_first),
        flip(fresh_up_first),
        flip(fresh_down_second),
        flip(fresh_up_second),
    )


def solution(mesh):
    placed = (
        P(("groups", "dp", "sub"), "tensor"),
        P("tensor", "sub"),
        P(("groups", "dp", "sub"), "tensor"),
        P(("groups", "dp"), ("tensor", "sub"), None),
        P(("groups", "dp"), ("tensor", "sub"), None),
        P(("groups", "dp"), ("tensor", "sub"), None),
        P(("groups", "dp"), ("tensor", "sub"), None),
        P(("groups", "dp"), ("tensor", "sub"), None),
        P(("groups", "dp"), ("tensor", "sub"), None),
        P(("groups", "dp")),
        P("groups"),
        P("groups"),
    )
    return jax.shard_map(
        on_device,
        mesh=mesh,
        in_specs=placed,
        out_specs=(
            P(("groups", "dp", "sub"), "tensor"),
            P(("groups", "dp"), ("tensor", "sub"), None),
            P(("groups", "dp"), ("tensor", "sub"), None),
            P(("groups", "dp"), ("tensor", "sub"), None),
            P(("groups", "dp"), ("tensor", "sub"), None),
            P(("groups", "dp"), ("tensor", "sub"), None),
            P(("groups", "dp"), ("tensor", "sub"), None),
        ),
        check_vma=False,
    )
```

```python
import functools

import jax
import jax.numpy as jnp
from jax import lax
from jax.experimental import pallas as pl
from jax.experimental.pallas import tpu as pltpu
from jax.sharding import PartitionSpec as P

BLK_ROWS = 128


ADAPTER_SCALE = 2.0
BETA_ONE = 0.9
BETA_TWO = 0.999
LEARN_RATE = 0.01
ADAM_EPS = 1e-08

SMEM = pl.BlockSpec(memory_space=pltpu.SMEM)
VMEM_BYTES = 63_000_000
TOP_CODE = 32767.0
LEVELS = 64.0
LEVEL_LANES = 128
COST = 20.0


def params():
    return pltpu.CompilerParams(vmem_limit_bytes=VMEM_BYTES)


def cost(micros):
    flops = int(micros * 1_000_000_000 * COST)
    return pl.CostEstimate(flops=flops, bytes_accessed=1000, transcendentals=0)


def rotate(value, axis, shift):
    size = lax.axis_size(axis)
    return lax.ppermute(value, axis, [(i, (i + shift) % size) for i in range(size)])


ANY = pl.BlockSpec(memory_space=pl.ANY)


def behind(kernel, deps, scalars=0):
    return lambda *refs: kernel(*refs[:scalars], *refs[scalars + len(deps) :])


def tie_kernel(*refs):
    pass


def tie(values, deps):
    return pl.pallas_call(
        tie_kernel,
        in_specs=[ANY] * (len(values) + len(deps)),
        out_specs=[ANY] * len(values),
        out_shape=[dims(v) for v in values],
        input_output_aliases={k: k for k in range(len(values))},
        cost_estimate=cost(100),
        name="tie",
    )(*values, *deps)


def dims(value):
    return jax.ShapeDtypeStruct(value.shape, value.dtype)


def tables_kernel(devices, cores, slots, block_count, place, slot_of, tenant_of, pick, owner_of, used):
    z, s = place[0], place[1]
    for k in range(slots):
        used[k] = 0

    def slot_at(device, b):
        return slot_of[tenant_of[device * block_count + b]]

    def per_device(device, carry):
        def per_block(b, found):
            local = slot_at(device, b) - z * slots
            mine = jnp.logical_and(local >= 0, local < slots)

            @pl.when(mine)
            def _():
                used[local] = 1

            return jnp.where(mine, local, found)

        pick[device] = lax.fori_loop(0, block_count, per_block, 0)
        return carry

    lax.fori_loop(0, devices, per_device, 0)
    for b in range(block_count):
        owner_of[b] = lax.div(slot_at(z * cores + s, b), slots)


def pack_kernel(devices, pick, own, out):
    for device in range(devices):
        out[device] = own[pick[device]].astype(jnp.bfloat16)


def pack_wide_kernel(owners, cores, place, pick, own, other, *outs):
    z, s = place[0], place[1]
    half = own.shape[2]
    for d in range(owners):
        k = pick[lax.rem(z + d, owners) * cores + s]
        near, far = own[k].astype(jnp.bfloat16), other[k].astype(jnp.bfloat16)
        outs[d][:, :half] = jnp.where(s == 0, near, far)
        outs[d][:, half:] = jnp.where(s == 0, far, near)


def product_kernel(owners, cores, rank, tile_rows, owner_of, *refs):
    halves, (rows, out) = refs[:cores], refs[cores:]
    step = pl.program_id(0)
    half = halves[0].shape[-1]
    full = 0.0
    for h in range(cores):
        full = full + lax.dot_general(
            halves[h][...].reshape(owners * rank, half),
            rows[:, h * half : (h + 1) * half],
            (((1,), (1,)), ((), ())),
            preferred_element_type=jnp.float32,
        )
    for b in range(tile_rows // BLK_ROWS):
        owner = owner_of[step * (tile_rows // BLK_ROWS) + b]
        span = slice(b * BLK_ROWS, (b + 1) * BLK_ROWS)
        value = full[:rank, span]
        for d in range(1, owners):
            value = jnp.where(owner == d, full[d * rank : (d + 1) * rank, span], value)
        out[:, span] = value


def steps_product_kernel(owners, rank, tile_rows, place, owner_of, *refs):
    parts, (rows, out, cat) = refs[:owners], refs[owners:]
    step = pl.program_id(0)

    @pl.when(step == 0)
    def _():
        for d in range(owners):
            owner = lax.rem(place[0] - d + owners, owners)
            cat[pl.ds(pl.multiple_of(owner * rank, rank), rank), :] = parts[d][...]

    full = lax.dot_general(
        cat[...], rows[...], (((1,), (1,)), ((), ())), preferred_element_type=jnp.float32
    )
    for b in range(tile_rows // BLK_ROWS):
        owner = owner_of[step * (tile_rows // BLK_ROWS) + b]
        span = slice(b * BLK_ROWS, (b + 1) * BLK_ROWS)
        value = full[:rank, span]
        for d in range(1, owners):
            value = jnp.where(owner == d, full[d * rank : (d + 1) * rank, span], value)
        out[:, span] = value


def steps_product(place, owner_of, parts, rows, deps):
    owners, (rank, features), row_count = len(parts), parts[0].shape, rows.shape[0]
    tile = min(256, row_count)
    return pl.pallas_call(
        behind(functools.partial(steps_product_kernel, owners, rank, tile), deps),
        grid=(row_count // tile,),
        in_specs=[ANY] * len(deps)
        + [SMEM] * 2
        + [pl.BlockSpec((rank, features), lambda i: (0, 0))] * owners
        + [pl.BlockSpec((tile, features), lambda i: (i, 0))],
        out_specs=[
            pl.BlockSpec((rank, tile), lambda i: (0, i)),
            pl.BlockSpec((owners * rank, features), lambda i: (0, 0)),
        ],
        out_shape=[
            jax.ShapeDtypeStruct((rank, row_count), jnp.float32),
            jax.ShapeDtypeStruct((owners * rank, features), jnp.bfloat16),
        ],
        compiler_params=params(),
        cost_estimate=cost(5),
        name="steps_product",
    )(*deps, place, owner_of, *parts, rows)


def halves_specs(owners, cores, rank, half):
    return [
        pl.BlockSpec((owners, None, rank, half), lambda *ids, h=h: (0, h, 0, 0))
        for h in range(cores)
    ]


def adapter_product(owner_of, adapters, rows, deps):
    (owners, cores, rank, half), (row_count, features) = adapters.shape, rows.shape
    tile = min(256, row_count)
    return pl.pallas_call(
        behind(functools.partial(product_kernel, owners, cores, rank, tile), deps),
        grid=(row_count // tile,),
        in_specs=[ANY] * len(deps)
        + [SMEM]
        + halves_specs(owners, cores, rank, half)
        + [pl.BlockSpec((tile, features), lambda i: (i, 0))],
        out_specs=pl.BlockSpec((rank, tile), lambda i: (0, i)),
        out_shape=jax.ShapeDtypeStruct((rank, row_count), jnp.float32),
        compiler_params=params(),
        cost_estimate=cost(5),
        name="adapter_product",
    )(*deps, owner_of, *[adapters] * cores, rows)


def encode(product, kind):
    if kind != jnp.int16:
        return product.astype(kind)
    top = jnp.maximum(jnp.max(jnp.abs(product), axis=1, keepdims=True), 1e-30)
    level = jnp.floor(jnp.log2(top) * LEVELS) + 2.0
    coded = jnp.round(product * (TOP_CODE * jnp.exp2(level * (-1.0 / LEVELS))))
    coded = jnp.clip(coded, -TOP_CODE, TOP_CODE).astype(jnp.int32).astype(jnp.int16)
    lanes = jnp.broadcast_to(level, (product.shape[0], LEVEL_LANES))
    return jnp.concatenate([coded, lanes.astype(jnp.int32).astype(jnp.int16)], axis=1)


def spread_rows(owners, rank, scale_in, owner_of, sums, wide):
    @pl.when(pl.program_id(0) == 0)
    def _():
        total = sums[0][...]
        for term in sums[1:]:
            total = total + term[...]
        value = (scale_in * total).astype(jnp.bfloat16)
        for b in range(value.shape[1] // BLK_ROWS):
            span = slice(b * BLK_ROWS, (b + 1) * BLK_ROWS)
            for d in range(owners):
                kept = jnp.where(owner_of[b] == d, value[:, span], jnp.zeros_like(value[:, span]))
                wide[d * rank : (d + 1) * rank, span] = kept


def steps_gradient_kernel(owners, rank, terms, scale_in, scale_out, place, owner_of, *refs):
    sums, rows, outs = refs[:terms], refs[terms], refs[terms + 1 : terms + 1 + owners]
    wide, coded = refs[-2:]
    spread_rows(owners, rank, scale_in, owner_of, sums, wide)
    product = scale_out * jnp.dot(wide[...], rows[...], preferred_element_type=jnp.float32)
    coded[...] = product.astype(coded.dtype)
    for d in range(owners):
        owner = lax.rem(place[0] - d + owners, owners)
        outs[d][...] = coded[pl.ds(pl.multiple_of(owner * rank, rank), rank), :]


def steps_gradients(place, owner_of, sums, rows, owners, half, scale_in, scale_out, deps):
    rank, row_count = sums[0].shape
    whole = pl.BlockSpec((rank, row_count), lambda h, place, owner_of: (0, 0))
    return pl.pallas_call(
        behind(
            functools.partial(
                steps_gradient_kernel, owners, rank, len(sums), scale_in, scale_out
            ),
            deps,
            2,
        ),
        grid_spec=pltpu.PrefetchScalarGridSpec(
            num_scalar_prefetch=2,
            grid=(2,),
            in_specs=[ANY] * len(deps)
            + [whole] * len(sums)
            + [
                pl.BlockSpec(
                    (row_count, half),
                    lambda h, place, owner_of: (0, jnp.where(h == 0, place[1], 1 - place[1])),
                )
            ],
            out_specs=[pl.BlockSpec((None, rank, half), lambda h, place, owner_of: (h, 0, 0))]
            * owners
            + [pl.BlockSpec((owners * rank, row_count), lambda h, place, owner_of: (0, 0))],
            scratch_shapes=[pltpu.VMEM((owners * rank, half), jnp.bfloat16)],
        ),
        out_shape=[jax.ShapeDtypeStruct((2, rank, half), jnp.bfloat16)] * owners
        + [jax.ShapeDtypeStruct((owners * rank, row_count), jnp.bfloat16)],
        compiler_params=params(),
        cost_estimate=cost(4),
        name="steps_gradients",
    )(place, owner_of, *deps, *sums, rows)


def collect_kernel(owners, *refs):
    for d in range(owners):
        refs[-1][d] = refs[d][...]


def collect(messages, deps):
    owners, (_, rank, half) = len(messages), messages[0].shape
    return pl.pallas_call(
        behind(functools.partial(collect_kernel, owners), deps),
        grid=(1,),
        in_specs=[ANY] * len(deps) + [pl.BlockSpec((None, rank, half), lambda i: (1, 0, 0))] * owners,
        out_specs=pl.BlockSpec((owners, rank, half), lambda i: (0, 0, 0)),
        out_shape=jax.ShapeDtypeStruct((owners, rank, half), messages[0].dtype),
        compiler_params=params(),
        cost_estimate=cost(1),
        name="collect",
    )(*deps, *messages)


def gradient_kernel(owners, rank, terms, scale_in, scale_out, owner_of, *refs):
    sums, (rows, out, wide) = refs[:terms], refs[terms:]
    spread_rows(owners, rank, scale_in, owner_of, sums, wide)
    product = scale_out * jnp.dot(wide[...], rows[...], preferred_element_type=jnp.float32)
    out[...] = encode(product, out.dtype).reshape(out.shape)


def gradients(owner_of, sums, rows, owners, half, scale_in, scale_out, kind, deps):
    rank, row_count = sums[0].shape
    cores = rows.shape[1] // half
    lanes = half + (LEVEL_LANES if kind == jnp.int16 else 0)
    whole = pl.BlockSpec((rank, row_count), lambda h: (0, 0))
    return pl.pallas_call(
        behind(
            functools.partial(gradient_kernel, owners, rank, len(sums), scale_in, scale_out), deps
        ),
        grid=(cores,),
        in_specs=[ANY] * len(deps)
        + [SMEM]
        + [whole] * len(sums)
        + [pl.BlockSpec((row_count, half), lambda h: (0, h))],
        out_specs=[
            pl.BlockSpec((owners, None, rank, lanes), lambda h: (0, h, 0, 0)),
            pl.BlockSpec((owners * rank, row_count), lambda h: (0, 0)),
        ],
        out_shape=[
            jax.ShapeDtypeStruct((owners, cores, rank, lanes), kind),
            jax.ShapeDtypeStruct((owners * rank, row_count), jnp.bfloat16),
        ],
        compiler_params=params(),
        cost_estimate=cost(4),
        name="gradients",
    )(*deps, owner_of, *sums, rows)


def share_kernel(spans, rows, weight, *outs):
    product = jnp.dot(rows[...], weight[...], preferred_element_type=jnp.float32)
    for out, (start, count) in zip(outs, spans):
        out[...] = product[start : start + count, :].astype(out.dtype)


def share(tokens, weight, piece, start, total, spans, width, deps):
    features = tokens.shape[1]
    tile = min(512, width)
    tiles = width // tile
    return pl.pallas_call(
        behind(functools.partial(share_kernel, spans), deps),
        grid=(tiles,),
        in_specs=[ANY] * len(deps)
        + [
            pl.BlockSpec((total, features), lambda j: (start // total, 0)),
            pl.BlockSpec((features, tile), lambda j: (0, piece * tiles + j)),
        ],
        out_specs=[pl.BlockSpec((count, tile), lambda j: (0, j)) for _, count in spans],
        out_shape=[jax.ShapeDtypeStruct((count, width), jnp.bfloat16) for _, count in spans],
        compiler_params=params(),
        cost_estimate=cost(4.0 * total / 256),
        name="share",
    )(*deps, tokens, weight)


def finish_kernel(flags, spans, mine_is_own, wide, adapters, *refs):
    arrays, out = refs[: len(flags)], refs[-1]
    step = pl.program_id(0)
    turned = wide[...].T
    half = adapters.shape[1] // 2
    for h in range(2):
        span = slice(h * half, (h + 1) * half)
        total = ADAPTER_SCALE * jnp.dot(
            turned, adapters[:, span], preferred_element_type=jnp.float32
        )
        for array, flag, (first, last) in zip(arrays, flags, spans):
            active = jnp.logical_and(step >= first, step < last)
            active = jnp.logical_and(active, mine_is_own[0] == flag)
            total = total + jnp.where(active, array[:, span].astype(jnp.float32), 0.0)
        out[:, span] = total.astype(out.dtype)


def finish(mine_is_own, wide, adapters, row_count, start, count, terms, previous, deps):
    stacked, width = adapters.shape
    tile = min(256, count)
    first = start // tile
    specs, spans = [], []
    for array, row, flag in terms:
        low, many = (row - start) // tile, array.shape[0] // tile

        def block_of(i, mine, low=low, many=many, flag=flag):
            return (jnp.where(mine[0] == flag, jnp.clip(i - low, 0, many - 1), 0), 0)

        specs.append(pl.BlockSpec((tile, width), block_of))
        spans.append((low, low + many))
    operands = [mine_is_own, *deps, wide, adapters]
    operands += [t[0] for t in terms]
    in_specs = (
        [ANY] * len(deps)
        + [
            pl.BlockSpec((stacked, tile), lambda i, mine: (0, first + i)),
            pl.BlockSpec((stacked, width), lambda i, mine: (0, 0)),
        ]
        + specs
    )
    aliases = {}
    if previous is not None:
        aliases = {len(operands): 0}
        operands.append(previous)
        in_specs.append(ANY)
    return pl.pallas_call(
        behind(functools.partial(finish_kernel, [t[2] for t in terms], spans), deps, 1),
        grid_spec=pltpu.PrefetchScalarGridSpec(
            num_scalar_prefetch=1,
            grid=(count // tile,),
            in_specs=in_specs,
            out_specs=pl.BlockSpec((tile, width), lambda i, mine: (first + i, 0)),
        ),
        out_shape=jax.ShapeDtypeStruct((row_count, width), jnp.bfloat16),
        input_output_aliases=aliases,
        compiler_params=params(),
        cost_estimate=cost(4),
        name="finish",
    )(*operands)


def adam_step(slots, used, corr, param, first, second, new_param, new_first, new_second, grads):
    for k in range(slots):
        grad = grads[k]
        one = BETA_ONE * first[k] + (1.0 - BETA_ONE) * grad
        two = BETA_TWO * second[k] + (1.0 - BETA_TWO) * grad * grad
        update = LEARN_RATE * (one / corr[k]) / (jnp.sqrt(two / corr[slots + k]) + ADAM_EPS)
        keep = used[k] == 1
        new_param[k] = jnp.where(keep, param[k] - update, param[k])
        new_first[k] = jnp.where(keep, one, first[k])
        new_second[k] = jnp.where(keep, two, second[k])


def coded_adam_kernel(devices, slots, place, pick, used, corr, param, first, second, *refs):
    messages, levels = refs[:2]
    grads = refs[-1]
    grads[...] = jnp.zeros_like(grads)
    for device in range(devices):
        k = pick[device]
        level = levels[device].astype(jnp.float32)[:, :1]
        scale = jnp.exp2(level * (1.0 / LEVELS)) * (1.0 / TOP_CODE)
        grads[k] = grads[k] + messages[device].astype(jnp.float32) * scale
    adam_step(slots, used, corr, param, first, second, *refs[-4:])


def steps_adam_kernel(owners, slots, place, pick, used, corr, param, first, second, *refs):
    near, far, grads = refs[:owners], refs[owners], refs[-1]
    grads[...] = jnp.zeros_like(grads)
    for d in range(owners):
        device = lax.rem(place[0] + d, owners) * 2
        k = pick[device + place[1]]
        grads[k] = grads[k] + near[d][...].astype(jnp.float32)
        k = pick[device + 1 - place[1]]
        grads[k] = grads[k] + far[d].astype(jnp.float32)
    adam_step(slots, used, corr, param, first, second, *refs[-4:])


def adam(kernel, tables, states, messages, message_specs, deps):
    slots, rank, half = states[0].shape
    tile = feature_tile(half)
    state = pl.BlockSpec((slots, rank, tile), lambda i: (0, 0, i))
    return pl.pallas_call(
        behind(kernel, deps),
        grid=(half // tile,),
        in_specs=[ANY] * len(deps) + [SMEM] * len(tables) + [state] * 3 + message_specs,
        out_specs=[state] * 3,
        out_shape=[dims(states[0])] * 3,
        scratch_shapes=[pltpu.VMEM((slots, rank, tile), jnp.float32)],
        compiler_params=params(),
        cost_estimate=cost(4),
        name="adam",
    )(*deps, *tables, *states, *messages)


def feature_tile(half):
    return min(256, half)


def coded_adam(tables, states, messages, deps):
    devices, rank, _ = messages.shape
    slots, _, half = states[0].shape
    specs = [
        pl.BlockSpec((devices, rank, feature_tile(half)), lambda i: (0, 0, i)),
        pl.BlockSpec((devices, rank, LEVEL_LANES), lambda i: (0, 0, half // LEVEL_LANES)),
    ]
    kernel = functools.partial(coded_adam_kernel, devices, slots)
    return adam(kernel, tables, states, [messages] * 2, specs, deps)


def steps_adam(tables, states, near, far, deps):
    owners, rank, half = far.shape
    tile = feature_tile(half)
    specs = [pl.BlockSpec((None, rank, tile), lambda i: (0, 0, i))] * owners
    specs.append(pl.BlockSpec((owners, rank, tile), lambda i: (0, 0, i)))
    kernel = functools.partial(steps_adam_kernel, owners, states[0].shape[0])
    return adam(kernel, tables, states, [*near, far], specs, deps)


def on_device(
    tokens,
    frozen_weight,
    cotangent,
    down_adapters,
    up_adapters,
    down_first_moment,
    up_first_moment,
    down_second_moment,
    up_second_moment,
    optimizer_steps,
    slot_of_tenant,
    tenant_of_block,
):
    row_count, din_local = tokens.shape
    width = cotangent.shape[1]
    block_count = row_count // BLK_ROWS
    owners = lax.axis_size("dp")
    cores = lax.axis_size("sub")
    columns = lax.axis_size("tensor")
    z = lax.axis_index("dp")
    s = lax.axis_index("sub")
    x = lax.axis_index("tensor")
    slots, half, rank = down_adapters.shape
    flip = lambda v: jnp.swapaxes(v, 1, 2)
    down_adapters, up_adapters = flip(down_adapters), flip(up_adapters)
    down_first_moment, up_first_moment = flip(down_first_moment), flip(up_first_moment)
    down_second_moment, up_second_moment = flip(down_second_moment), flip(up_second_moment)
    per_half = columns // cores
    place = jnp.stack([z, s]).astype(jnp.int32)

    devices = owners * cores

    def tables(deps):
        return pl.pallas_call(
            behind(functools.partial(tables_kernel, devices, cores, slots, block_count), deps),
            in_specs=[ANY] * len(deps) + [SMEM] * 3,
            out_specs=[SMEM] * 3,
            out_shape=[
                jax.ShapeDtypeStruct((devices,), jnp.int32),
                jax.ShapeDtypeStruct((block_count,), jnp.int32),
                jax.ShapeDtypeStruct((slots,), jnp.int32),
            ],
            cost_estimate=cost(2),
            name="tables",
        )(*deps, place, slot_of_tenant, tenant_of_block)

    steps = (optimizer_steps + 1).astype(jnp.float32)
    corr = jnp.concatenate(
        [
            1.0 - jnp.power(jnp.float32(BETA_ONE), steps),
            1.0 - jnp.power(jnp.float32(BETA_TWO), steps),
        ]
    )

    def pack(own, deps):
        return pl.pallas_call(
            behind(functools.partial(pack_kernel, devices), deps),
            in_specs=[ANY] * len(deps) + [SMEM, pl.BlockSpec(memory_space=pltpu.VMEM)],
            out_specs=pl.BlockSpec(memory_space=pltpu.VMEM),
            out_shape=jax.ShapeDtypeStruct((devices, rank, half), jnp.bfloat16),
            compiler_params=params(),
            cost_estimate=cost(1),
            name="pack",
        )(*deps, pick, own)

    def spread_out(messages):
        flat = messages.reshape((devices,) + messages.shape[-2:])
        return lax.all_to_all(flat, ("dp", "sub"), split_axis=0, concat_axis=0, tiled=True)

    def by_owner(arrived):
        return arrived.reshape(owners, cores, rank, half)

    def pack_wide(own, other, deps):
        return pl.pallas_call(
            behind(functools.partial(pack_wide_kernel, owners, cores), deps),
            in_specs=[ANY] * len(deps)
            + [SMEM] * 2
            + [pl.BlockSpec(memory_space=pltpu.VMEM)] * 2,
            out_specs=[pl.BlockSpec(memory_space=pltpu.VMEM)] * owners,
            out_shape=[jax.ShapeDtypeStruct((rank, cores * half), jnp.bfloat16)] * owners,
            compiler_params=params(),
            cost_estimate=cost(1),
            name="pack_wide",
        )(*deps, place, pick, own, other)

    def along(messages, sign):
        return [m if d == 0 else rotate(m, "dp", sign * d) for d, m in enumerate(messages)]

    def shares(rows, start, total, spans, deps):
        pieces = []
        for piece in range(per_half):
            pieces.append(share(rows, frozen_weight, piece, start, total, spans, width, deps))
            deps = [pieces[-1][0]]
        return [list(chunk) for chunk in zip(*pieces)]

    def piece_for(chunk, target):
        if per_half == 1:
            return chunk[0]
        out = chunk[0]
        for piece in range(1, per_half):
            out = jnp.where(lax.rem(target, per_half) == piece, chunk[piece], out)
        return out

    def send(chunk, cross):
        got = []
        for step in range(1, columns):
            pairs = []
            for t in range(columns):
                for c in range(cores):
                    target = (t + step) % columns
                    if target // per_half == c:
                        pairs.append((t * cores + c, target * cores + (c + cross) % cores))
            operand = piece_for(chunk, lax.rem(x + step, columns))
            got.append(lax.ppermute(operand, ("tensor", "sub"), pairs))
        return got

    def send_local(chunk):
        pairs = []
        for t in range(columns):
            c = t // per_half
            pairs.append((t * cores + c, t * cores + (c + 1) % cores))
        return lax.ppermute(piece_for(chunk, x), ("tensor", "sub"), pairs)

    def exchange(part):
        return [part] + [rotate(part, "tensor", step) for step in range(1, columns)]

    half_rows = row_count // 2
    one_half = [(0, half_rows)]
    both = one_half * 2
    up_other = rotate(up_adapters, "sub", 1)
    other_tokens = rotate(tokens, "sub", 1)
    pick, owner_of, used = tables([])
    down_packed = pack(down_adapters, [])
    down_arrived = by_owner(spread_out(down_packed))
    own_a, = shares(tokens, 0, half_rows, one_half, [down_packed])
    got_a = send(own_a, 0)
    up_packed = pack_wide(up_adapters, up_other, [own_a[-1]])
    up_parts = along(up_packed, 1)
    own_b, = shares(tokens, half_rows, half_rows, one_half, [up_packed[0]])

    down_part = adapter_product(owner_of, down_arrived, tokens, [own_b[-1], other_tokens])
    down_sums = exchange(down_part)
    own_b = tie(own_b, [down_part] + got_a)
    got_b = send(own_b, 0)
    cross_a, cross_a_near = shares(other_tokens, 0, half_rows, both, [own_b[-1]])
    back_part, up_cat = steps_product(place, owner_of, up_parts, cotangent, [cross_a[-1]])
    back_sums = exchange(back_part)
    *up_messages, down_wide = steps_gradients(
        place, owner_of, down_sums, cotangent, owners, half, 1.0, ADAPTER_SCALE, [back_part]
    )
    up_returned = along(up_messages, -1)
    cross_a = tie(cross_a, [up_messages[0]] + got_b)
    late_a = send(cross_a, 1)
    cross_b, cross_b_near = shares(other_tokens, half_rows, half_rows, both, [cross_a[-1]])
    down_messages, back_wide = gradients(
        owner_of, back_sums, tokens, owners, half, ADAPTER_SCALE, 1.0, jnp.int16,
        [cross_b[-1]],
    )
    down_returned = spread_out(down_messages)
    cross_b = tie(cross_b, late_a + [down_messages])
    late_b = send(cross_b, 1)
    up_far = rotate(collect(up_returned, [cross_b[-1]]), "sub", 1)
    cross_a_near = tie(cross_a_near, [cross_b[-1]])
    local_a = send_local(cross_a_near)
    cross_b_near = tie(cross_b_near, [local_a])
    local_b = send_local(cross_b_near)

    tables_in = [place, pick, used, corr]
    fresh_up, fresh_up_first, fresh_up_second = steps_adam(
        tables_in, [up_adapters, up_first_moment, up_second_moment], up_returned, up_far,
        [cross_b[-1]],
    )
    mine_is_own = (lax.div(x, per_half) == s).astype(jnp.int32).reshape(1)
    terms_a = [(piece_for(own_a, x), 0, 1), (local_a, 0, 0)]
    terms_a += [(g, 0, 1) for g in got_a] + [(g, 0, 0) for g in late_a]
    terms_b = [(piece_for(own_b, x), half_rows, 1), (local_b, half_rows, 0)]
    terms_b += [(g, half_rows, 1) for g in got_b] + [(g, half_rows, 0) for g in late_b]
    projected = finish(
        mine_is_own, down_wide, up_cat, row_count, 0, half_rows, terms_a, None, [fresh_up]
    )
    projected = finish(
        mine_is_own, down_wide, up_cat, row_count, half_rows, half_rows, terms_b, projected, []
    )
    fresh_down, fresh_down_first, fresh_down_second = coded_adam(
        tables_in, [down_adapters, down_first_moment, down_second_moment], down_returned,
        [projected],
    )
    return (
        projected,
        flip(fresh_down),
        flip(fresh_up),
        flip(fresh_down_first),
        flip(fresh_up_first),
        flip(fresh_down_second),
        flip(fresh_up_second),
    )


def solution(mesh):
    placed = (
        P(("groups", "dp", "sub"), "tensor"),
        P("tensor", "sub"),
        P(("groups", "dp", "sub"), "tensor"),
        P(("groups", "dp"), ("tensor", "sub"), None),
        P(("groups", "dp"), ("tensor", "sub"), None),
        P(("groups", "dp"), ("tensor", "sub"), None),
        P(("groups", "dp"), ("tensor", "sub"), None),
        P(("groups", "dp"), ("tensor", "sub"), None),
        P(("groups", "dp"), ("tensor", "sub"), None),
        P(("groups", "dp")),
        P("groups"),
        P("groups"),
    )
    return jax.shard_map(
        on_device,
        mesh=mesh,
        in_specs=placed,
        out_specs=(
            P(("groups", "dp", "sub"), "tensor"),
            P(("groups", "dp"), ("tensor", "sub"), None),
            P(("groups", "dp"), ("tensor", "sub"), None),
            P(("groups", "dp"), ("tensor", "sub"), None),
            P(("groups", "dp"), ("tensor", "sub"), None),
            P(("groups", "dp"), ("tensor", "sub"), None),
            P(("groups", "dp"), ("tensor", "sub"), None),
        ),
        check_vma=False,
    )
```

```python
import functools

import jax
import jax.numpy as jnp
from jax import lax
from jax.experimental import pallas as pl
from jax.experimental.pallas import tpu as pltpu
from jax.sharding import PartitionSpec as P

BLK_ROWS = 128


ADAPTER_SCALE = 2.0
BETA_ONE = 0.9
BETA_TWO = 0.999
LEARN_RATE = 0.01
ADAM_EPS = 1e-08

SMEM = pl.BlockSpec(memory_space=pltpu.SMEM)
VMEM_BYTES = 63_000_000
TOP_CODE = 32767.0
LEVELS = 64.0
LEVEL_LANES = 128
COST = 20.0


def params():
    return pltpu.CompilerParams(vmem_limit_bytes=VMEM_BYTES)


def cost(micros):
    flops = int(micros * 1_000_000_000 * COST)
    return pl.CostEstimate(flops=flops, bytes_accessed=1000, transcendentals=0)


def rotate(value, axis, shift):
    size = lax.axis_size(axis)
    return lax.ppermute(value, axis, [(i, (i + shift) % size) for i in range(size)])


ANY = pl.BlockSpec(memory_space=pl.ANY)


def behind(kernel, deps, scalars=0):
    return lambda *refs: kernel(*refs[:scalars], *refs[scalars + len(deps) :])


def tie_kernel(*refs):
    pass


def tie(values, deps):
    return pl.pallas_call(
        tie_kernel,
        in_specs=[ANY] * (len(values) + len(deps)),
        out_specs=[ANY] * len(values),
        out_shape=[dims(v) for v in values],
        input_output_aliases={k: k for k in range(len(values))},
        cost_estimate=cost(100),
        name="tie",
    )(*values, *deps)


def dims(value):
    return jax.ShapeDtypeStruct(value.shape, value.dtype)


def tables_kernel(devices, cores, slots, block_count, place, slot_of, tenant_of, pick, owner_of, used):
    z, s = place[0], place[1]
    for k in range(slots):
        used[k] = 0

    def slot_at(device, b):
        return slot_of[tenant_of[device * block_count + b]]

    def per_device(device, carry):
        def per_block(b, found):
            local = slot_at(device, b) - z * slots
            mine = jnp.logical_and(local >= 0, local < slots)

            @pl.when(mine)
            def _():
                used[local] = 1

            return jnp.where(mine, local, found)

        pick[device] = lax.fori_loop(0, block_count, per_block, 0)
        return carry

    lax.fori_loop(0, devices, per_device, 0)
    for b in range(block_count):
        owner_of[b] = lax.div(slot_at(z * cores + s, b), slots)


def pack_kernel(devices, pick, down, up, out):
    rank = down.shape[1]
    for device in range(devices):
        out[device, :rank] = down[pick[device]].astype(jnp.bfloat16)
        out[device, rank:] = up[pick[device]].astype(jnp.bfloat16)


def product_kernel(owners, cores, rank, tile_rows, owner_of, *refs):
    halves, (rows, out, cat) = refs[:cores], refs[cores:]
    step = pl.program_id(0)
    half = halves[0].shape[-1]

    @pl.when(step == 0)
    def _():
        for h in range(cores):
            cat[:, h * half : (h + 1) * half] = halves[h][...].reshape(owners * rank, half)

    full = lax.dot_general(
        cat[...], rows[...], (((1,), (1,)), ((), ())), preferred_element_type=jnp.float32
    )
    for b in range(tile_rows // BLK_ROWS):
        owner = owner_of[step * (tile_rows // BLK_ROWS) + b]
        span = slice(b * BLK_ROWS, (b + 1) * BLK_ROWS)
        value = full[:rank, span]
        for d in range(1, owners):
            value = jnp.where(owner == d, full[d * rank : (d + 1) * rank, span], value)
        out[:, span] = value


def adapter_product(owner_of, adapters, kind, rank, rows, deps):
    (owners, cores, _, half), (row_count, features) = adapters.shape, rows.shape
    tile = min(256, row_count)
    return pl.pallas_call(
        behind(functools.partial(product_kernel, owners, cores, rank, tile), deps),
        grid=(row_count // tile,),
        in_specs=[ANY] * len(deps)
        + [SMEM]
        + [
            pl.BlockSpec((owners, None, rank, half), lambda i, h=h: (0, h, kind, 0))
            for h in range(cores)
        ]
        + [pl.BlockSpec((tile, features), lambda i: (i, 0))],
        out_specs=[
            pl.BlockSpec((rank, tile), lambda i: (0, i)),
            pl.BlockSpec((owners * rank, features), lambda i: (0, 0)),
        ],
        out_shape=[
            jax.ShapeDtypeStruct((rank, row_count), jnp.float32),
            jax.ShapeDtypeStruct((owners * rank, features), jnp.bfloat16),
        ],
        compiler_params=params(),
        cost_estimate=cost(5),
        name="adapter_product",
    )(*deps, owner_of, *[adapters] * cores, rows)


def encode(product, kind):
    if kind != jnp.int16:
        return product.astype(kind)
    top = jnp.maximum(jnp.max(jnp.abs(product), axis=1, keepdims=True), 1e-30)
    level = jnp.floor(jnp.log2(top) * LEVELS) + 2.0
    coded = jnp.round(product * (TOP_CODE * jnp.exp2(level * (-1.0 / LEVELS))))
    coded = jnp.clip(coded, -TOP_CODE, TOP_CODE).astype(jnp.int32).astype(jnp.int16)
    lanes = jnp.broadcast_to(level, (product.shape[0], LEVEL_LANES))
    return jnp.concatenate([coded, lanes.astype(jnp.int32).astype(jnp.int16)], axis=1)


def spread_rows(owners, rank, scale_in, owner_of, sums, wide):
    @pl.when(pl.program_id(0) == 0)
    def _():
        total = sums[0][...]
        for term in sums[1:]:
            total = total + term[...]
        value = (scale_in * total).astype(jnp.bfloat16)
        for b in range(value.shape[1] // BLK_ROWS):
            span = slice(b * BLK_ROWS, (b + 1) * BLK_ROWS)
            for d in range(owners):
                kept = jnp.where(owner_of[b] == d, value[:, span], jnp.zeros_like(value[:, span]))
                wide[d * rank : (d + 1) * rank, span] = kept


def steps_gradient_kernel(owners, rank, terms, scale_in, scale_out, place, owner_of, *refs):
    sums, rows, outs = refs[:terms], refs[terms], refs[terms + 1 : terms + 1 + owners]
    wide, coded = refs[-2:]
    spread_rows(owners, rank, scale_in, owner_of, sums, wide)
    product = scale_out * jnp.dot(wide[...], rows[...], preferred_element_type=jnp.float32)
    coded[...] = product.astype(coded.dtype)
    for d in range(owners):
        owner = lax.rem(place[0] - d + owners, owners)
        outs[d][...] = coded[pl.ds(pl.multiple_of(owner * rank, rank), rank), :]


def steps_gradients(place, owner_of, sums, rows, owners, half, scale_in, scale_out, deps):
    rank, row_count = sums[0].shape
    whole = pl.BlockSpec((rank, row_count), lambda h, place, owner_of: (0, 0))
    return pl.pallas_call(
        behind(
            functools.partial(
                steps_gradient_kernel, owners, rank, len(sums), scale_in, scale_out
            ),
            deps,
            2,
        ),
        grid_spec=pltpu.PrefetchScalarGridSpec(
            num_scalar_prefetch=2,
            grid=(2,),
            in_specs=[ANY] * len(deps)
            + [whole] * len(sums)
            + [
                pl.BlockSpec(
                    (row_count, half),
                    lambda h, place, owner_of: (0, jnp.where(h == 0, place[1], 1 - place[1])),
                )
            ],
            out_specs=[pl.BlockSpec((None, rank, half), lambda h, place, owner_of: (h, 0, 0))]
            * owners
            + [pl.BlockSpec((owners * rank, row_count), lambda h, place, owner_of: (0, 0))],
            scratch_shapes=[pltpu.VMEM((owners * rank, half), jnp.bfloat16)],
        ),
        out_shape=[jax.ShapeDtypeStruct((2, rank, half), jnp.bfloat16)] * owners
        + [jax.ShapeDtypeStruct((owners * rank, row_count), jnp.bfloat16)],
        compiler_params=params(),
        cost_estimate=cost(4),
        name="steps_gradients",
    )(place, owner_of, *deps, *sums, rows)


def collect_kernel(owners, *refs):
    for d in range(owners):
        refs[-1][d] = refs[d][...]


def collect(messages, deps):
    owners, (_, rank, half) = len(messages), messages[0].shape
    return pl.pallas_call(
        behind(functools.partial(collect_kernel, owners), deps),
        grid=(1,),
        in_specs=[ANY] * len(deps) + [pl.BlockSpec((None, rank, half), lambda i: (1, 0, 0))] * owners,
        out_specs=pl.BlockSpec((owners, rank, half), lambda i: (0, 0, 0)),
        out_shape=jax.ShapeDtypeStruct((owners, rank, half), messages[0].dtype),
        compiler_params=params(),
        cost_estimate=cost(1),
        name="collect",
    )(*deps, *messages)


def gradient_kernel(owners, rank, terms, scale_in, scale_out, owner_of, *refs):
    sums, (rows, out, wide) = refs[:terms], refs[terms:]
    spread_rows(owners, rank, scale_in, owner_of, sums, wide)
    product = scale_out * jnp.dot(wide[...], rows[...], preferred_element_type=jnp.float32)
    out[...] = encode(product, out.dtype).reshape(out.shape)


def gradients(owner_of, sums, rows, owners, half, scale_in, scale_out, kind, deps):
    rank, row_count = sums[0].shape
    cores = rows.shape[1] // half
    lanes = half + (LEVEL_LANES if kind == jnp.int16 else 0)
    whole = pl.BlockSpec((rank, row_count), lambda h: (0, 0))
    return pl.pallas_call(
        behind(
            functools.partial(gradient_kernel, owners, rank, len(sums), scale_in, scale_out), deps
        ),
        grid=(cores,),
        in_specs=[ANY] * len(deps)
        + [SMEM]
        + [whole] * len(sums)
        + [pl.BlockSpec((row_count, half), lambda h: (0, h))],
        out_specs=[
            pl.BlockSpec((owners, None, rank, lanes), lambda h: (0, h, 0, 0)),
            pl.BlockSpec((owners * rank, row_count), lambda h: (0, 0)),
        ],
        out_shape=[
            jax.ShapeDtypeStruct((owners, cores, rank, lanes), kind),
            jax.ShapeDtypeStruct((owners * rank, row_count), jnp.bfloat16),
        ],
        compiler_params=params(),
        cost_estimate=cost(4),
        name="gradients",
    )(*deps, owner_of, *sums, rows)


def share_kernel(spans, rows, weight, *outs):
    product = jnp.dot(rows[...], weight[...], preferred_element_type=jnp.float32)
    for out, (start, count) in zip(outs, spans):
        out[...] = product[start : start + count, :].astype(out.dtype)


def share(tokens, weight, piece, start, total, spans, width, deps):
    features = tokens.shape[1]
    tile = min(512, width)
    tiles = width // tile
    return pl.pallas_call(
        behind(functools.partial(share_kernel, spans), deps),
        grid=(tiles,),
        in_specs=[ANY] * len(deps)
        + [
            pl.BlockSpec((total, features), lambda j: (start // total, 0)),
            pl.BlockSpec((features, tile), lambda j: (0, piece * tiles + j)),
        ],
        out_specs=[pl.BlockSpec((count, tile), lambda j: (0, j)) for _, count in spans],
        out_shape=[jax.ShapeDtypeStruct((count, width), jnp.bfloat16) for _, count in spans],
        compiler_params=params(),
        cost_estimate=cost(4.0 * total / 256),
        name="share",
    )(*deps, tokens, weight)


def finish_kernel(flags, spans, mine_is_own, wide, adapters, *refs):
    arrays, out = refs[: len(flags)], refs[-1]
    step = pl.program_id(0)
    turned = wide[...].T
    half = adapters.shape[1] // 2
    for h in range(2):
        span = slice(h * half, (h + 1) * half)
        total = ADAPTER_SCALE * jnp.dot(
            turned, adapters[:, span], preferred_element_type=jnp.float32
        )
        for array, flag, (first, last) in zip(arrays, flags, spans):
            active = jnp.logical_and(step >= first, step < last)
            active = jnp.logical_and(active, mine_is_own[0] == flag)
            total = total + jnp.where(active, array[:, span].astype(jnp.float32), 0.0)
        out[:, span] = total.astype(out.dtype)


def finish(mine_is_own, wide, adapters, row_count, start, count, terms, previous, deps):
    stacked, width = adapters.shape
    tile = 256 if all(t[1] % 256 == 0 for t in terms) else BLK_ROWS
    first = start // tile
    specs, spans = [], []
    for array, row, flag in terms:
        low, many = (row - start) // tile, array.shape[0] // tile

        def block_of(i, mine, low=low, many=many, flag=flag):
            return (jnp.where(mine[0] == flag, jnp.clip(i - low, 0, many - 1), 0), 0)

        specs.append(pl.BlockSpec((tile, width), block_of))
        spans.append((low, low + many))
    operands = [mine_is_own, *deps, wide, adapters]
    operands += [t[0] for t in terms]
    in_specs = (
        [ANY] * len(deps)
        + [
            pl.BlockSpec((stacked, tile), lambda i, mine: (0, first + i)),
            pl.BlockSpec((stacked, width), lambda i, mine: (0, 0)),
        ]
        + specs
    )
    aliases = {}
    if previous is not None:
        aliases = {len(operands): 0}
        operands.append(previous)
        in_specs.append(ANY)
    return pl.pallas_call(
        behind(functools.partial(finish_kernel, [t[2] for t in terms], spans), deps, 1),
        grid_spec=pltpu.PrefetchScalarGridSpec(
            num_scalar_prefetch=1,
            grid=(count // tile,),
            in_specs=in_specs,
            out_specs=pl.BlockSpec((tile, width), lambda i, mine: (first + i, 0)),
        ),
        out_shape=jax.ShapeDtypeStruct((row_count, width), jnp.bfloat16),
        input_output_aliases=aliases,
        compiler_params=params(),
        cost_estimate=cost(4),
        name="finish",
    )(*operands)


def adam_step(slots, used, corr, param, first, second, new_param, new_first, new_second, grads):
    for k in range(slots):
        grad = grads[k]
        one = BETA_ONE * first[k] + (1.0 - BETA_ONE) * grad
        two = BETA_TWO * second[k] + (1.0 - BETA_TWO) * grad * grad
        update = LEARN_RATE * (one / corr[k]) / (jnp.sqrt(two / corr[slots + k]) + ADAM_EPS)
        keep = used[k] == 1
        new_param[k] = jnp.where(keep, param[k] - update, param[k])
        new_first[k] = jnp.where(keep, one, first[k])
        new_second[k] = jnp.where(keep, two, second[k])


def coded_adam_kernel(devices, slots, place, pick, used, corr, param, first, second, *refs):
    messages, levels = refs[:2]
    grads = refs[-1]
    grads[...] = jnp.zeros_like(grads)
    for device in range(devices):
        k = pick[device]
        level = levels[device].astype(jnp.float32)[:, :1]
        scale = jnp.exp2(level * (1.0 / LEVELS)) * (1.0 / TOP_CODE)
        grads[k] = grads[k] + messages[device].astype(jnp.float32) * scale
    adam_step(slots, used, corr, param, first, second, *refs[-4:])


def steps_adam_kernel(owners, slots, place, pick, used, corr, param, first, second, *refs):
    near, far, grads = refs[:owners], refs[owners], refs[-1]
    grads[...] = jnp.zeros_like(grads)
    for d in range(owners):
        device = lax.rem(place[0] + d, owners) * 2
        k = pick[device + place[1]]
        grads[k] = grads[k] + near[d][...].astype(jnp.float32)
        k = pick[device + 1 - place[1]]
        grads[k] = grads[k] + far[d].astype(jnp.float32)
    adam_step(slots, used, corr, param, first, second, *refs[-4:])


def adam(kernel, tables, states, messages, message_specs, deps):
    slots, rank, half = states[0].shape
    tile = feature_tile(half)
    state = pl.BlockSpec((slots, rank, tile), lambda i: (0, 0, i))
    return pl.pallas_call(
        behind(kernel, deps),
        grid=(half // tile,),
        in_specs=[ANY] * len(deps) + [SMEM] * len(tables) + [state] * 3 + message_specs,
        out_specs=[state] * 3,
        out_shape=[dims(states[0])] * 3,
        scratch_shapes=[pltpu.VMEM((slots, rank, tile), jnp.float32)],
        compiler_params=params(),
        cost_estimate=cost(4),
        name="adam",
    )(*deps, *tables, *states, *messages)


def feature_tile(half):
    return min(256, half)


def coded_adam(tables, states, messages, deps):
    devices, rank, _ = messages.shape
    slots, _, half = states[0].shape
    specs = [
        pl.BlockSpec((devices, rank, feature_tile(half)), lambda i: (0, 0, i)),
        pl.BlockSpec((devices, rank, LEVEL_LANES), lambda i: (0, 0, half // LEVEL_LANES)),
    ]
    kernel = functools.partial(coded_adam_kernel, devices, slots)
    return adam(kernel, tables, states, [messages] * 2, specs, deps)


def steps_adam(tables, states, near, far, deps):
    owners, rank, half = far.shape
    tile = feature_tile(half)
    specs = [pl.BlockSpec((None, rank, tile), lambda i: (0, 0, i))] * owners
    specs.append(pl.BlockSpec((owners, rank, tile), lambda i: (0, 0, i)))
    kernel = functools.partial(steps_adam_kernel, owners, states[0].shape[0])
    return adam(kernel, tables, states, [*near, far], specs, deps)


def on_device(
    tokens,
    frozen_weight,
    cotangent,
    down_adapters,
    up_adapters,
    down_first_moment,
    up_first_moment,
    down_second_moment,
    up_second_moment,
    optimizer_steps,
    slot_of_tenant,
    tenant_of_block,
):
    row_count, din_local = tokens.shape
    width = cotangent.shape[1]
    block_count = row_count // BLK_ROWS
    owners = lax.axis_size("dp")
    cores = lax.axis_size("sub")
    columns = lax.axis_size("tensor")
    z = lax.axis_index("dp")
    s = lax.axis_index("sub")
    x = lax.axis_index("tensor")
    slots, half, rank = down_adapters.shape
    flip = lambda v: jnp.swapaxes(v, 1, 2)
    down_adapters, up_adapters = flip(down_adapters), flip(up_adapters)
    down_first_moment, up_first_moment = flip(down_first_moment), flip(up_first_moment)
    down_second_moment, up_second_moment = flip(down_second_moment), flip(up_second_moment)
    per_half = columns // cores
    place = jnp.stack([z, s]).astype(jnp.int32)

    devices = owners * cores

    def tables(deps):
        return pl.pallas_call(
            behind(functools.partial(tables_kernel, devices, cores, slots, block_count), deps),
            in_specs=[ANY] * len(deps) + [SMEM] * 3,
            out_specs=[SMEM] * 3,
            out_shape=[
                jax.ShapeDtypeStruct((devices,), jnp.int32),
                jax.ShapeDtypeStruct((block_count,), jnp.int32),
                jax.ShapeDtypeStruct((slots,), jnp.int32),
            ],
            cost_estimate=cost(2),
            name="tables",
        )(*deps, place, slot_of_tenant, tenant_of_block)

    steps = (optimizer_steps + 1).astype(jnp.float32)
    corr = jnp.concatenate(
        [
            1.0 - jnp.power(jnp.float32(BETA_ONE), steps),
            1.0 - jnp.power(jnp.float32(BETA_TWO), steps),
        ]
    )

    def pack():
        return pl.pallas_call(
            functools.partial(pack_kernel, devices),
            in_specs=[SMEM] + [pl.BlockSpec(memory_space=pltpu.VMEM)] * 2,
            out_specs=pl.BlockSpec(memory_space=pltpu.VMEM),
            out_shape=jax.ShapeDtypeStruct((devices, 2 * rank, half), jnp.bfloat16),
            compiler_params=params(),
            cost_estimate=cost(3),
            name="pack",
        )(pick, down_adapters, up_adapters)

    def spread_out(messages):
        flat = messages.reshape((devices,) + messages.shape[-2:])
        return lax.all_to_all(flat, ("dp", "sub"), split_axis=0, concat_axis=0, tiled=True)

    def along(messages, sign):
        return [m if d == 0 else rotate(m, "dp", sign * d) for d, m in enumerate(messages)]

    def shares(rows, start, total, spans, deps):
        pieces = []
        for piece in range(per_half):
            pieces.append(share(rows, frozen_weight, piece, start, total, spans, width, deps))
            deps = [pieces[-1][0]]
        return [list(chunk) for chunk in zip(*pieces)]

    def piece_for(chunk, target):
        if per_half == 1:
            return chunk[0]
        out = chunk[0]
        for piece in range(1, per_half):
            out = jnp.where(lax.rem(target, per_half) == piece, chunk[piece], out)
        return out

    def send(chunk, cross):
        got = []
        for step in range(1, columns):
            pairs = []
            for t in range(columns):
                for c in range(cores):
                    target = (t + step) % columns
                    if target // per_half == c:
                        pairs.append((t * cores + c, target * cores + (c + cross) % cores))
            operand = piece_for(chunk, lax.rem(x + step, columns))
            got.append(lax.ppermute(operand, ("tensor", "sub"), pairs))
        return got

    def send_local(chunk):
        pairs = []
        for t in range(columns):
            c = t // per_half
            pairs.append((t * cores + c, t * cores + (c + 1) % cores))
        return lax.ppermute(piece_for(chunk, x), ("tensor", "sub"), pairs)

    def exchange(part):
        return [part] + [rotate(part, "tensor", step) for step in range(1, columns)]

    half_rows = row_count // 2
    cut = half_rows * 3 // 4
    one_half = [(0, half_rows)]
    both = one_half * 2
    other_tokens = rotate(tokens, "sub", 1)
    pick, owner_of, used = tables([])
    packed = pack()
    arrived = spread_out(packed).reshape(owners, cores, 2 * rank, half)
    own_a, = shares(tokens, 0, half_rows, one_half, [packed])
    got_a = send(own_a, 0)
    own_b, own_c = shares(
        tokens, half_rows, half_rows, [(0, cut), (cut, half_rows - cut)], [own_a[-1]]
    )
    got_b = send(own_b, 0)
    cross_a, cross_a_near = shares(other_tokens, 0, half_rows, both, [own_b[-1]])
    cross_b, cross_b_near = shares(other_tokens, half_rows, half_rows, both, [cross_a[-1]])

    down_part, _ = adapter_product(owner_of, arrived, 0, rank, tokens, [cross_b[-1]] + got_a)
    down_sums = exchange(down_part)
    back_part, up_cat = adapter_product(owner_of, arrived, 1, rank, cotangent, [down_part])
    back_sums = exchange(back_part)
    own_c = tie(own_c, [back_part])
    got_c = send(own_c, 0)
    *up_messages, down_wide = steps_gradients(
        place, owner_of, down_sums, cotangent, owners, half, 1.0, ADAPTER_SCALE,
        [own_c[-1]] + got_b,
    )
    up_returned = along(up_messages, -1)
    cross_a = tie(cross_a, [up_messages[0], back_sums[-1]])
    late_a = send(cross_a, 1)
    down_messages, back_wide = gradients(
        owner_of, back_sums, tokens, owners, half, ADAPTER_SCALE, 1.0, jnp.int16,
        [cross_a[-1]],
    )
    down_returned = spread_out(down_messages)
    cross_b = tie(cross_b, [down_messages] + got_c)
    late_b = send(cross_b, 1)
    up_far = rotate(collect(up_returned, [cross_b[-1]]), "sub", 1)
    cross_a_near = tie(cross_a_near, [cross_b[-1]] + up_returned[1:])
    local_a = send_local(cross_a_near)
    cross_b_near = tie(cross_b_near, [local_a])
    local_b = send_local(cross_b_near)

    tables_in = [place, pick, used, corr]
    fresh_up, fresh_up_first, fresh_up_second = steps_adam(
        tables_in, [up_adapters, up_first_moment, up_second_moment], up_returned, up_far,
        [cross_b[-1]],
    )
    mine_is_own = (lax.div(x, per_half) == s).astype(jnp.int32).reshape(1)
    terms_a = [(piece_for(own_a, x), 0, 1), (local_a, 0, 0)]
    terms_a += [(g, 0, 1) for g in got_a] + [(g, 0, 0) for g in late_a]
    terms_b = [(piece_for(own_b, x), half_rows, 1), (local_b, half_rows, 0)]
    terms_b.append((piece_for(own_c, x), half_rows + cut, 1))
    terms_b += [(g, half_rows + cut, 1) for g in got_c]
    terms_b += [(g, half_rows, 1) for g in got_b] + [(g, half_rows, 0) for g in late_b]
    projected = finish(
        mine_is_own, down_wide, up_cat, row_count, 0, half_rows, terms_a, None, [fresh_up]
    )
    projected = finish(
        mine_is_own, down_wide, up_cat, row_count, half_rows, half_rows, terms_b, projected, []
    )
    fresh_down, fresh_down_first, fresh_down_second = coded_adam(
        tables_in, [down_adapters, down_first_moment, down_second_moment], down_returned,
        [projected],
    )
    return (
        projected,
        flip(fresh_down),
        flip(fresh_up),
        flip(fresh_down_first),
        flip(fresh_up_first),
        flip(fresh_down_second),
        flip(fresh_up_second),
    )


def solution(mesh):
    placed = (
        P(("groups", "dp", "sub"), "tensor"),
        P("tensor", "sub"),
        P(("groups", "dp", "sub"), "tensor"),
        P(("groups", "dp"), ("tensor", "sub"), None),
        P(("groups", "dp"), ("tensor", "sub"), None),
        P(("groups", "dp"), ("tensor", "sub"), None),
        P(("groups", "dp"), ("tensor", "sub"), None),
        P(("groups", "dp"), ("tensor", "sub"), None),
        P(("groups", "dp"), ("tensor", "sub"), None),
        P(("groups", "dp")),
        P("groups"),
        P("groups"),
    )
    return jax.shard_map(
        on_device,
        mesh=mesh,
        in_specs=placed,
        out_specs=(
            P(("groups", "dp", "sub"), "tensor"),
            P(("groups", "dp"), ("tensor", "sub"), None),
            P(("groups", "dp"), ("tensor", "sub"), None),
            P(("groups", "dp"), ("tensor", "sub"), None),
            P(("groups", "dp"), ("tensor", "sub"), None),
            P(("groups", "dp"), ("tensor", "sub"), None),
            P(("groups", "dp"), ("tensor", "sub"), None),
        ),
        check_vma=False,
    )
```

```python
import functools

import jax
import jax.numpy as jnp
from jax import lax
from jax.experimental import pallas as pl
from jax.experimental.pallas import tpu as pltpu
from jax.sharding import PartitionSpec as P

BLK_ROWS = 128


ADAPTER_SCALE = 2.0
BETA_ONE = 0.9
BETA_TWO = 0.999
LEARN_RATE = 0.01
ADAM_EPS = 1e-08

SMEM = pl.BlockSpec(memory_space=pltpu.SMEM)
VMEM_BYTES = 63_000_000
TOP_CODE = 32767.0
LEVELS = 64.0
LEVEL_LANES = 128
COST = 20.0


def params():
    return pltpu.CompilerParams(vmem_limit_bytes=VMEM_BYTES)


def cost(micros):
    flops = int(micros * 1_000_000_000 * COST)
    return pl.CostEstimate(flops=flops, bytes_accessed=1000, transcendentals=0)


def rotate(value, axis, shift):
    size = lax.axis_size(axis)
    return lax.ppermute(value, axis, [(i, (i + shift) % size) for i in range(size)])


ANY = pl.BlockSpec(memory_space=pl.ANY)


def behind(kernel, deps, scalars=0):
    return lambda *refs: kernel(*refs[:scalars], *refs[scalars + len(deps) :])


def tie_kernel(*refs):
    pass


def tie(values, deps):
    return pl.pallas_call(
        tie_kernel,
        in_specs=[ANY] * (len(values) + len(deps)),
        out_specs=[ANY] * len(values),
        out_shape=[dims(v) for v in values],
        input_output_aliases={k: k for k in range(len(values))},
        cost_estimate=cost(100),
        name="tie",
    )(*values, *deps)


def dims(value):
    return jax.ShapeDtypeStruct(value.shape, value.dtype)


def tables_kernel(devices, cores, slots, block_count, place, slot_of, tenant_of, pick, owner_of, used):
    z, s = place[0], place[1]
    for k in range(slots):
        used[k] = 0

    def slot_at(device, b):
        return slot_of[tenant_of[device * block_count + b]]

    def per_device(device, carry):
        def per_block(b, found):
            local = slot_at(device, b) - z * slots
            mine = jnp.logical_and(local >= 0, local < slots)

            @pl.when(mine)
            def _():
                used[local] = 1

            return jnp.where(mine, local, found)

        pick[device] = lax.fori_loop(0, block_count, per_block, 0)
        return carry

    lax.fori_loop(0, devices, per_device, 0)
    for b in range(block_count):
        owner_of[b] = lax.div(slot_at(z * cores + s, b), slots)


def pack_kernel(devices, pick, own, out):
    for device in range(devices):
        out[device] = own[pick[device]].astype(jnp.bfloat16)


def pack_wide_kernel(owners, cores, place, pick, own, other, *outs):
    z, s = place[0], place[1]
    half = own.shape[2]
    for d in range(owners):
        k = pick[lax.rem(z + d, owners) * cores + s]
        near, far = own[k].astype(jnp.bfloat16), other[k].astype(jnp.bfloat16)
        outs[d][:, :half] = jnp.where(s == 0, near, far)
        outs[d][:, half:] = jnp.where(s == 0, far, near)


def product_kernel(owners, cores, rank, tile_rows, owner_of, *refs):
    halves, (rows, out) = refs[:cores], refs[cores:]
    step = pl.program_id(0)
    half = halves[0].shape[-1]
    full = 0.0
    for h in range(cores):
        full = full + lax.dot_general(
            halves[h][...].reshape(owners * rank, half),
            rows[:, h * half : (h + 1) * half],
            (((1,), (1,)), ((), ())),
            preferred_element_type=jnp.float32,
        )
    for b in range(tile_rows // BLK_ROWS):
        owner = owner_of[step * (tile_rows // BLK_ROWS) + b]
        span = slice(b * BLK_ROWS, (b + 1) * BLK_ROWS)
        value = full[:rank, span]
        for d in range(1, owners):
            value = jnp.where(owner == d, full[d * rank : (d + 1) * rank, span], value)
        out[:, span] = value


def steps_product_kernel(owners, rank, tile_rows, place, owner_of, *refs):
    parts, (rows, out, cat) = refs[:owners], refs[owners:]
    step = pl.program_id(0)

    @pl.when(step == 0)
    def _():
        for d in range(owners):
            owner = lax.rem(place[0] - d + owners, owners)
            cat[pl.ds(pl.multiple_of(owner * rank, rank), rank), :] = parts[d][...]

    full = lax.dot_general(
        cat[...], rows[...], (((1,), (1,)), ((), ())), preferred_element_type=jnp.float32
    )
    for b in range(tile_rows // BLK_ROWS):
        owner = owner_of[step * (tile_rows // BLK_ROWS) + b]
        span = slice(b * BLK_ROWS, (b + 1) * BLK_ROWS)
        value = full[:rank, span]
        for d in range(1, owners):
            value = jnp.where(owner == d, full[d * rank : (d + 1) * rank, span], value)
        out[:, span] = value


def steps_product(place, owner_of, parts, rows, deps):
    owners, (rank, features), row_count = len(parts), parts[0].shape, rows.shape[0]
    tile = min(256, row_count)
    return pl.pallas_call(
        behind(functools.partial(steps_product_kernel, owners, rank, tile), deps),
        grid=(row_count // tile,),
        in_specs=[ANY] * len(deps)
        + [SMEM] * 2
        + [pl.BlockSpec((rank, features), lambda i: (0, 0))] * owners
        + [pl.BlockSpec((tile, features), lambda i: (i, 0))],
        out_specs=[
            pl.BlockSpec((rank, tile), lambda i: (0, i)),
            pl.BlockSpec((owners * rank, features), lambda i: (0, 0)),
        ],
        out_shape=[
            jax.ShapeDtypeStruct((rank, row_count), jnp.float32),
            jax.ShapeDtypeStruct((owners * rank, features), jnp.bfloat16),
        ],
        compiler_params=params(),
        cost_estimate=cost(5),
        name="steps_product",
    )(*deps, place, owner_of, *parts, rows)


def halves_specs(owners, cores, rank, half):
    return [
        pl.BlockSpec((owners, None, rank, half), lambda *ids, h=h: (0, h, 0, 0))
        for h in range(cores)
    ]


def adapter_product(owner_of, adapters, rows, deps):
    (owners, cores, rank, half), (row_count, features) = adapters.shape, rows.shape
    tile = min(256, row_count)
    return pl.pallas_call(
        behind(functools.partial(product_kernel, owners, cores, rank, tile), deps),
        grid=(row_count // tile,),
        in_specs=[ANY] * len(deps)
        + [SMEM]
        + halves_specs(owners, cores, rank, half)
        + [pl.BlockSpec((tile, features), lambda i: (i, 0))],
        out_specs=pl.BlockSpec((rank, tile), lambda i: (0, i)),
        out_shape=jax.ShapeDtypeStruct((rank, row_count), jnp.float32),
        compiler_params=params(),
        cost_estimate=cost(5),
        name="adapter_product",
    )(*deps, owner_of, *[adapters] * cores, rows)


def encode(product, kind):
    if kind != jnp.int16:
        return product.astype(kind)
    top = jnp.maximum(jnp.max(jnp.abs(product), axis=1, keepdims=True), 1e-30)
    level = jnp.floor(jnp.log2(top) * LEVELS) + 2.0
    coded = jnp.round(product * (TOP_CODE * jnp.exp2(level * (-1.0 / LEVELS))))
    coded = jnp.clip(coded, -TOP_CODE, TOP_CODE).astype(jnp.int32).astype(jnp.int16)
    lanes = jnp.broadcast_to(level, (product.shape[0], LEVEL_LANES))
    return jnp.concatenate([coded, lanes.astype(jnp.int32).astype(jnp.int16)], axis=1)


def spread_rows(owners, rank, scale_in, owner_of, sums, wide):
    @pl.when(pl.program_id(0) == 0)
    def _():
        total = sums[0][...]
        for term in sums[1:]:
            total = total + term[...]
        value = (scale_in * total).astype(jnp.bfloat16)
        for b in range(value.shape[1] // BLK_ROWS):
            span = slice(b * BLK_ROWS, (b + 1) * BLK_ROWS)
            for d in range(owners):
                kept = jnp.where(owner_of[b] == d, value[:, span], jnp.zeros_like(value[:, span]))
                wide[d * rank : (d + 1) * rank, span] = kept


def steps_gradient_kernel(owners, rank, terms, scale_in, scale_out, place, owner_of, *refs):
    sums, rows, outs = refs[:terms], refs[terms], refs[terms + 1 : terms + 1 + owners]
    wide, coded = refs[-2:]
    spread_rows(owners, rank, scale_in, owner_of, sums, wide)
    product = scale_out * jnp.dot(wide[...], rows[...], preferred_element_type=jnp.float32)
    coded[...] = product.astype(coded.dtype)
    for d in range(owners):
        owner = lax.rem(place[0] - d + owners, owners)
        outs[d][...] = coded[pl.ds(pl.multiple_of(owner * rank, rank), rank), :]


def steps_gradients(place, owner_of, sums, rows, owners, half, scale_in, scale_out, deps):
    rank, row_count = sums[0].shape
    whole = pl.BlockSpec((rank, row_count), lambda h, place, owner_of: (0, 0))
    return pl.pallas_call(
        behind(
            functools.partial(
                steps_gradient_kernel, owners, rank, len(sums), scale_in, scale_out
            ),
            deps,
            2,
        ),
        grid_spec=pltpu.PrefetchScalarGridSpec(
            num_scalar_prefetch=2,
            grid=(2,),
            in_specs=[ANY] * len(deps)
            + [whole] * len(sums)
            + [
                pl.BlockSpec(
                    (row_count, half),
                    lambda h, place, owner_of: (0, jnp.where(h == 0, place[1], 1 - place[1])),
                )
            ],
            out_specs=[pl.BlockSpec((None, rank, half), lambda h, place, owner_of: (h, 0, 0))]
            * owners
            + [pl.BlockSpec((owners * rank, row_count), lambda h, place, owner_of: (0, 0))],
            scratch_shapes=[pltpu.VMEM((owners * rank, half), jnp.bfloat16)],
        ),
        out_shape=[jax.ShapeDtypeStruct((2, rank, half), jnp.bfloat16)] * owners
        + [jax.ShapeDtypeStruct((owners * rank, row_count), jnp.bfloat16)],
        compiler_params=params(),
        cost_estimate=cost(4),
        name="steps_gradients",
    )(place, owner_of, *deps, *sums, rows)


def collect_kernel(owners, *refs):
    for d in range(owners):
        refs[-1][d] = refs[d][...]


def collect(messages, deps):
    owners, (_, rank, half) = len(messages), messages[0].shape
    return pl.pallas_call(
        behind(functools.partial(collect_kernel, owners), deps),
        grid=(1,),
        in_specs=[ANY] * len(deps) + [pl.BlockSpec((None, rank, half), lambda i: (1, 0, 0))] * owners,
        out_specs=pl.BlockSpec((owners, rank, half), lambda i: (0, 0, 0)),
        out_shape=jax.ShapeDtypeStruct((owners, rank, half), messages[0].dtype),
        compiler_params=params(),
        cost_estimate=cost(1),
        name="collect",
    )(*deps, *messages)


def gradient_kernel(owners, rank, terms, scale_in, scale_out, owner_of, *refs):
    sums, (rows, out, wide) = refs[:terms], refs[terms:]
    spread_rows(owners, rank, scale_in, owner_of, sums, wide)
    product = scale_out * jnp.dot(wide[...], rows[...], preferred_element_type=jnp.float32)
    out[...] = encode(product, out.dtype).reshape(out.shape)


def gradients(owner_of, sums, rows, owners, half, scale_in, scale_out, kind, deps):
    rank, row_count = sums[0].shape
    cores = rows.shape[1] // half
    lanes = half + (LEVEL_LANES if kind == jnp.int16 else 0)
    whole = pl.BlockSpec((rank, row_count), lambda h: (0, 0))
    return pl.pallas_call(
        behind(
            functools.partial(gradient_kernel, owners, rank, len(sums), scale_in, scale_out), deps
        ),
        grid=(cores,),
        in_specs=[ANY] * len(deps)
        + [SMEM]
        + [whole] * len(sums)
        + [pl.BlockSpec((row_count, half), lambda h: (0, h))],
        out_specs=[
            pl.BlockSpec((owners, None, rank, lanes), lambda h: (0, h, 0, 0)),
            pl.BlockSpec((owners * rank, row_count), lambda h: (0, 0)),
        ],
        out_shape=[
            jax.ShapeDtypeStruct((owners, cores, rank, lanes), kind),
            jax.ShapeDtypeStruct((owners * rank, row_count), jnp.bfloat16),
        ],
        compiler_params=params(),
        cost_estimate=cost(4),
        name="gradients",
    )(*deps, owner_of, *sums, rows)


def share_kernel(spans, rows, weight, *outs):
    product = jnp.dot(rows[...], weight[...], preferred_element_type=jnp.float32)
    for out, (start, count) in zip(outs, spans):
        out[...] = product[start : start + count, :].astype(out.dtype)


def share(tokens, weight, piece, start, total, spans, width, deps):
    features = tokens.shape[1]
    tile = min(512, width)
    tiles = width // tile
    return pl.pallas_call(
        behind(functools.partial(share_kernel, spans), deps),
        grid=(tiles,),
        in_specs=[ANY] * len(deps)
        + [
            pl.BlockSpec((total, features), lambda j: (start // total, 0)),
            pl.BlockSpec((features, tile), lambda j: (0, piece * tiles + j)),
        ],
        out_specs=[pl.BlockSpec((count, tile), lambda j: (0, j)) for _, count in spans],
        out_shape=[jax.ShapeDtypeStruct((count, width), jnp.bfloat16) for _, count in spans],
        compiler_params=params(),
        cost_estimate=cost(4.0 * total / 256),
        name="share",
    )(*deps, tokens, weight)


def finish_kernel(flags, spans, mine_is_own, wide, adapters, *refs):
    arrays, out = refs[: len(flags)], refs[-1]
    step = pl.program_id(0)
    turned = wide[...].T
    half = adapters.shape[1] // 2
    for h in range(2):
        span = slice(h * half, (h + 1) * half)
        total = ADAPTER_SCALE * jnp.dot(
            turned, adapters[:, span], preferred_element_type=jnp.float32
        )
        for array, flag, (first, last) in zip(arrays, flags, spans):
            active = jnp.logical_and(step >= first, step < last)
            active = jnp.logical_and(active, mine_is_own[0] == flag)
            total = total + jnp.where(active, array[:, span].astype(jnp.float32), 0.0)
        out[:, span] = total.astype(out.dtype)


def finish(mine_is_own, wide, adapters, row_count, start, count, terms, previous, deps):
    stacked, width = adapters.shape
    tile = min(256, count)
    first = start // tile
    specs, spans = [], []
    for array, row, flag in terms:
        low, many = (row - start) // tile, array.shape[0] // tile

        def block_of(i, mine, low=low, many=many, flag=flag):
            return (jnp.where(mine[0] == flag, jnp.clip(i - low, 0, many - 1), 0), 0)

        specs.append(pl.BlockSpec((tile, width), block_of))
        spans.append((low, low + many))
    operands = [mine_is_own, *deps, wide, adapters]
    operands += [t[0] for t in terms]
    in_specs = (
        [ANY] * len(deps)
        + [
            pl.BlockSpec((stacked, tile), lambda i, mine: (0, first + i)),
            pl.BlockSpec((stacked, width), lambda i, mine: (0, 0)),
        ]
        + specs
    )
    aliases = {}
    if previous is not None:
        aliases = {len(operands): 0}
        operands.append(previous)
        in_specs.append(ANY)
    return pl.pallas_call(
        behind(functools.partial(finish_kernel, [t[2] for t in terms], spans), deps, 1),
        grid_spec=pltpu.PrefetchScalarGridSpec(
            num_scalar_prefetch=1,
            grid=(count // tile,),
            in_specs=in_specs,
            out_specs=pl.BlockSpec((tile, width), lambda i, mine: (first + i, 0)),
        ),
        out_shape=jax.ShapeDtypeStruct((row_count, width), jnp.bfloat16),
        input_output_aliases=aliases,
        compiler_params=params(),
        cost_estimate=cost(4),
        name="finish",
    )(*operands)


def adam_step(slots, used, corr, param, first, second, new_param, new_first, new_second, grads):
    for k in range(slots):
        grad = grads[k]
        one = BETA_ONE * first[k] + (1.0 - BETA_ONE) * grad
        two = BETA_TWO * second[k] + (1.0 - BETA_TWO) * grad * grad
        update = LEARN_RATE * (one / corr[k]) / (jnp.sqrt(two / corr[slots + k]) + ADAM_EPS)
        keep = used[k] == 1
        new_param[k] = jnp.where(keep, param[k] - update, param[k])
        new_first[k] = jnp.where(keep, one, first[k])
        new_second[k] = jnp.where(keep, two, second[k])


def coded_adam_kernel(devices, slots, place, pick, used, corr, param, first, second, *refs):
    messages, levels = refs[:2]
    grads = refs[-1]
    grads[...] = jnp.zeros_like(grads)
    for device in range(devices):
        k = pick[device]
        level = levels[device].astype(jnp.float32)[:, :1]
        scale = jnp.exp2(level * (1.0 / LEVELS)) * (1.0 / TOP_CODE)
        grads[k] = grads[k] + messages[device].astype(jnp.float32) * scale
    adam_step(slots, used, corr, param, first, second, *refs[-4:])


def steps_adam_kernel(owners, slots, place, pick, used, corr, param, first, second, *refs):
    near, far, grads = refs[:owners], refs[owners], refs[-1]
    grads[...] = jnp.zeros_like(grads)
    for d in range(owners):
        device = lax.rem(place[0] + d, owners) * 2
        k = pick[device + place[1]]
        grads[k] = grads[k] + near[d][...].astype(jnp.float32)
        k = pick[device + 1 - place[1]]
        grads[k] = grads[k] + far[d].astype(jnp.float32)
    adam_step(slots, used, corr, param, first, second, *refs[-4:])


def adam(kernel, tables, states, messages, message_specs, deps):
    slots, rank, half = states[0].shape
    tile = feature_tile(half)
    state = pl.BlockSpec((slots, rank, tile), lambda i: (0, 0, i))
    return pl.pallas_call(
        behind(kernel, deps),
        grid=(half // tile,),
        in_specs=[ANY] * len(deps) + [SMEM] * len(tables) + [state] * 3 + message_specs,
        out_specs=[state] * 3,
        out_shape=[dims(states[0])] * 3,
        scratch_shapes=[pltpu.VMEM((slots, rank, tile), jnp.float32)],
        compiler_params=params(),
        cost_estimate=cost(4),
        name="adam",
    )(*deps, *tables, *states, *messages)


def feature_tile(half):
    return min(256, half)


def coded_adam(tables, states, messages, deps):
    devices, rank, _ = messages.shape
    slots, _, half = states[0].shape
    specs = [
        pl.BlockSpec((devices, rank, feature_tile(half)), lambda i: (0, 0, i)),
        pl.BlockSpec((devices, rank, LEVEL_LANES), lambda i: (0, 0, half // LEVEL_LANES)),
    ]
    kernel = functools.partial(coded_adam_kernel, devices, slots)
    return adam(kernel, tables, states, [messages] * 2, specs, deps)


def steps_adam(tables, states, near, far, deps):
    owners, rank, half = far.shape
    tile = feature_tile(half)
    specs = [pl.BlockSpec((None, rank, tile), lambda i: (0, 0, i))] * owners
    specs.append(pl.BlockSpec((owners, rank, tile), lambda i: (0, 0, i)))
    kernel = functools.partial(steps_adam_kernel, owners, states[0].shape[0])
    return adam(kernel, tables, states, [*near, far], specs, deps)


def on_device(
    tokens,
    frozen_weight,
    cotangent,
    down_adapters,
    up_adapters,
    down_first_moment,
    up_first_moment,
    down_second_moment,
    up_second_moment,
    optimizer_steps,
    slot_of_tenant,
    tenant_of_block,
):
    row_count, din_local = tokens.shape
    width = cotangent.shape[1]
    block_count = row_count // BLK_ROWS
    owners = lax.axis_size("dp")
    cores = lax.axis_size("sub")
    columns = lax.axis_size("tensor")
    z = lax.axis_index("dp")
    s = lax.axis_index("sub")
    x = lax.axis_index("tensor")
    slots, half, rank = down_adapters.shape
    flip = lambda v: jnp.swapaxes(v, 1, 2)
    down_adapters, up_adapters = flip(down_adapters), flip(up_adapters)
    down_first_moment, up_first_moment = flip(down_first_moment), flip(up_first_moment)
    down_second_moment, up_second_moment = flip(down_second_moment), flip(up_second_moment)
    per_half = columns // cores
    place = jnp.stack([z, s]).astype(jnp.int32)

    devices = owners * cores

    def tables(deps):
        return pl.pallas_call(
            behind(functools.partial(tables_kernel, devices, cores, slots, block_count), deps),
            in_specs=[ANY] * len(deps) + [SMEM] * 3,
            out_specs=[SMEM] * 3,
            out_shape=[
                jax.ShapeDtypeStruct((devices,), jnp.int32),
                jax.ShapeDtypeStruct((block_count,), jnp.int32),
                jax.ShapeDtypeStruct((slots,), jnp.int32),
            ],
            cost_estimate=cost(2),
            name="tables",
        )(*deps, place, slot_of_tenant, tenant_of_block)

    steps = (optimizer_steps + 1).astype(jnp.float32)
    corr = jnp.concatenate(
        [
            1.0 - jnp.power(jnp.float32(BETA_ONE), steps),
            1.0 - jnp.power(jnp.float32(BETA_TWO), steps),
        ]
    )

    def pack(own, deps):
        return pl.pallas_call(
            behind(functools.partial(pack_kernel, devices), deps),
            in_specs=[ANY] * len(deps) + [SMEM, pl.BlockSpec(memory_space=pltpu.VMEM)],
            out_specs=pl.BlockSpec(memory_space=pltpu.VMEM),
            out_shape=jax.ShapeDtypeStruct((devices, rank, half), jnp.bfloat16),
            compiler_params=params(),
            cost_estimate=cost(1),
            name="pack",
        )(*deps, pick, own)

    def spread_out(messages):
        flat = messages.reshape((devices,) + messages.shape[-2:])
        return lax.all_to_all(flat, ("dp", "sub"), split_axis=0, concat_axis=0, tiled=True)

    def by_owner(arrived):
        return arrived.reshape(owners, cores, rank, half)

    def pack_wide(own, other, deps):
        return pl.pallas_call(
            behind(functools.partial(pack_wide_kernel, owners, cores), deps),
            in_specs=[ANY] * len(deps)
            + [SMEM] * 2
            + [pl.BlockSpec(memory_space=pltpu.VMEM)] * 2,
            out_specs=[pl.BlockSpec(memory_space=pltpu.VMEM)] * owners,
            out_shape=[jax.ShapeDtypeStruct((rank, cores * half), jnp.bfloat16)] * owners,
            compiler_params=params(),
            cost_estimate=cost(1),
            name="pack_wide",
        )(*deps, place, pick, own, other)

    def along(messages, sign):
        return [m if d == 0 else rotate(m, "dp", sign * d) for d, m in enumerate(messages)]

    def shares(rows, start, total, spans, deps):
        pieces = []
        for piece in range(per_half):
            pieces.append(share(rows, frozen_weight, piece, start, total, spans, width, deps))
            deps = [pieces[-1][0]]
        return [list(chunk) for chunk in zip(*pieces)]

    def piece_for(chunk, target):
        if per_half == 1:
            return chunk[0]
        out = chunk[0]
        for piece in range(1, per_half):
            out = jnp.where(lax.rem(target, per_half) == piece, chunk[piece], out)
        return out

    def send(chunk, cross):
        got = []
        for step in range(1, columns):
            pairs = []
            for t in range(columns):
                for c in range(cores):
                    target = (t + step) % columns
                    if target // per_half == c:
                        pairs.append((t * cores + c, target * cores + (c + cross) % cores))
            operand = piece_for(chunk, lax.rem(x + step, columns))
            got.append(lax.ppermute(operand, ("tensor", "sub"), pairs))
        return got

    def send_local(chunk):
        pairs = []
        for t in range(columns):
            c = t // per_half
            pairs.append((t * cores + c, t * cores + (c + 1) % cores))
        return lax.ppermute(piece_for(chunk, x), ("tensor", "sub"), pairs)

    def exchange(part):
        return [part] + [rotate(part, "tensor", step) for step in range(1, columns)]

    half_rows = row_count // 2
    one_half = [(0, half_rows)]
    both = one_half * 2
    up_other = rotate(up_adapters, "sub", 1)
    other_tokens = rotate(tokens, "sub", 1)
    pick, owner_of, used = tables([])
    down_packed = pack(down_adapters, [])
    down_arrived = by_owner(spread_out(down_packed))
    own_a, = shares(tokens, 0, half_rows, one_half, [down_packed])
    got_a = send(own_a, 0)
    up_packed = pack_wide(up_adapters, up_other, [own_a[-1]])
    own_b, = shares(tokens, half_rows, half_rows, one_half, [up_packed[0]])
    up_packed = tie(up_packed, [down_arrived, own_b[-1]])
    up_parts = along(up_packed, 1)

    down_part = adapter_product(owner_of, down_arrived, tokens, [up_packed[0], other_tokens])
    down_sums = exchange(down_part)
    own_b = tie(own_b, [down_part] + got_a)
    got_b = send(own_b, 0)
    cross_a, cross_a_near = shares(other_tokens, 0, half_rows, both, [own_b[-1]])
    *up_messages, down_wide = steps_gradients(
        place, owner_of, down_sums, cotangent, owners, half, 1.0, ADAPTER_SCALE, [cross_a[-1]]
    )
    up_messages = tie(up_messages, up_parts[1:])
    up_returned = along(up_messages, -1)
    back_part, up_cat = steps_product(place, owner_of, up_parts, cotangent, [up_messages[0]])
    back_sums = exchange(back_part)
    cross_a = tie(cross_a, [back_part] + got_b)
    late_a = send(cross_a, 1)
    cross_b, cross_b_near = shares(other_tokens, half_rows, half_rows, both, [cross_a[-1]])
    down_messages, back_wide = gradients(
        owner_of, back_sums, tokens, owners, half, ADAPTER_SCALE, 1.0, jnp.int16, [cross_b[-1]]
    )
    down_returned = spread_out(down_messages)
    collected = collect(up_returned, late_a + [down_messages])
    up_far = rotate(collected, "sub", 1)
    cross_b = tie(cross_b, [collected])
    late_b = send(cross_b, 1)
    cross_a_near = tie(cross_a_near, [cross_b[-1]])
    local_a = send_local(cross_a_near)
    cross_b_near = tie(cross_b_near, [local_a])
    local_b = send_local(cross_b_near)

    tables_in = [place, pick, used, corr]
    fresh_up, fresh_up_first, fresh_up_second = steps_adam(
        tables_in, [up_adapters, up_first_moment, up_second_moment], up_returned, up_far,
        [cross_a_near[-1]],
    )
    mine_is_own = (lax.div(x, per_half) == s).astype(jnp.int32).reshape(1)
    terms_a = [(piece_for(own_a, x), 0, 1), (local_a, 0, 0)]
    terms_a += [(g, 0, 1) for g in got_a] + [(g, 0, 0) for g in late_a]
    terms_b = [(piece_for(own_b, x), half_rows, 1), (local_b, half_rows, 0)]
    terms_b += [(g, half_rows, 1) for g in got_b] + [(g, half_rows, 0) for g in late_b]
    projected = finish(
        mine_is_own, down_wide, up_cat, row_count, 0, half_rows, terms_a, None, [fresh_up]
    )
    fresh_down, fresh_down_first, fresh_down_second = coded_adam(
        tables_in, [down_adapters, down_first_moment, down_second_moment], down_returned,
        [projected],
    )
    projected = finish(
        mine_is_own, down_wide, up_cat, row_count, half_rows, half_rows, terms_b, projected,
        [fresh_down],
    )
    return (
        projected,
        flip(fresh_down),
        flip(fresh_up),
        flip(fresh_down_first),
        flip(fresh_up_first),
        flip(fresh_down_second),
        flip(fresh_up_second),
    )


def solution(mesh):
    placed = (
        P(("groups", "dp", "sub"), "tensor"),
        P("tensor", "sub"),
        P(("groups", "dp", "sub"), "tensor"),
        P(("groups", "dp"), ("tensor", "sub"), None),
        P(("groups", "dp"), ("tensor", "sub"), None),
        P(("groups", "dp"), ("tensor", "sub"), None),
        P(("groups", "dp"), ("tensor", "sub"), None),
        P(("groups", "dp"), ("tensor", "sub"), None),
        P(("groups", "dp"), ("tensor", "sub"), None),
        P(("groups", "dp")),
        P("groups"),
        P("groups"),
    )
    return jax.shard_map(
        on_device,
        mesh=mesh,
        in_specs=placed,
        out_specs=(
            P(("groups", "dp", "sub"), "tensor"),
            P(("groups", "dp"), ("tensor", "sub"), None),
            P(("groups", "dp"), ("tensor", "sub"), None),
            P(("groups", "dp"), ("tensor", "sub"), None),
            P(("groups", "dp"), ("tensor", "sub"), None),
            P(("groups", "dp"), ("tensor", "sub"), None),
            P(("groups", "dp"), ("tensor", "sub"), None),
        ),
        check_vma=False,
    )
```

```python
import functools

import jax
import jax.numpy as jnp
from jax import lax
from jax.experimental import pallas as pl
from jax.experimental.pallas import tpu as pltpu
from jax.sharding import PartitionSpec as P

BLK_ROWS = 128


ADAPTER_SCALE = 2.0
BETA_ONE = 0.9
BETA_TWO = 0.999
LEARN_RATE = 0.01
ADAM_EPS = 1e-08

SMEM = pl.BlockSpec(memory_space=pltpu.SMEM)
VMEM_BYTES = 63_000_000
TOP_CODE = 32767.0
LEVELS = 64.0
LEVEL_LANES = 128
COST = 20.0


def params():
    return pltpu.CompilerParams(vmem_limit_bytes=VMEM_BYTES)


def cost(micros):
    flops = int(micros * 1_000_000_000 * COST)
    return pl.CostEstimate(flops=flops, bytes_accessed=1000, transcendentals=0)


def rotate(value, axis, shift):
    size = lax.axis_size(axis)
    return lax.ppermute(value, axis, [(i, (i + shift) % size) for i in range(size)])


ANY = pl.BlockSpec(memory_space=pl.ANY)


def behind(kernel, deps, scalars=0):
    return lambda *refs: kernel(*refs[:scalars], *refs[scalars + len(deps) :])


def tie_kernel(*refs):
    pass


def tie(values, deps):
    return pl.pallas_call(
        tie_kernel,
        in_specs=[ANY] * (len(values) + len(deps)),
        out_specs=[ANY] * len(values),
        out_shape=[dims(v) for v in values],
        input_output_aliases={k: k for k in range(len(values))},
        compiler_params=params(),
        cost_estimate=cost(100),
        name="tie",
    )(*values, *deps)


def dims(value):
    return jax.ShapeDtypeStruct(value.shape, value.dtype)


def tables_kernel(devices, cores, slots, block_count, place, slot_of, tenant_of, pick, owner_of, used):
    z, s = place[0], place[1]
    for k in range(slots):
        used[k] = 0

    def slot_at(device, b):
        return slot_of[tenant_of[device * block_count + b]]

    def per_device(device, carry):
        def per_block(b, found):
            local = slot_at(device, b) - z * slots
            mine = jnp.logical_and(local >= 0, local < slots)

            @pl.when(mine)
            def _():
                used[local] = 1

            return jnp.where(mine, local, found)

        pick[device] = lax.fori_loop(0, block_count, per_block, 0)
        return carry

    lax.fori_loop(0, devices, per_device, 0)
    for b in range(block_count):
        owner_of[b] = lax.div(slot_at(z * cores + s, b), slots)


def pack_kernel(devices, pick, own, out):
    for device in range(devices):
        out[device] = own[pick[device]].astype(jnp.bfloat16)


def pack_wide_kernel(owners, cores, place, pick, own, other, *outs):
    z, s = place[0], place[1]
    half = own.shape[2]
    for d in range(owners):
        k = pick[lax.rem(z + d, owners) * cores + s]
        near, far = own[k].astype(jnp.bfloat16), other[k].astype(jnp.bfloat16)
        outs[d][:, :half] = jnp.where(s == 0, near, far)
        outs[d][:, half:] = jnp.where(s == 0, far, near)


def product_kernel(owners, cores, rank, tile_rows, owner_of, *refs):
    halves, (rows, out) = refs[:cores], refs[cores:]
    step = pl.program_id(0)
    half = halves[0].shape[-1]
    full = 0.0
    for h in range(cores):
        full = full + lax.dot_general(
            halves[h][...].reshape(owners * rank, half),
            rows[:, h * half : (h + 1) * half],
            (((1,), (1,)), ((), ())),
            preferred_element_type=jnp.float32,
        )
    for b in range(tile_rows // BLK_ROWS):
        owner = owner_of[step * (tile_rows // BLK_ROWS) + b]
        span = slice(b * BLK_ROWS, (b + 1) * BLK_ROWS)
        value = full[:rank, span]
        for d in range(1, owners):
            value = jnp.where(owner == d, full[d * rank : (d + 1) * rank, span], value)
        out[:, span] = value


def steps_product_kernel(owners, rank, tile_rows, place, owner_of, *refs):
    parts, (rows, out, cat) = refs[:owners], refs[owners:]
    step = pl.program_id(0)

    @pl.when(step == 0)
    def _():
        for d in range(owners):
            owner = lax.rem(place[0] - d + owners, owners)
            cat[pl.ds(pl.multiple_of(owner * rank, rank), rank), :] = parts[d][...]

    full = lax.dot_general(
        cat[...], rows[...], (((1,), (1,)), ((), ())), preferred_element_type=jnp.float32
    )
    for b in range(tile_rows // BLK_ROWS):
        owner = owner_of[step * (tile_rows // BLK_ROWS) + b]
        span = slice(b * BLK_ROWS, (b + 1) * BLK_ROWS)
        value = full[:rank, span]
        for d in range(1, owners):
            value = jnp.where(owner == d, full[d * rank : (d + 1) * rank, span], value)
        out[:, span] = value


def steps_product(place, owner_of, parts, rows, deps):
    owners, (rank, features), row_count = len(parts), parts[0].shape, rows.shape[0]
    tile = min(256, row_count)
    return pl.pallas_call(
        behind(functools.partial(steps_product_kernel, owners, rank, tile), deps),
        grid=(row_count // tile,),
        in_specs=[ANY] * len(deps)
        + [SMEM] * 2
        + [pl.BlockSpec((rank, features), lambda i: (0, 0))] * owners
        + [pl.BlockSpec((tile, features), lambda i: (i, 0))],
        out_specs=[
            pl.BlockSpec((rank, tile), lambda i: (0, i)),
            pl.BlockSpec((owners * rank, features), lambda i: (0, 0)),
        ],
        out_shape=[
            jax.ShapeDtypeStruct((rank, row_count), jnp.float32),
            jax.ShapeDtypeStruct((owners * rank, features), jnp.bfloat16),
        ],
        compiler_params=params(),
        cost_estimate=cost(5),
        name="steps_product",
    )(*deps, place, owner_of, *parts, rows)


def halves_specs(owners, cores, rank, half):
    return [
        pl.BlockSpec((owners, None, rank, half), lambda *ids, h=h: (0, h, 0, 0))
        for h in range(cores)
    ]


def adapter_product(owner_of, adapters, rows, deps):
    (owners, cores, rank, half), (row_count, features) = adapters.shape, rows.shape
    tile = min(256, row_count)
    return pl.pallas_call(
        behind(functools.partial(product_kernel, owners, cores, rank, tile), deps),
        grid=(row_count // tile,),
        in_specs=[ANY] * len(deps)
        + [SMEM]
        + halves_specs(owners, cores, rank, half)
        + [pl.BlockSpec((tile, features), lambda i: (i, 0))],
        out_specs=pl.BlockSpec((rank, tile), lambda i: (0, i)),
        out_shape=jax.ShapeDtypeStruct((rank, row_count), jnp.float32),
        compiler_params=params(),
        cost_estimate=cost(5),
        name="adapter_product",
    )(*deps, owner_of, *[adapters] * cores, rows)


def encode(product, kind):
    if kind != jnp.int16:
        return product.astype(kind)
    top = jnp.maximum(jnp.max(jnp.abs(product), axis=1, keepdims=True), 1e-30)
    level = jnp.floor(jnp.log2(top) * LEVELS) + 2.0
    coded = jnp.round(product * (TOP_CODE * jnp.exp2(level * (-1.0 / LEVELS))))
    coded = jnp.clip(coded, -TOP_CODE, TOP_CODE).astype(jnp.int32).astype(jnp.int16)
    lanes = jnp.broadcast_to(level, (product.shape[0], LEVEL_LANES))
    return jnp.concatenate([coded, lanes.astype(jnp.int32).astype(jnp.int16)], axis=1)


def spread_rows(owners, rank, scale_in, owner_of, sums, wide):
    @pl.when(pl.program_id(0) == 0)
    def _():
        total = sums[0][...]
        for term in sums[1:]:
            total = total + term[...]
        value = (scale_in * total).astype(jnp.bfloat16)
        for b in range(value.shape[1] // BLK_ROWS):
            span = slice(b * BLK_ROWS, (b + 1) * BLK_ROWS)
            for d in range(owners):
                kept = jnp.where(owner_of[b] == d, value[:, span], jnp.zeros_like(value[:, span]))
                wide[d * rank : (d + 1) * rank, span] = kept


def steps_gradient_kernel(owners, rank, terms, scale_in, scale_out, place, owner_of, *refs):
    sums, rows, outs = refs[:terms], refs[terms], refs[terms + 1 : terms + 1 + owners]
    wide, coded = refs[-2:]
    spread_rows(owners, rank, scale_in, owner_of, sums, wide)
    product = scale_out * jnp.dot(wide[...], rows[...], preferred_element_type=jnp.float32)
    coded[...] = product.astype(coded.dtype)
    for d in range(owners):
        owner = lax.rem(place[0] - d + owners, owners)
        outs[d][...] = coded[pl.ds(pl.multiple_of(owner * rank, rank), rank), :]


def steps_gradients(place, owner_of, sums, rows, owners, half, scale_in, scale_out, deps):
    rank, row_count = sums[0].shape
    whole = pl.BlockSpec((rank, row_count), lambda h, place, owner_of: (0, 0))
    return pl.pallas_call(
        behind(
            functools.partial(
                steps_gradient_kernel, owners, rank, len(sums), scale_in, scale_out
            ),
            deps,
            2,
        ),
        grid_spec=pltpu.PrefetchScalarGridSpec(
            num_scalar_prefetch=2,
            grid=(2,),
            in_specs=[ANY] * len(deps)
            + [whole] * len(sums)
            + [
                pl.BlockSpec(
                    (row_count, half),
                    lambda h, place, owner_of: (0, jnp.where(h == 0, place[1], 1 - place[1])),
                )
            ],
            out_specs=[pl.BlockSpec((None, rank, half), lambda h, place, owner_of: (h, 0, 0))]
            * owners
            + [pl.BlockSpec((owners * rank, row_count), lambda h, place, owner_of: (0, 0))],
            scratch_shapes=[pltpu.VMEM((owners * rank, half), jnp.bfloat16)],
        ),
        out_shape=[jax.ShapeDtypeStruct((2, rank, half), jnp.bfloat16)] * owners
        + [jax.ShapeDtypeStruct((owners * rank, row_count), jnp.bfloat16)],
        compiler_params=params(),
        cost_estimate=cost(4),
        name="steps_gradients",
    )(place, owner_of, *deps, *sums, rows)


def collect_kernel(owners, *refs):
    for d in range(owners):
        refs[-1][d] = refs[d][...]


def collect(messages, deps):
    owners, (_, rank, half) = len(messages), messages[0].shape
    return pl.pallas_call(
        behind(functools.partial(collect_kernel, owners), deps),
        grid=(1,),
        in_specs=[ANY] * len(deps) + [pl.BlockSpec((None, rank, half), lambda i: (1, 0, 0))] * owners,
        out_specs=pl.BlockSpec((owners, rank, half), lambda i: (0, 0, 0)),
        out_shape=jax.ShapeDtypeStruct((owners, rank, half), messages[0].dtype),
        compiler_params=params(),
        cost_estimate=cost(1),
        name="collect",
    )(*deps, *messages)


def gradient_kernel(owners, rank, terms, scale_in, scale_out, owner_of, *refs):
    sums, (rows, out, wide) = refs[:terms], refs[terms:]
    spread_rows(owners, rank, scale_in, owner_of, sums, wide)
    product = scale_out * jnp.dot(wide[...], rows[...], preferred_element_type=jnp.float32)
    out[...] = encode(product, out.dtype).reshape(out.shape)


def gradients(owner_of, sums, rows, owners, half, scale_in, scale_out, kind, deps):
    rank, row_count = sums[0].shape
    cores = rows.shape[1] // half
    lanes = half + (LEVEL_LANES if kind == jnp.int16 else 0)
    whole = pl.BlockSpec((rank, row_count), lambda h: (0, 0))
    return pl.pallas_call(
        behind(
            functools.partial(gradient_kernel, owners, rank, len(sums), scale_in, scale_out), deps
        ),
        grid=(cores,),
        in_specs=[ANY] * len(deps)
        + [SMEM]
        + [whole] * len(sums)
        + [pl.BlockSpec((row_count, half), lambda h: (0, h))],
        out_specs=[
            pl.BlockSpec((owners, None, rank, lanes), lambda h: (0, h, 0, 0)),
            pl.BlockSpec((owners * rank, row_count), lambda h: (0, 0)),
        ],
        out_shape=[
            jax.ShapeDtypeStruct((owners, cores, rank, lanes), kind),
            jax.ShapeDtypeStruct((owners * rank, row_count), jnp.bfloat16),
        ],
        compiler_params=params(),
        cost_estimate=cost(4),
        name="gradients",
    )(*deps, owner_of, *sums, rows)


def share_kernel(spans, rows, weight, *outs):
    product = jnp.dot(rows[...], weight[...], preferred_element_type=jnp.float32)
    for out, (start, count) in zip(outs, spans):
        out[...] = product[start : start + count, :].astype(out.dtype)


def share(tokens, weight, piece, start, total, spans, width, deps):
    features = tokens.shape[1]
    tile = min(512, width)
    tiles = width // tile
    return pl.pallas_call(
        behind(functools.partial(share_kernel, spans), deps),
        grid=(tiles,),
        in_specs=[ANY] * len(deps)
        + [
            pl.BlockSpec((total, features), lambda j: (start // total, 0)),
            pl.BlockSpec((features, tile), lambda j: (0, piece * tiles + j)),
        ],
        out_specs=[pl.BlockSpec((count, tile), lambda j: (0, j)) for _, count in spans],
        out_shape=[jax.ShapeDtypeStruct((count, width), jnp.bfloat16) for _, count in spans],
        compiler_params=params(),
        cost_estimate=cost(4.0 * total / 256),
        name="share",
    )(*deps, tokens, weight)


def finish_kernel(flags, spans, mine_is_own, wide, adapters, *refs):
    arrays, out = refs[: len(flags)], refs[-1]
    step = pl.program_id(0)
    turned = wide[...].T
    half = adapters.shape[1] // 2
    for h in range(2):
        span = slice(h * half, (h + 1) * half)
        total = ADAPTER_SCALE * jnp.dot(
            turned, adapters[:, span], preferred_element_type=jnp.float32
        )
        for array, flag, (first, last) in zip(arrays, flags, spans):
            active = jnp.logical_and(step >= first, step < last)
            active = jnp.logical_and(active, mine_is_own[0] == flag)
            total = total + jnp.where(active, array[:, span].astype(jnp.float32), 0.0)
        out[:, span] = total.astype(out.dtype)


def finish(mine_is_own, wide, adapters, row_count, start, count, terms, previous, deps):
    stacked, width = adapters.shape
    tile = min(256, count)
    first = start // tile
    specs, spans = [], []
    for array, row, flag in terms:
        low, many = (row - start) // tile, array.shape[0] // tile

        def block_of(i, mine, low=low, many=many, flag=flag):
            return (jnp.where(mine[0] == flag, jnp.clip(i - low, 0, many - 1), 0), 0)

        specs.append(pl.BlockSpec((tile, width), block_of))
        spans.append((low, low + many))
    operands = [mine_is_own, *deps, wide, adapters]
    operands += [t[0] for t in terms]
    in_specs = (
        [ANY] * len(deps)
        + [
            pl.BlockSpec((stacked, tile), lambda i, mine: (0, first + i)),
            pl.BlockSpec((stacked, width), lambda i, mine: (0, 0)),
        ]
        + specs
    )
    aliases = {}
    if previous is not None:
        aliases = {len(operands): 0}
        operands.append(previous)
        in_specs.append(ANY)
    return pl.pallas_call(
        behind(functools.partial(finish_kernel, [t[2] for t in terms], spans), deps, 1),
        grid_spec=pltpu.PrefetchScalarGridSpec(
            num_scalar_prefetch=1,
            grid=(count // tile,),
            in_specs=in_specs,
            out_specs=pl.BlockSpec((tile, width), lambda i, mine: (first + i, 0)),
        ),
        out_shape=jax.ShapeDtypeStruct((row_count, width), jnp.bfloat16),
        input_output_aliases=aliases,
        compiler_params=params(),
        cost_estimate=cost(4),
        name="finish",
    )(*operands)


def adam_step(slots, used, corr, param, first, second, new_param, new_first, new_second, grads):
    for k in range(slots):
        grad = grads[k]
        one = BETA_ONE * first[k] + (1.0 - BETA_ONE) * grad
        two = BETA_TWO * second[k] + (1.0 - BETA_TWO) * grad * grad
        update = LEARN_RATE * (one / corr[k]) / (jnp.sqrt(two / corr[slots + k]) + ADAM_EPS)
        keep = used[k] == 1
        new_param[k] = jnp.where(keep, param[k] - update, param[k])
        new_first[k] = jnp.where(keep, one, first[k])
        new_second[k] = jnp.where(keep, two, second[k])


def coded_adam_kernel(devices, slots, place, pick, used, corr, param, first, second, *refs):
    messages, levels = refs[:2]
    grads = refs[-1]
    grads[...] = jnp.zeros_like(grads)
    for device in range(devices):
        k = pick[device]
        level = levels[device].astype(jnp.float32)[:, :1]
        scale = jnp.exp2(level * (1.0 / LEVELS)) * (1.0 / TOP_CODE)
        grads[k] = grads[k] + messages[device].astype(jnp.float32) * scale
    adam_step(slots, used, corr, param, first, second, *refs[-4:])


def steps_adam_kernel(owners, slots, place, pick, used, corr, param, first, second, *refs):
    near, far, grads = refs[:owners], refs[owners], refs[-1]
    grads[...] = jnp.zeros_like(grads)
    for d in range(owners):
        device = lax.rem(place[0] + d, owners) * 2
        k = pick[device + place[1]]
        grads[k] = grads[k] + near[d][...].astype(jnp.float32)
        k = pick[device + 1 - place[1]]
        grads[k] = grads[k] + far[d].astype(jnp.float32)
    adam_step(slots, used, corr, param, first, second, *refs[-4:])


def adam(kernel, tables, states, messages, message_specs, deps):
    slots, rank, half = states[0].shape
    tile = feature_tile(half)
    state = pl.BlockSpec((slots, rank, tile), lambda i: (0, 0, i))
    return pl.pallas_call(
        behind(kernel, deps),
        grid=(half // tile,),
        in_specs=[ANY] * len(deps) + [SMEM] * len(tables) + [state] * 3 + message_specs,
        out_specs=[state] * 3,
        out_shape=[dims(states[0])] * 3,
        scratch_shapes=[pltpu.VMEM((slots, rank, tile), jnp.float32)],
        compiler_params=params(),
        cost_estimate=cost(4),
        name="adam",
    )(*deps, *tables, *states, *messages)


def feature_tile(half):
    return min(256, half)


def coded_adam(tables, states, messages, deps):
    devices, rank, _ = messages.shape
    slots, _, half = states[0].shape
    specs = [
        pl.BlockSpec((devices, rank, feature_tile(half)), lambda i: (0, 0, i)),
        pl.BlockSpec((devices, rank, LEVEL_LANES), lambda i: (0, 0, half // LEVEL_LANES)),
    ]
    kernel = functools.partial(coded_adam_kernel, devices, slots)
    return adam(kernel, tables, states, [messages] * 2, specs, deps)


def steps_adam(tables, states, near, far, deps):
    owners, rank, half = far.shape
    tile = feature_tile(half)
    specs = [pl.BlockSpec((None, rank, tile), lambda i: (0, 0, i))] * owners
    specs.append(pl.BlockSpec((owners, rank, tile), lambda i: (0, 0, i)))
    kernel = functools.partial(steps_adam_kernel, owners, states[0].shape[0])
    return adam(kernel, tables, states, [*near, far], specs, deps)


def on_device(
    tokens,
    frozen_weight,
    cotangent,
    down_adapters,
    up_adapters,
    down_first_moment,
    up_first_moment,
    down_second_moment,
    up_second_moment,
    optimizer_steps,
    slot_of_tenant,
    tenant_of_block,
):
    row_count, din_local = tokens.shape
    width = cotangent.shape[1]
    block_count = row_count // BLK_ROWS
    owners = lax.axis_size("dp")
    cores = lax.axis_size("sub")
    columns = lax.axis_size("tensor")
    z = lax.axis_index("dp")
    s = lax.axis_index("sub")
    x = lax.axis_index("tensor")
    slots, half, rank = down_adapters.shape
    flip = lambda v: jnp.swapaxes(v, 1, 2)
    down_adapters, up_adapters = flip(down_adapters), flip(up_adapters)
    down_first_moment, up_first_moment = flip(down_first_moment), flip(up_first_moment)
    down_second_moment, up_second_moment = flip(down_second_moment), flip(up_second_moment)
    per_half = columns // cores
    place = jnp.stack([z, s]).astype(jnp.int32)

    devices = owners * cores

    def tables(deps):
        return pl.pallas_call(
            behind(functools.partial(tables_kernel, devices, cores, slots, block_count), deps),
            in_specs=[ANY] * len(deps) + [SMEM] * 3,
            out_specs=[SMEM] * 3,
            out_shape=[
                jax.ShapeDtypeStruct((devices,), jnp.int32),
                jax.ShapeDtypeStruct((block_count,), jnp.int32),
                jax.ShapeDtypeStruct((slots,), jnp.int32),
            ],
            compiler_params=params(),
            cost_estimate=cost(2),
            name="tables",
        )(*deps, place, slot_of_tenant, tenant_of_block)

    steps = (optimizer_steps + 1).astype(jnp.float32)
    corr = jnp.concatenate(
        [
            1.0 - jnp.power(jnp.float32(BETA_ONE), steps),
            1.0 - jnp.power(jnp.float32(BETA_TWO), steps),
        ]
    )

    def pack(own, deps):
        return pl.pallas_call(
            behind(functools.partial(pack_kernel, devices), deps),
            in_specs=[ANY] * len(deps) + [SMEM, pl.BlockSpec(memory_space=pltpu.VMEM)],
            out_specs=pl.BlockSpec(memory_space=pltpu.VMEM),
            out_shape=jax.ShapeDtypeStruct((devices, rank, half), jnp.bfloat16),
            compiler_params=params(),
            cost_estimate=cost(1),
            name="pack",
        )(*deps, pick, own)

    def spread_out(messages):
        flat = messages.reshape((devices,) + messages.shape[-2:])
        return lax.all_to_all(flat, ("dp", "sub"), split_axis=0, concat_axis=0, tiled=True)

    def by_owner(arrived):
        return arrived.reshape(owners, cores, rank, half)

    def pack_wide(own, other, deps):
        return pl.pallas_call(
            behind(functools.partial(pack_wide_kernel, owners, cores), deps),
            in_specs=[ANY] * len(deps)
            + [SMEM] * 2
            + [pl.BlockSpec(memory_space=pltpu.VMEM)] * 2,
            out_specs=[pl.BlockSpec(memory_space=pltpu.VMEM)] * owners,
            out_shape=[jax.ShapeDtypeStruct((rank, cores * half), jnp.bfloat16)] * owners,
            compiler_params=params(),
            cost_estimate=cost(1),
            name="pack_wide",
        )(*deps, place, pick, own, other)

    def along(messages, sign):
        return [m if d == 0 else rotate(m, "dp", sign * d) for d, m in enumerate(messages)]

    def shares(rows, start, total, spans, deps):
        pieces = []
        for piece in range(per_half):
            pieces.append(share(rows, frozen_weight, piece, start, total, spans, width, deps))
            deps = [pieces[-1][0]]
        return [list(chunk) for chunk in zip(*pieces)]

    def piece_for(chunk, target):
        if per_half == 1:
            return chunk[0]
        out = chunk[0]
        for piece in range(1, per_half):
            out = jnp.where(lax.rem(target, per_half) == piece, chunk[piece], out)
        return out

    def send(chunk, cross):
        got = []
        for step in range(1, columns):
            pairs = []
            for t in range(columns):
                for c in range(cores):
                    target = (t + step) % columns
                    if target // per_half == c:
                        pairs.append((t * cores + c, target * cores + (c + cross) % cores))
            operand = piece_for(chunk, lax.rem(x + step, columns))
            got.append(lax.ppermute(operand, ("tensor", "sub"), pairs))
        return got

    def send_local(chunk):
        pairs = []
        for t in range(columns):
            c = t // per_half
            pairs.append((t * cores + c, t * cores + (c + 1) % cores))
        return lax.ppermute(piece_for(chunk, x), ("tensor", "sub"), pairs)

    def exchange(part):
        return [part] + [rotate(part, "tensor", step) for step in range(1, columns)]

    half_rows = row_count // 2
    one_half = [(0, half_rows)]
    both = one_half * 2
    up_other = rotate(up_adapters, "sub", 1)
    other_tokens = rotate(tokens, "sub", 1)
    pick, owner_of, used = tables([])
    down_packed = pack(down_adapters, [])
    down_arrived = by_owner(spread_out(down_packed))
    own_a, = shares(tokens, 0, half_rows, one_half, [down_packed])
    got_a = send(own_a, 0)
    up_packed = pack_wide(up_adapters, up_other, [own_a[-1]])
    own_b, = shares(tokens, half_rows, half_rows, one_half, [up_packed[0]])
    up_packed = tie(up_packed, [down_arrived, own_b[-1]])
    up_parts = along(up_packed, 1)

    down_part = adapter_product(owner_of, down_arrived, tokens, [up_packed[0], other_tokens])
    down_sums = exchange(down_part)
    own_b = tie(own_b, [down_part] + got_a)
    got_b = send(own_b, 0)
    cross_a, cross_a_near = shares(other_tokens, 0, half_rows, both, [own_b[-1]])
    *up_messages, down_wide = steps_gradients(
        place, owner_of, down_sums, cotangent, owners, half, 1.0, ADAPTER_SCALE, [cross_a[-1]]
    )
    up_messages = tie(up_messages, up_parts[1:])
    up_returned = along(up_messages, -1)
    back_part, up_cat = steps_product(place, owner_of, up_parts, cotangent, [up_messages[0]])
    back_sums = exchange(back_part)
    cross_a = tie(cross_a, [back_part] + got_b)
    late_a = send(cross_a, 1)
    cross_b, cross_b_near = shares(other_tokens, half_rows, half_rows, both, [cross_a[-1]])
    down_messages, back_wide = gradients(
        owner_of, back_sums, tokens, owners, half, ADAPTER_SCALE, 1.0, jnp.int16, [cross_b[-1]]
    )
    down_returned = spread_out(down_messages)
    cross_b = tie(cross_b, [down_messages])
    late_b = send(cross_b, 1)
    collected = collect(up_returned, late_a + [cross_b[-1]])
    up_far = rotate(collected, "sub", 1)
    cross_a_near = tie(cross_a_near, [collected])
    local_a = send_local(cross_a_near)
    cross_b_near = tie(cross_b_near, [local_a])
    local_b = send_local(cross_b_near)

    tables_in = [place, pick, used, corr]
    fresh_up, fresh_up_first, fresh_up_second = steps_adam(
        tables_in, [up_adapters, up_first_moment, up_second_moment], up_returned, up_far,
        [cross_a_near[-1]],
    )
    mine_is_own = (lax.div(x, per_half) == s).astype(jnp.int32).reshape(1)
    terms_a = [(piece_for(own_a, x), 0, 1), (local_a, 0, 0)]
    terms_a += [(g, 0, 1) for g in got_a] + [(g, 0, 0) for g in late_a]
    terms_b = [(piece_for(own_b, x), half_rows, 1), (local_b, half_rows, 0)]
    terms_b += [(g, half_rows, 1) for g in got_b] + [(g, half_rows, 0) for g in late_b]
    projected = finish(
        mine_is_own, down_wide, up_cat, row_count, 0, half_rows, terms_a, None, [fresh_up]
    )
    fresh_down, fresh_down_first, fresh_down_second = coded_adam(
        tables_in, [down_adapters, down_first_moment, down_second_moment], down_returned,
        [projected],
    )
    projected = finish(
        mine_is_own, down_wide, up_cat, row_count, half_rows, half_rows, terms_b, projected,
        [fresh_down],
    )
    return (
        projected,
        flip(fresh_down),
        flip(fresh_up),
        flip(fresh_down_first),
        flip(fresh_up_first),
        flip(fresh_down_second),
        flip(fresh_up_second),
    )


def solution(mesh):
    placed = (
        P(("groups", "dp", "sub"), "tensor"),
        P("tensor", "sub"),
        P(("groups", "dp", "sub"), "tensor"),
        P(("groups", "dp"), ("tensor", "sub"), None),
        P(("groups", "dp"), ("tensor", "sub"), None),
        P(("groups", "dp"), ("tensor", "sub"), None),
        P(("groups", "dp"), ("tensor", "sub"), None),
        P(("groups", "dp"), ("tensor", "sub"), None),
        P(("groups", "dp"), ("tensor", "sub"), None),
        P(("groups", "dp")),
        P("groups"),
        P("groups"),
    )
    return jax.shard_map(
        on_device,
        mesh=mesh,
        in_specs=placed,
        out_specs=(
            P(("groups", "dp", "sub"), "tensor"),
            P(("groups", "dp"), ("tensor", "sub"), None),
            P(("groups", "dp"), ("tensor", "sub"), None),
            P(("groups", "dp"), ("tensor", "sub"), None),
            P(("groups", "dp"), ("tensor", "sub"), None),
            P(("groups", "dp"), ("tensor", "sub"), None),
            P(("groups", "dp"), ("tensor", "sub"), None),
        ),
        check_vma=False,
    )
```

```python
import functools

import jax
import jax.numpy as jnp
from jax import lax
from jax.experimental import pallas as pl
from jax.experimental.pallas import tpu as pltpu
from jax.sharding import PartitionSpec as P

BLK_ROWS = 128


ADAPTER_SCALE = 2.0
BETA_ONE = 0.9
BETA_TWO = 0.999
LEARN_RATE = 0.01
ADAM_EPS = 1e-08

SMEM = pl.BlockSpec(memory_space=pltpu.SMEM)
VMEM_BYTES = 63_000_000
TOP_CODE = 32767.0
LEVELS = 64.0
LEVEL_LANES = 128
COST = 20.0


def params():
    return pltpu.CompilerParams(vmem_limit_bytes=VMEM_BYTES)


def cost(micros):
    flops = int(micros * 1_000_000_000 * COST)
    return pl.CostEstimate(flops=flops, bytes_accessed=1000, transcendentals=0)


def rotate(value, axis, shift):
    size = lax.axis_size(axis)
    return lax.ppermute(value, axis, [(i, (i + shift) % size) for i in range(size)])


ANY = pl.BlockSpec(memory_space=pl.ANY)


def behind(kernel, deps, scalars=0):
    return lambda *refs: kernel(*refs[:scalars], *refs[scalars + len(deps) :])


def tie_kernel(*refs):
    pass


def tie(values, deps):
    return pl.pallas_call(
        tie_kernel,
        in_specs=[ANY] * (len(values) + len(deps)),
        out_specs=[ANY] * len(values),
        out_shape=[dims(v) for v in values],
        input_output_aliases={k: k for k in range(len(values))},
        compiler_params=params(),
        cost_estimate=cost(100),
        name="tie",
    )(*values, *deps)


def dims(value):
    return jax.ShapeDtypeStruct(value.shape, value.dtype)


def tables_kernel(devices, cores, slots, block_count, place, slot_of, tenant_of, pick, owner_of, used):
    z, s = place[0], place[1]
    for k in range(slots):
        used[k] = 0

    def slot_at(device, b):
        return slot_of[tenant_of[device * block_count + b]]

    def per_device(device, carry):
        def per_block(b, found):
            local = slot_at(device, b) - z * slots
            mine = jnp.logical_and(local >= 0, local < slots)

            @pl.when(mine)
            def _():
                used[local] = 1

            return jnp.where(mine, local, found)

        pick[device] = lax.fori_loop(0, block_count, per_block, 0)
        return carry

    lax.fori_loop(0, devices, per_device, 0)
    for b in range(block_count):
        owner_of[b] = lax.div(slot_at(z * cores + s, b), slots)


def pack_kernel(devices, pick, own, out):
    for device in range(devices):
        out[device] = own[pick[device]].astype(jnp.bfloat16)


def pack_wide_kernel(owners, cores, place, pick, own, other, *outs):
    z, s = place[0], place[1]
    half = own.shape[2]
    for d in range(owners):
        k = pick[lax.rem(z + d, owners) * cores + s]
        near, far = own[k].astype(jnp.bfloat16), other[k].astype(jnp.bfloat16)
        outs[d][:, :half] = jnp.where(s == 0, near, far)
        outs[d][:, half:] = jnp.where(s == 0, far, near)


def product_kernel(owners, cores, rank, tile_rows, owner_of, *refs):
    halves, (rows, out) = refs[:cores], refs[cores:]
    step = pl.program_id(0)
    half = halves[0].shape[-1]
    full = 0.0
    for h in range(cores):
        full = full + lax.dot_general(
            halves[h][...].reshape(owners * rank, half),
            rows[:, h * half : (h + 1) * half],
            (((1,), (1,)), ((), ())),
            preferred_element_type=jnp.float32,
        )
    for b in range(tile_rows // BLK_ROWS):
        owner = owner_of[step * (tile_rows // BLK_ROWS) + b]
        span = slice(b * BLK_ROWS, (b + 1) * BLK_ROWS)
        value = full[:rank, span]
        for d in range(1, owners):
            value = jnp.where(owner == d, full[d * rank : (d + 1) * rank, span], value)
        out[:, span] = value


def steps_product_kernel(owners, rank, tile_rows, place, owner_of, *refs):
    parts, (rows, out, cat) = refs[:owners], refs[owners:]
    step = pl.program_id(0)

    @pl.when(step == 0)
    def _():
        for d in range(owners):
            owner = lax.rem(place[0] - d + owners, owners)
            cat[pl.ds(pl.multiple_of(owner * rank, rank), rank), :] = parts[d][...]

    full = lax.dot_general(
        cat[...], rows[...], (((1,), (1,)), ((), ())), preferred_element_type=jnp.float32
    )
    for b in range(tile_rows // BLK_ROWS):
        owner = owner_of[step * (tile_rows // BLK_ROWS) + b]
        span = slice(b * BLK_ROWS, (b + 1) * BLK_ROWS)
        value = full[:rank, span]
        for d in range(1, owners):
            value = jnp.where(owner == d, full[d * rank : (d + 1) * rank, span], value)
        out[:, span] = value


def steps_product(place, owner_of, parts, rows, deps):
    owners, (rank, features), row_count = len(parts), parts[0].shape, rows.shape[0]
    tile = min(256, row_count)
    return pl.pallas_call(
        behind(functools.partial(steps_product_kernel, owners, rank, tile), deps),
        grid=(row_count // tile,),
        in_specs=[ANY] * len(deps)
        + [SMEM] * 2
        + [pl.BlockSpec((rank, features), lambda i: (0, 0))] * owners
        + [pl.BlockSpec((tile, features), lambda i: (i, 0))],
        out_specs=[
            pl.BlockSpec((rank, tile), lambda i: (0, i)),
            pl.BlockSpec((owners * rank, features), lambda i: (0, 0)),
        ],
        out_shape=[
            jax.ShapeDtypeStruct((rank, row_count), jnp.float32),
            jax.ShapeDtypeStruct((owners * rank, features), jnp.bfloat16),
        ],
        compiler_params=params(),
        cost_estimate=cost(5),
        name="steps_product",
    )(*deps, place, owner_of, *parts, rows)


def halves_specs(owners, cores, rank, half):
    return [
        pl.BlockSpec((owners, None, rank, half), lambda *ids, h=h: (0, h, 0, 0))
        for h in range(cores)
    ]


def adapter_product(owner_of, adapters, rows, deps):
    (owners, cores, rank, half), (row_count, features) = adapters.shape, rows.shape
    tile = min(256, row_count)
    return pl.pallas_call(
        behind(functools.partial(product_kernel, owners, cores, rank, tile), deps),
        grid=(row_count // tile,),
        in_specs=[ANY] * len(deps)
        + [SMEM]
        + halves_specs(owners, cores, rank, half)
        + [pl.BlockSpec((tile, features), lambda i: (i, 0))],
        out_specs=pl.BlockSpec((rank, tile), lambda i: (0, i)),
        out_shape=jax.ShapeDtypeStruct((rank, row_count), jnp.float32),
        compiler_params=params(),
        cost_estimate=cost(5),
        name="adapter_product",
    )(*deps, owner_of, *[adapters] * cores, rows)


def encode(product, kind):
    if kind != jnp.int16:
        return product.astype(kind)
    top = jnp.maximum(jnp.max(jnp.abs(product), axis=1, keepdims=True), 1e-30)
    level = jnp.floor(jnp.log2(top) * LEVELS) + 2.0
    coded = jnp.round(product * (TOP_CODE * jnp.exp2(level * (-1.0 / LEVELS))))
    coded = jnp.clip(coded, -TOP_CODE, TOP_CODE).astype(jnp.int32).astype(jnp.int16)
    lanes = jnp.broadcast_to(level, (product.shape[0], LEVEL_LANES))
    return jnp.concatenate([coded, lanes.astype(jnp.int32).astype(jnp.int16)], axis=1)


def spread_rows(owners, rank, scale_in, owner_of, sums, wide):
    @pl.when(pl.program_id(0) == 0)
    def _():
        total = sums[0][...]
        for term in sums[1:]:
            total = total + term[...]
        value = (scale_in * total).astype(jnp.bfloat16)
        for b in range(value.shape[1] // BLK_ROWS):
            span = slice(b * BLK_ROWS, (b + 1) * BLK_ROWS)
            for d in range(owners):
                kept = jnp.where(owner_of[b] == d, value[:, span], jnp.zeros_like(value[:, span]))
                wide[d * rank : (d + 1) * rank, span] = kept


def steps_gradient_kernel(owners, rank, terms, scale_in, scale_out, place, owner_of, *refs):
    sums, rows, outs = refs[:terms], refs[terms], refs[terms + 1 : terms + 1 + owners]
    wide, coded = refs[-2:]
    spread_rows(owners, rank, scale_in, owner_of, sums, wide)
    product = scale_out * jnp.dot(wide[...], rows[...], preferred_element_type=jnp.float32)
    coded[...] = product.astype(coded.dtype)
    for d in range(owners):
        owner = lax.rem(place[0] - d + owners, owners)
        outs[d][...] = coded[pl.ds(pl.multiple_of(owner * rank, rank), rank), :]


def steps_gradients(place, owner_of, sums, rows, owners, half, scale_in, scale_out, deps):
    rank, row_count = sums[0].shape
    whole = pl.BlockSpec((rank, row_count), lambda h, place, owner_of: (0, 0))
    return pl.pallas_call(
        behind(
            functools.partial(
                steps_gradient_kernel, owners, rank, len(sums), scale_in, scale_out
            ),
            deps,
            2,
        ),
        grid_spec=pltpu.PrefetchScalarGridSpec(
            num_scalar_prefetch=2,
            grid=(2,),
            in_specs=[ANY] * len(deps)
            + [whole] * len(sums)
            + [
                pl.BlockSpec(
                    (row_count, half),
                    lambda h, place, owner_of: (0, jnp.where(h == 0, place[1], 1 - place[1])),
                )
            ],
            out_specs=[pl.BlockSpec((None, rank, half), lambda h, place, owner_of: (h, 0, 0))]
            * owners
            + [pl.BlockSpec((owners * rank, row_count), lambda h, place, owner_of: (0, 0))],
            scratch_shapes=[pltpu.VMEM((owners * rank, half), jnp.bfloat16)],
        ),
        out_shape=[jax.ShapeDtypeStruct((2, rank, half), jnp.bfloat16)] * owners
        + [jax.ShapeDtypeStruct((owners * rank, row_count), jnp.bfloat16)],
        compiler_params=params(),
        cost_estimate=cost(4),
        name="steps_gradients",
    )(place, owner_of, *deps, *sums, rows)


def collect_kernel(owners, *refs):
    for d in range(owners):
        refs[-1][d] = refs[d][...]


def collect(messages, deps):
    owners, (_, rank, half) = len(messages), messages[0].shape
    return pl.pallas_call(
        behind(functools.partial(collect_kernel, owners), deps),
        grid=(1,),
        in_specs=[ANY] * len(deps) + [pl.BlockSpec((None, rank, half), lambda i: (1, 0, 0))] * owners,
        out_specs=pl.BlockSpec((owners, rank, half), lambda i: (0, 0, 0)),
        out_shape=jax.ShapeDtypeStruct((owners, rank, half), messages[0].dtype),
        compiler_params=params(),
        cost_estimate=cost(1),
        name="collect",
    )(*deps, *messages)


def gradient_kernel(owners, rank, terms, scale_in, scale_out, owner_of, *refs):
    sums, (rows, out, wide) = refs[:terms], refs[terms:]
    spread_rows(owners, rank, scale_in, owner_of, sums, wide)
    product = scale_out * jnp.dot(wide[...], rows[...], preferred_element_type=jnp.float32)
    out[...] = encode(product, out.dtype).reshape(out.shape)


def gradients(owner_of, sums, rows, owners, half, scale_in, scale_out, kind, deps):
    rank, row_count = sums[0].shape
    cores = rows.shape[1] // half
    lanes = half + (LEVEL_LANES if kind == jnp.int16 else 0)
    whole = pl.BlockSpec((rank, row_count), lambda h: (0, 0))
    return pl.pallas_call(
        behind(
            functools.partial(gradient_kernel, owners, rank, len(sums), scale_in, scale_out), deps
        ),
        grid=(cores,),
        in_specs=[ANY] * len(deps)
        + [SMEM]
        + [whole] * len(sums)
        + [pl.BlockSpec((row_count, half), lambda h: (0, h))],
        out_specs=[
            pl.BlockSpec((owners, None, rank, lanes), lambda h: (0, h, 0, 0)),
            pl.BlockSpec((owners * rank, row_count), lambda h: (0, 0)),
        ],
        out_shape=[
            jax.ShapeDtypeStruct((owners, cores, rank, lanes), kind),
            jax.ShapeDtypeStruct((owners * rank, row_count), jnp.bfloat16),
        ],
        compiler_params=params(),
        cost_estimate=cost(4),
        name="gradients",
    )(*deps, owner_of, *sums, rows)


def share_kernel(spans, rows, weight, *outs):
    product = jnp.dot(rows[...], weight[...], preferred_element_type=jnp.float32)
    for out, (start, count) in zip(outs, spans):
        out[...] = product[start : start + count, :].astype(out.dtype)


def share(tokens, weight, piece, start, total, spans, width, deps):
    features = tokens.shape[1]
    tile = min(512, width)
    tiles = width // tile
    return pl.pallas_call(
        behind(functools.partial(share_kernel, spans), deps),
        grid=(tiles,),
        in_specs=[ANY] * len(deps)
        + [
            pl.BlockSpec((total, features), lambda j: (start // total, 0)),
            pl.BlockSpec((features, tile), lambda j: (0, piece * tiles + j)),
        ],
        out_specs=[pl.BlockSpec((count, tile), lambda j: (0, j)) for _, count in spans],
        out_shape=[jax.ShapeDtypeStruct((count, width), jnp.bfloat16) for _, count in spans],
        compiler_params=params(),
        cost_estimate=cost(4.0 * total / 256),
        name="share",
    )(*deps, tokens, weight)


def finish_kernel(flags, spans, mine_is_own, wide, adapters, *refs):
    arrays, out = refs[: len(flags)], refs[-1]
    step = pl.program_id(0)
    turned = wide[...].T
    half = adapters.shape[1] // 2
    for h in range(2):
        span = slice(h * half, (h + 1) * half)
        total = ADAPTER_SCALE * jnp.dot(
            turned, adapters[:, span], preferred_element_type=jnp.float32
        )
        for array, flag, (first, last) in zip(arrays, flags, spans):
            active = jnp.logical_and(step >= first, step < last)
            active = jnp.logical_and(active, mine_is_own[0] == flag)
            total = total + jnp.where(active, array[:, span].astype(jnp.float32), 0.0)
        out[:, span] = total.astype(out.dtype)


def finish(mine_is_own, wide, adapters, row_count, start, count, terms, previous, deps):
    stacked, width = adapters.shape
    tile = min(256, count)
    first = start // tile
    specs, spans = [], []
    for array, row, flag in terms:
        low, many = (row - start) // tile, array.shape[0] // tile

        def block_of(i, mine, low=low, many=many, flag=flag):
            return (jnp.where(mine[0] == flag, jnp.clip(i - low, 0, many - 1), 0), 0)

        specs.append(pl.BlockSpec((tile, width), block_of))
        spans.append((low, low + many))
    operands = [mine_is_own, *deps, wide, adapters]
    operands += [t[0] for t in terms]
    in_specs = (
        [ANY] * len(deps)
        + [
            pl.BlockSpec((stacked, tile), lambda i, mine: (0, first + i)),
            pl.BlockSpec((stacked, width), lambda i, mine: (0, 0)),
        ]
        + specs
    )
    aliases = {}
    if previous is not None:
        aliases = {len(operands): 0}
        operands.append(previous)
        in_specs.append(ANY)
    return pl.pallas_call(
        behind(functools.partial(finish_kernel, [t[2] for t in terms], spans), deps, 1),
        grid_spec=pltpu.PrefetchScalarGridSpec(
            num_scalar_prefetch=1,
            grid=(count // tile,),
            in_specs=in_specs,
            out_specs=pl.BlockSpec((tile, width), lambda i, mine: (first + i, 0)),
        ),
        out_shape=jax.ShapeDtypeStruct((row_count, width), jnp.bfloat16),
        input_output_aliases=aliases,
        compiler_params=params(),
        cost_estimate=cost(4),
        name="finish",
    )(*operands)


def adam_step(slots, used, corr, param, first, second, new_param, new_first, new_second, grads):
    for k in range(slots):
        grad = grads[k]
        one = BETA_ONE * first[k] + (1.0 - BETA_ONE) * grad
        two = BETA_TWO * second[k] + (1.0 - BETA_TWO) * grad * grad
        update = LEARN_RATE * (one / corr[k]) / (jnp.sqrt(two / corr[slots + k]) + ADAM_EPS)
        keep = used[k] == 1
        new_param[k] = jnp.where(keep, param[k] - update, param[k])
        new_first[k] = jnp.where(keep, one, first[k])
        new_second[k] = jnp.where(keep, two, second[k])


def coded_adam_kernel(devices, slots, place, pick, used, corr, param, first, second, *refs):
    messages, levels = refs[:2]
    grads = refs[-1]
    grads[...] = jnp.zeros_like(grads)
    for device in range(devices):
        k = pick[device]
        level = levels[device].astype(jnp.float32)[:, :1]
        scale = jnp.exp2(level * (1.0 / LEVELS)) * (1.0 / TOP_CODE)
        grads[k] = grads[k] + messages[device].astype(jnp.float32) * scale
    adam_step(slots, used, corr, param, first, second, *refs[-4:])


def steps_adam_kernel(owners, slots, place, pick, used, corr, param, first, second, *refs):
    near, far, grads = refs[:owners], refs[owners], refs[-1]
    grads[...] = jnp.zeros_like(grads)
    for d in range(owners):
        device = lax.rem(place[0] + d, owners) * 2
        k = pick[device + place[1]]
        grads[k] = grads[k] + near[d][...].astype(jnp.float32)
        k = pick[device + 1 - place[1]]
        grads[k] = grads[k] + far[d].astype(jnp.float32)
    adam_step(slots, used, corr, param, first, second, *refs[-4:])


def adam(kernel, tables, states, messages, message_specs, deps):
    slots, rank, half = states[0].shape
    tile = feature_tile(half)
    state = pl.BlockSpec((slots, rank, tile), lambda i: (0, 0, i))
    return pl.pallas_call(
        behind(kernel, deps),
        grid=(half // tile,),
        in_specs=[ANY] * len(deps) + [SMEM] * len(tables) + [state] * 3 + message_specs,
        out_specs=[state] * 3,
        out_shape=[dims(states[0])] * 3,
        scratch_shapes=[pltpu.VMEM((slots, rank, tile), jnp.float32)],
        compiler_params=params(),
        cost_estimate=cost(4),
        name="adam",
    )(*deps, *tables, *states, *messages)


def feature_tile(half):
    return min(256, half)


def coded_adam(tables, states, messages, deps):
    devices, rank, _ = messages.shape
    slots, _, half = states[0].shape
    specs = [
        pl.BlockSpec((devices, rank, feature_tile(half)), lambda i: (0, 0, i)),
        pl.BlockSpec((devices, rank, LEVEL_LANES), lambda i: (0, 0, half // LEVEL_LANES)),
    ]
    kernel = functools.partial(coded_adam_kernel, devices, slots)
    return adam(kernel, tables, states, [messages] * 2, specs, deps)


def steps_adam(tables, states, near, far, deps):
    owners, rank, half = far.shape
    tile = feature_tile(half)
    specs = [pl.BlockSpec((None, rank, tile), lambda i: (0, 0, i))] * owners
    specs.append(pl.BlockSpec((owners, rank, tile), lambda i: (0, 0, i)))
    kernel = functools.partial(steps_adam_kernel, owners, states[0].shape[0])
    return adam(kernel, tables, states, [*near, far], specs, deps)


def on_device(
    tokens,
    frozen_weight,
    cotangent,
    down_adapters,
    up_adapters,
    down_first_moment,
    up_first_moment,
    down_second_moment,
    up_second_moment,
    optimizer_steps,
    slot_of_tenant,
    tenant_of_block,
):
    row_count, din_local = tokens.shape
    width = cotangent.shape[1]
    block_count = row_count // BLK_ROWS
    owners = lax.axis_size("dp")
    cores = lax.axis_size("sub")
    columns = lax.axis_size("tensor")
    z = lax.axis_index("dp")
    s = lax.axis_index("sub")
    x = lax.axis_index("tensor")
    slots, half, rank = down_adapters.shape
    flip = lambda v: jnp.swapaxes(v, 1, 2)
    down_adapters, up_adapters = flip(down_adapters), flip(up_adapters)
    down_first_moment, up_first_moment = flip(down_first_moment), flip(up_first_moment)
    down_second_moment, up_second_moment = flip(down_second_moment), flip(up_second_moment)
    per_half = columns // cores
    place = jnp.stack([z, s]).astype(jnp.int32)

    devices = owners * cores

    def tables(deps):
        return pl.pallas_call(
            behind(functools.partial(tables_kernel, devices, cores, slots, block_count), deps),
            in_specs=[ANY] * len(deps) + [SMEM] * 3,
            out_specs=[SMEM] * 3,
            out_shape=[
                jax.ShapeDtypeStruct((devices,), jnp.int32),
                jax.ShapeDtypeStruct((block_count,), jnp.int32),
                jax.ShapeDtypeStruct((slots,), jnp.int32),
            ],
            compiler_params=params(),
            cost_estimate=cost(2),
            name="tables",
        )(*deps, place, slot_of_tenant, tenant_of_block)

    steps = (optimizer_steps + 1).astype(jnp.float32)
    corr = jnp.concatenate(
        [
            1.0 - jnp.power(jnp.float32(BETA_ONE), steps),
            1.0 - jnp.power(jnp.float32(BETA_TWO), steps),
        ]
    )

    def pack(own, deps):
        return pl.pallas_call(
            behind(functools.partial(pack_kernel, devices), deps),
            in_specs=[ANY] * len(deps) + [SMEM, pl.BlockSpec(memory_space=pltpu.VMEM)],
            out_specs=pl.BlockSpec(memory_space=pltpu.VMEM),
            out_shape=jax.ShapeDtypeStruct((devices, rank, half), jnp.bfloat16),
            compiler_params=params(),
            cost_estimate=cost(1),
            name="pack",
        )(*deps, pick, own)

    def spread_out(messages):
        flat = messages.reshape((devices,) + messages.shape[-2:])
        return lax.all_to_all(flat, ("dp", "sub"), split_axis=0, concat_axis=0, tiled=True)

    def by_owner(arrived):
        return arrived.reshape(owners, cores, rank, half)

    def pack_wide(own, other, deps):
        return pl.pallas_call(
            behind(functools.partial(pack_wide_kernel, owners, cores), deps),
            in_specs=[ANY] * len(deps)
            + [SMEM] * 2
            + [pl.BlockSpec(memory_space=pltpu.VMEM)] * 2,
            out_specs=[pl.BlockSpec(memory_space=pltpu.VMEM)] * owners,
            out_shape=[jax.ShapeDtypeStruct((rank, cores * half), jnp.bfloat16)] * owners,
            compiler_params=params(),
            cost_estimate=cost(1),
            name="pack_wide",
        )(*deps, place, pick, own, other)

    def along(messages, sign):
        return [m if d == 0 else rotate(m, "dp", sign * d) for d, m in enumerate(messages)]

    def shares(rows, start, total, spans, deps):
        pieces = []
        for piece in range(per_half):
            pieces.append(share(rows, frozen_weight, piece, start, total, spans, width, deps))
            deps = [pieces[-1][0]]
        return [list(chunk) for chunk in zip(*pieces)]

    def piece_for(chunk, target):
        if per_half == 1:
            return chunk[0]
        out = chunk[0]
        for piece in range(1, per_half):
            out = jnp.where(lax.rem(target, per_half) == piece, chunk[piece], out)
        return out

    def send(chunk, cross):
        got = []
        for step in range(1, columns):
            pairs = []
            for t in range(columns):
                for c in range(cores):
                    target = (t + step) % columns
                    if target // per_half == c:
                        pairs.append((t * cores + c, target * cores + (c + cross) % cores))
            operand = piece_for(chunk, lax.rem(x + step, columns))
            got.append(lax.ppermute(operand, ("tensor", "sub"), pairs))
        return got

    def send_local(chunk):
        pairs = []
        for t in range(columns):
            c = t // per_half
            pairs.append((t * cores + c, t * cores + (c + 1) % cores))
        return lax.ppermute(piece_for(chunk, x), ("tensor", "sub"), pairs)

    def exchange(part):
        return [part] + [rotate(part, "tensor", step) for step in range(1, columns)]

    half_rows = row_count // 2
    one_half = [(0, half_rows)]
    both = one_half * 2
    up_other = rotate(up_adapters, "sub", 1)
    other_tokens = rotate(tokens, "sub", 1)
    pick, owner_of, used = tables([])
    down_packed = pack(down_adapters, [])
    down_arrived = by_owner(spread_out(down_packed))
    own_a, = shares(tokens, 0, half_rows, one_half, [down_packed])
    got_a = send(own_a, 0)
    up_packed = pack_wide(up_adapters, up_other, [own_a[-1]])
    own_b, = shares(tokens, half_rows, half_rows, one_half, [up_packed[0]])
    up_packed = tie(up_packed, [down_arrived, own_b[-1]])
    up_parts = along(up_packed, 1)

    down_part = adapter_product(owner_of, down_arrived, tokens, [up_packed[0], other_tokens])
    down_sums = exchange(down_part)
    own_b = tie(own_b, [down_part] + got_a)
    got_b = send(own_b, 0)
    cross_a, cross_a_near = shares(other_tokens, 0, half_rows, both, [own_b[-1]])
    *up_messages, down_wide = steps_gradients(
        place, owner_of, down_sums, cotangent, owners, half, 1.0, ADAPTER_SCALE, [cross_a[-1]]
    )
    up_messages = tie(up_messages, up_parts[1:])
    up_returned = along(up_messages, -1)
    back_part, up_cat = steps_product(place, owner_of, up_parts, cotangent, [up_messages[0]])
    back_sums = exchange(back_part)
    cross_a = tie(cross_a, [back_part] + got_b)
    late_a = send(cross_a, 1)
    down_messages, back_wide = gradients(
        owner_of, back_sums, tokens, owners, half, ADAPTER_SCALE, 1.0, jnp.int16, [cross_a[-1]]
    )
    down_returned = spread_out(down_messages)
    cross_b, cross_b_near = shares(other_tokens, half_rows, half_rows, both, [down_messages])
    late_b = send(cross_b, 1)
    collected = collect(up_returned, late_a + [cross_b[-1]])
    up_far = rotate(collected, "sub", 1)
    cross_a_near = tie(cross_a_near, [collected])
    local_a = send_local(cross_a_near)
    cross_b_near = tie(cross_b_near, [local_a])
    local_b = send_local(cross_b_near)

    tables_in = [place, pick, used, corr]
    fresh_up, fresh_up_first, fresh_up_second = steps_adam(
        tables_in, [up_adapters, up_first_moment, up_second_moment], up_returned, up_far,
        [cross_a_near[-1]],
    )
    mine_is_own = (lax.div(x, per_half) == s).astype(jnp.int32).reshape(1)
    terms_a = [(piece_for(own_a, x), 0, 1), (local_a, 0, 0)]
    terms_a += [(g, 0, 1) for g in got_a] + [(g, 0, 0) for g in late_a]
    terms_b = [(piece_for(own_b, x), half_rows, 1), (local_b, half_rows, 0)]
    terms_b += [(g, half_rows, 1) for g in got_b] + [(g, half_rows, 0) for g in late_b]
    projected = finish(
        mine_is_own, down_wide, up_cat, row_count, 0, half_rows, terms_a, None, [fresh_up]
    )
    fresh_down, fresh_down_first, fresh_down_second = coded_adam(
        tables_in, [down_adapters, down_first_moment, down_second_moment], down_returned,
        [projected],
    )
    projected = finish(
        mine_is_own, down_wide, up_cat, row_count, half_rows, half_rows, terms_b, projected,
        [fresh_down],
    )
    return (
        projected,
        flip(fresh_down),
        flip(fresh_up),
        flip(fresh_down_first),
        flip(fresh_up_first),
        flip(fresh_down_second),
        flip(fresh_up_second),
    )


def solution(mesh):
    placed = (
        P(("groups", "dp", "sub"), "tensor"),
        P("tensor", "sub"),
        P(("groups", "dp", "sub"), "tensor"),
        P(("groups", "dp"), ("tensor", "sub"), None),
        P(("groups", "dp"), ("tensor", "sub"), None),
        P(("groups", "dp"), ("tensor", "sub"), None),
        P(("groups", "dp"), ("tensor", "sub"), None),
        P(("groups", "dp"), ("tensor", "sub"), None),
        P(("groups", "dp"), ("tensor", "sub"), None),
        P(("groups", "dp")),
        P("groups"),
        P("groups"),
    )
    return jax.shard_map(
        on_device,
        mesh=mesh,
        in_specs=placed,
        out_specs=(
            P(("groups", "dp", "sub"), "tensor"),
            P(("groups", "dp"), ("tensor", "sub"), None),
            P(("groups", "dp"), ("tensor", "sub"), None),
            P(("groups", "dp"), ("tensor", "sub"), None),
            P(("groups", "dp"), ("tensor", "sub"), None),
            P(("groups", "dp"), ("tensor", "sub"), None),
            P(("groups", "dp"), ("tensor", "sub"), None),
        ),
        check_vma=False,
    )
```

```python
import functools

import jax
import jax.numpy as jnp
from jax import lax
from jax.experimental import pallas as pl
from jax.experimental.pallas import tpu as pltpu
from jax.sharding import PartitionSpec as P

BLK_ROWS = 128


ADAPTER_SCALE = 2.0
BETA_ONE = 0.9
BETA_TWO = 0.999
LEARN_RATE = 0.01
ADAM_EPS = 1e-08

SMEM = pl.BlockSpec(memory_space=pltpu.SMEM)
VMEM_BYTES = 65_500_000
TOP_CODE = 32767.0
LEVELS = 64.0
LEVEL_LANES = 128
COST = 20.0


def params():
    return pltpu.CompilerParams(vmem_limit_bytes=VMEM_BYTES)


def cost(micros):
    flops = int(micros * 1_000_000_000 * COST)
    return pl.CostEstimate(flops=flops, bytes_accessed=1000, transcendentals=0)


def rotate(value, axis, shift):
    size = lax.axis_size(axis)
    return lax.ppermute(value, axis, [(i, (i + shift) % size) for i in range(size)])


ANY = pl.BlockSpec(memory_space=pl.ANY)


def behind(kernel, deps, scalars=0):
    return lambda *refs: kernel(*refs[:scalars], *refs[scalars + len(deps) :])


def tie_kernel(*refs):
    pass


def tie(values, deps):
    return pl.pallas_call(
        tie_kernel,
        in_specs=[ANY] * (len(values) + len(deps)),
        out_specs=[ANY] * len(values),
        out_shape=[dims(v) for v in values],
        input_output_aliases={k: k for k in range(len(values))},
        compiler_params=params(),
        cost_estimate=cost(100),
        name="tie",
    )(*values, *deps)


def dims(value):
    return jax.ShapeDtypeStruct(value.shape, value.dtype)


def tables_kernel(devices, cores, slots, block_count, slot_of, tenant_of, pick, owner_of, used, place):
    z, s = lax.axis_index("dp"), lax.axis_index("sub")
    place[0] = z
    place[1] = s
    for k in range(slots):
        used[k] = 0

    def slot_at(device, b):
        return slot_of[tenant_of[device * block_count + b]]

    def per_device(device, carry):
        def per_block(b, found):
            local = slot_at(device, b) - z * slots
            mine = jnp.logical_and(local >= 0, local < slots)

            @pl.when(mine)
            def _():
                used[local] = 1

            return jnp.where(mine, local, found)

        pick[device] = lax.fori_loop(0, block_count, per_block, 0)
        return carry

    lax.fori_loop(0, devices, per_device, 0)
    for b in range(block_count):
        owner_of[b] = lax.div(slot_at(z * cores + s, b), slots)


def pack_kernel(devices, pick, own, out):
    for device in range(devices):
        out[device] = own[pick[device]].astype(jnp.bfloat16)


def pack_wide_kernel(owners, cores, place, pick, own, other, *outs):
    z, s = place[0], place[1]
    half = own.shape[2]
    for d in range(owners):
        k = pick[lax.rem(z + d, owners) * cores + s]
        near, far = own[k].astype(jnp.bfloat16), other[k].astype(jnp.bfloat16)
        outs[d][:, :half] = jnp.where(s == 0, near, far)
        outs[d][:, half:] = jnp.where(s == 0, far, near)


def product_kernel(owners, cores, rank, tile_rows, owner_of, *refs):
    halves, (rows, out) = refs[:cores], refs[cores:]
    step = pl.program_id(0)
    half = halves[0].shape[-1]
    full = 0.0
    for h in range(cores):
        full = full + lax.dot_general(
            halves[h][...].reshape(owners * rank, half),
            rows[:, h * half : (h + 1) * half],
            (((1,), (1,)), ((), ())),
            preferred_element_type=jnp.float32,
        )
    for b in range(tile_rows // BLK_ROWS):
        owner = owner_of[step * (tile_rows // BLK_ROWS) + b]
        span = slice(b * BLK_ROWS, (b + 1) * BLK_ROWS)
        value = full[:rank, span]
        for d in range(1, owners):
            value = jnp.where(owner == d, full[d * rank : (d + 1) * rank, span], value)
        out[:, span] = value


def steps_product_kernel(owners, rank, tile_rows, place, owner_of, *refs):
    parts, (rows, out, cat) = refs[:owners], refs[owners:]
    step = pl.program_id(0)

    @pl.when(step == 0)
    def _():
        for d in range(owners):
            owner = lax.rem(place[0] - d + owners, owners)
            cat[pl.ds(pl.multiple_of(owner * rank, rank), rank), :] = parts[d][...]

    full = lax.dot_general(
        cat[...], rows[...], (((1,), (1,)), ((), ())), preferred_element_type=jnp.float32
    )
    for b in range(tile_rows // BLK_ROWS):
        owner = owner_of[step * (tile_rows // BLK_ROWS) + b]
        span = slice(b * BLK_ROWS, (b + 1) * BLK_ROWS)
        value = full[:rank, span]
        for d in range(1, owners):
            value = jnp.where(owner == d, full[d * rank : (d + 1) * rank, span], value)
        out[:, span] = value


def steps_product(place, owner_of, parts, rows, deps):
    owners, (rank, features), row_count = len(parts), parts[0].shape, rows.shape[0]
    tile = min(256, row_count)
    return pl.pallas_call(
        behind(functools.partial(steps_product_kernel, owners, rank, tile), deps),
        grid=(row_count // tile,),
        in_specs=[ANY] * len(deps)
        + [SMEM] * 2
        + [pl.BlockSpec((rank, features), lambda i: (0, 0))] * owners
        + [pl.BlockSpec((tile, features), lambda i: (i, 0))],
        out_specs=[
            pl.BlockSpec((rank, tile), lambda i: (0, i)),
            pl.BlockSpec((owners * rank, features), lambda i: (0, 0)),
        ],
        out_shape=[
            jax.ShapeDtypeStruct((rank, row_count), jnp.float32),
            jax.ShapeDtypeStruct((owners * rank, features), jnp.bfloat16),
        ],
        compiler_params=params(),
        cost_estimate=cost(5),
        name="steps_product",
    )(*deps, place, owner_of, *parts, rows)


def halves_specs(owners, cores, rank, half):
    return [
        pl.BlockSpec((owners, None, rank, half), lambda *ids, h=h: (0, h, 0, 0))
        for h in range(cores)
    ]


def adapter_product(owner_of, adapters, rows, deps):
    (owners, cores, rank, half), (row_count, features) = adapters.shape, rows.shape
    tile = min(256, row_count)
    return pl.pallas_call(
        behind(functools.partial(product_kernel, owners, cores, rank, tile), deps),
        grid=(row_count // tile,),
        in_specs=[ANY] * len(deps)
        + [SMEM]
        + halves_specs(owners, cores, rank, half)
        + [pl.BlockSpec((tile, features), lambda i: (i, 0))],
        out_specs=pl.BlockSpec((rank, tile), lambda i: (0, i)),
        out_shape=jax.ShapeDtypeStruct((rank, row_count), jnp.float32),
        compiler_params=params(),
        cost_estimate=cost(5),
        name="adapter_product",
    )(*deps, owner_of, *[adapters] * cores, rows)


def encode(product, kind):
    if kind != jnp.int16:
        return product.astype(kind)
    top = jnp.maximum(jnp.max(jnp.abs(product), axis=1, keepdims=True), 1e-30)
    level = jnp.floor(jnp.log2(top) * LEVELS) + 2.0
    coded = jnp.round(product * (TOP_CODE * jnp.exp2(level * (-1.0 / LEVELS))))
    coded = jnp.clip(coded, -TOP_CODE, TOP_CODE).astype(jnp.int32).astype(jnp.int16)
    lanes = jnp.broadcast_to(level, (product.shape[0], LEVEL_LANES))
    return jnp.concatenate([coded, lanes.astype(jnp.int32).astype(jnp.int16)], axis=1)


def spread_rows(owners, rank, scale_in, owner_of, sums, wide):
    @pl.when(pl.program_id(0) == 0)
    def _():
        total = sums[0][...]
        for term in sums[1:]:
            total = total + term[...]
        value = (scale_in * total).astype(jnp.bfloat16)
        for b in range(value.shape[1] // BLK_ROWS):
            span = slice(b * BLK_ROWS, (b + 1) * BLK_ROWS)
            for d in range(owners):
                kept = jnp.where(owner_of[b] == d, value[:, span], jnp.zeros_like(value[:, span]))
                wide[d * rank : (d + 1) * rank, span] = kept


def steps_gradient_kernel(owners, rank, terms, scale_in, scale_out, place, owner_of, *refs):
    sums, rows, outs = refs[:terms], refs[terms], refs[terms + 1 : terms + 1 + owners]
    wide, coded = refs[-2:]
    spread_rows(owners, rank, scale_in, owner_of, sums, wide)
    product = scale_out * jnp.dot(wide[...], rows[...], preferred_element_type=jnp.float32)
    coded[...] = product.astype(coded.dtype)
    for d in range(owners):
        owner = lax.rem(place[0] - d + owners, owners)
        outs[d][...] = coded[pl.ds(pl.multiple_of(owner * rank, rank), rank), :]


def steps_gradients(place, owner_of, sums, rows, owners, half, scale_in, scale_out, deps):
    rank, row_count = sums[0].shape
    whole = pl.BlockSpec((rank, row_count), lambda h, place, owner_of: (0, 0))
    return pl.pallas_call(
        behind(
            functools.partial(
                steps_gradient_kernel, owners, rank, len(sums), scale_in, scale_out
            ),
            deps,
            2,
        ),
        grid_spec=pltpu.PrefetchScalarGridSpec(
            num_scalar_prefetch=2,
            grid=(2,),
            in_specs=[ANY] * len(deps)
            + [whole] * len(sums)
            + [
                pl.BlockSpec(
                    (row_count, half),
                    lambda h, place, owner_of: (0, jnp.where(h == 0, place[1], 1 - place[1])),
                )
            ],
            out_specs=[pl.BlockSpec((None, rank, half), lambda h, place, owner_of: (h, 0, 0))]
            * owners
            + [pl.BlockSpec((owners * rank, row_count), lambda h, place, owner_of: (0, 0))],
            scratch_shapes=[pltpu.VMEM((owners * rank, half), jnp.bfloat16)],
        ),
        out_shape=[jax.ShapeDtypeStruct((2, rank, half), jnp.bfloat16)] * owners
        + [jax.ShapeDtypeStruct((owners * rank, row_count), jnp.bfloat16)],
        compiler_params=params(),
        cost_estimate=cost(4),
        name="steps_gradients",
    )(place, owner_of, *deps, *sums, rows)


def collect_kernel(owners, *refs):
    for d in range(owners):
        refs[-1][d] = refs[d][...]


def collect(messages, deps):
    owners, (_, rank, half) = len(messages), messages[0].shape
    return pl.pallas_call(
        behind(functools.partial(collect_kernel, owners), deps),
        grid=(1,),
        in_specs=[ANY] * len(deps) + [pl.BlockSpec((None, rank, half), lambda i: (1, 0, 0))] * owners,
        out_specs=pl.BlockSpec((owners, rank, half), lambda i: (0, 0, 0)),
        out_shape=jax.ShapeDtypeStruct((owners, rank, half), messages[0].dtype),
        compiler_params=params(),
        cost_estimate=cost(1),
        name="collect",
    )(*deps, *messages)


def gradient_kernel(owners, rank, terms, scale_in, scale_out, owner_of, *refs):
    sums, (rows, out, wide) = refs[:terms], refs[terms:]
    spread_rows(owners, rank, scale_in, owner_of, sums, wide)
    product = scale_out * jnp.dot(wide[...], rows[...], preferred_element_type=jnp.float32)
    out[...] = encode(product, out.dtype).reshape(out.shape)


def gradients(owner_of, sums, rows, owners, half, scale_in, scale_out, kind, deps):
    rank, row_count = sums[0].shape
    cores = rows.shape[1] // half
    lanes = half + (LEVEL_LANES if kind == jnp.int16 else 0)
    whole = pl.BlockSpec((rank, row_count), lambda h: (0, 0))
    return pl.pallas_call(
        behind(
            functools.partial(gradient_kernel, owners, rank, len(sums), scale_in, scale_out), deps
        ),
        grid=(cores,),
        in_specs=[ANY] * len(deps)
        + [SMEM]
        + [whole] * len(sums)
        + [pl.BlockSpec((row_count, half), lambda h: (0, h))],
        out_specs=[
            pl.BlockSpec((owners, None, rank, lanes), lambda h: (0, h, 0, 0)),
            pl.BlockSpec((owners * rank, row_count), lambda h: (0, 0)),
        ],
        out_shape=[
            jax.ShapeDtypeStruct((owners, cores, rank, lanes), kind),
            jax.ShapeDtypeStruct((owners * rank, row_count), jnp.bfloat16),
        ],
        compiler_params=params(),
        cost_estimate=cost(4),
        name="gradients",
    )(*deps, owner_of, *sums, rows)


def share_kernel(spans, rows, weight, *outs):
    product = jnp.dot(rows[...], weight[...], preferred_element_type=jnp.float32)
    for out, (start, count) in zip(outs, spans):
        out[...] = product[start : start + count, :].astype(out.dtype)


def share(tokens, weight, piece, start, total, spans, width, deps):
    features = tokens.shape[1]
    tile = min(512, width)
    tiles = width // tile
    return pl.pallas_call(
        behind(functools.partial(share_kernel, spans), deps),
        grid=(tiles,),
        in_specs=[ANY] * len(deps)
        + [
            pl.BlockSpec((total, features), lambda j: (start // total, 0)),
            pl.BlockSpec((features, tile), lambda j: (0, piece * tiles + j)),
        ],
        out_specs=[pl.BlockSpec((count, tile), lambda j: (0, j)) for _, count in spans],
        out_shape=[jax.ShapeDtypeStruct((count, width), jnp.bfloat16) for _, count in spans],
        compiler_params=params(),
        cost_estimate=cost(4.0 * total / 256),
        name="share",
    )(*deps, tokens, weight)


def finish_kernel(steps, flags, spans, mine_is_own, wide, adapters, *refs):
    arrays, out = refs[: len(flags)], refs[-1]
    step = pl.program_id(0)
    turned = wide[...].T
    half = adapters.shape[1] // 2

    def run(kind):
        for h in range(2):
            span = slice(h * half, (h + 1) * half)
            total = ADAPTER_SCALE * jnp.dot(
                turned, adapters[:, span], preferred_element_type=jnp.float32
            )
            for array, flag, (first, last) in zip(arrays, flags, spans):
                if flag == kind:
                    value = array[:, span].astype(jnp.float32)
                    if last - first < steps:
                        active = jnp.logical_and(step >= first, step < last)
                        value = jnp.where(active, value, 0.0)
                    total = total + value
            out[:, span] = total.astype(out.dtype)

    for kind in (0, 1):
        pl.when(mine_is_own[0] == kind)(functools.partial(run, kind))


def finish(mine_is_own, wide, adapters, row_count, start, count, terms, previous, deps):
    stacked, width = adapters.shape
    tile = min(256, count)
    first = start // tile
    specs, spans = [], []
    for array, row, flag in terms:
        low, many = (row - start) // tile, array.shape[0] // tile

        def block_of(i, mine, low=low, many=many, flag=flag):
            return (jnp.where(mine[0] == flag, jnp.clip(i - low, 0, many - 1), 0), 0)

        specs.append(pl.BlockSpec((tile, width), block_of))
        spans.append((low, low + many))
    operands = [mine_is_own, *deps, wide, adapters]
    operands += [t[0] for t in terms]
    in_specs = (
        [ANY] * len(deps)
        + [
            pl.BlockSpec((stacked, tile), lambda i, mine: (0, first + i)),
            pl.BlockSpec((stacked, width), lambda i, mine: (0, 0)),
        ]
        + specs
    )
    aliases = {}
    if previous is not None:
        aliases = {len(operands): 0}
        operands.append(previous)
        in_specs.append(ANY)
    return pl.pallas_call(
        behind(functools.partial(finish_kernel, count // tile, [t[2] for t in terms], spans), deps, 1),
        grid_spec=pltpu.PrefetchScalarGridSpec(
            num_scalar_prefetch=1,
            grid=(count // tile,),
            in_specs=in_specs,
            out_specs=pl.BlockSpec((tile, width), lambda i, mine: (first + i, 0)),
        ),
        out_shape=jax.ShapeDtypeStruct((row_count, width), jnp.bfloat16),
        input_output_aliases=aliases,
        compiler_params=params(),
        cost_estimate=cost(4),
        name="finish",
    )(*operands)


def adam_step(slots, used, corr, param, first, second, new_param, new_first, new_second, grads):
    for k in range(slots):
        grad = grads[k]
        one = BETA_ONE * first[k] + (1.0 - BETA_ONE) * grad
        two = BETA_TWO * second[k] + (1.0 - BETA_TWO) * grad * grad
        update = LEARN_RATE * (one / corr[k]) / (jnp.sqrt(two / corr[slots + k]) + ADAM_EPS)
        keep = used[k] == 1
        new_param[k] = jnp.where(keep, param[k] - update, param[k])
        new_first[k] = jnp.where(keep, one, first[k])
        new_second[k] = jnp.where(keep, two, second[k])


def coded_adam_kernel(devices, slots, place, pick, used, corr, param, first, second, *refs):
    messages, levels = refs[:2]
    grads = refs[-1]
    grads[...] = jnp.zeros_like(grads)
    for device in range(devices):
        k = pick[device]
        level = levels[device].astype(jnp.float32)[:, :1]
        scale = jnp.exp2(level * (1.0 / LEVELS)) * (1.0 / TOP_CODE)
        grads[k] = grads[k] + messages[device].astype(jnp.float32) * scale
    adam_step(slots, used, corr, param, first, second, *refs[-4:])


def steps_adam_kernel(owners, slots, place, pick, used, corr, param, first, second, *refs):
    near, far, grads = refs[:owners], refs[owners], refs[-1]
    grads[...] = jnp.zeros_like(grads)
    for d in range(owners):
        device = lax.rem(place[0] + d, owners) * 2
        k = pick[device + place[1]]
        grads[k] = grads[k] + near[d][...].astype(jnp.float32)
        k = pick[device + 1 - place[1]]
        grads[k] = grads[k] + far[d].astype(jnp.float32)
    adam_step(slots, used, corr, param, first, second, *refs[-4:])


def adam(kernel, tables, states, messages, message_specs, deps):
    slots, rank, half = states[0].shape
    tile = feature_tile(half)
    state = pl.BlockSpec((slots, rank, tile), lambda i: (0, 0, i))
    return pl.pallas_call(
        behind(kernel, deps),
        grid=(half // tile,),
        in_specs=[ANY] * len(deps) + [SMEM] * len(tables) + [state] * 3 + message_specs,
        out_specs=[state] * 3,
        out_shape=[dims(states[0])] * 3,
        scratch_shapes=[pltpu.VMEM((slots, rank, tile), jnp.float32)],
        compiler_params=params(),
        cost_estimate=cost(4),
        name="adam",
    )(*deps, *tables, *states, *messages)


def feature_tile(half):
    return min(256, half)


def coded_adam(tables, states, messages, deps):
    devices, rank, _ = messages.shape
    slots, _, half = states[0].shape
    specs = [
        pl.BlockSpec((devices, rank, feature_tile(half)), lambda i: (0, 0, i)),
        pl.BlockSpec((devices, rank, LEVEL_LANES), lambda i: (0, 0, half // LEVEL_LANES)),
    ]
    kernel = functools.partial(coded_adam_kernel, devices, slots)
    return adam(kernel, tables, states, [messages] * 2, specs, deps)


def steps_adam(tables, states, near, far, deps):
    owners, rank, half = far.shape
    tile = feature_tile(half)
    specs = [pl.BlockSpec((None, rank, tile), lambda i: (0, 0, i))] * owners
    specs.append(pl.BlockSpec((owners, rank, tile), lambda i: (0, 0, i)))
    kernel = functools.partial(steps_adam_kernel, owners, states[0].shape[0])
    return adam(kernel, tables, states, [*near, far], specs, deps)


def on_device(
    tokens,
    frozen_weight,
    cotangent,
    down_adapters,
    up_adapters,
    down_first_moment,
    up_first_moment,
    down_second_moment,
    up_second_moment,
    optimizer_steps,
    slot_of_tenant,
    tenant_of_block,
):
    row_count, din_local = tokens.shape
    width = cotangent.shape[1]
    block_count = row_count // BLK_ROWS
    owners = lax.axis_size("dp")
    cores = lax.axis_size("sub")
    columns = lax.axis_size("tensor")
    s = lax.axis_index("sub")
    x = lax.axis_index("tensor")
    slots, half, rank = down_adapters.shape
    flip = lambda v: jnp.swapaxes(v, 1, 2)
    down_adapters, up_adapters = flip(down_adapters), flip(up_adapters)
    down_first_moment, up_first_moment = flip(down_first_moment), flip(up_first_moment)
    down_second_moment, up_second_moment = flip(down_second_moment), flip(up_second_moment)
    per_half = columns // cores

    devices = owners * cores

    pick, owner_of, used, place = pl.pallas_call(
        functools.partial(tables_kernel, devices, cores, slots, block_count),
        in_specs=[SMEM] * 2,
        out_specs=[SMEM] * 4,
        out_shape=[
            jax.ShapeDtypeStruct((devices,), jnp.int32),
            jax.ShapeDtypeStruct((block_count,), jnp.int32),
            jax.ShapeDtypeStruct((slots,), jnp.int32),
            jax.ShapeDtypeStruct((2,), jnp.int32),
        ],
        compiler_params=params(),
        cost_estimate=cost(2),
        name="tables",
    )(slot_of_tenant, tenant_of_block)
    steps = (optimizer_steps + 1).astype(jnp.float32)
    corr = jnp.concatenate(
        [
            1.0 - jnp.power(jnp.float32(BETA_ONE), steps),
            1.0 - jnp.power(jnp.float32(BETA_TWO), steps),
        ]
    )

    def pack(own):
        tile = feature_tile(half)
        return pl.pallas_call(
            functools.partial(pack_kernel, devices),
            grid=(half // tile,),
            in_specs=[SMEM, pl.BlockSpec((slots, rank, tile), lambda i: (0, 0, i))],
            out_specs=pl.BlockSpec((devices, rank, tile), lambda i: (0, 0, i)),
            out_shape=jax.ShapeDtypeStruct((devices, rank, half), jnp.bfloat16),
            compiler_params=params(),
            cost_estimate=cost(1),
            name="pack",
        )(pick, own)

    def spread_out(messages):
        flat = messages.reshape((devices,) + messages.shape[-2:])
        return lax.all_to_all(flat, ("dp", "sub"), split_axis=0, concat_axis=0, tiled=True)

    def by_owner(arrived):
        return arrived.reshape(owners, cores, rank, half)

    def pack_wide(own, other, deps):
        return pl.pallas_call(
            behind(functools.partial(pack_wide_kernel, owners, cores), deps),
            in_specs=[ANY] * len(deps)
            + [SMEM] * 2
            + [pl.BlockSpec(memory_space=pltpu.VMEM)] * 2,
            out_specs=[pl.BlockSpec(memory_space=pltpu.VMEM)] * owners,
            out_shape=[jax.ShapeDtypeStruct((rank, cores * half), jnp.bfloat16)] * owners,
            compiler_params=params(),
            cost_estimate=cost(1),
            name="pack_wide",
        )(*deps, place, pick, own, other)

    def along(messages, sign):
        return [m if d == 0 else rotate(m, "dp", sign * d) for d, m in enumerate(messages)]

    def shares(rows, start, total, spans, deps):
        pieces = []
        for piece in range(per_half):
            pieces.append(share(rows, frozen_weight, piece, start, total, spans, width, deps))
            deps = [pieces[-1][0]]
        return [list(chunk) for chunk in zip(*pieces)]

    def piece_for(chunk, target):
        if per_half == 1:
            return chunk[0]
        out = chunk[0]
        for piece in range(1, per_half):
            out = jnp.where(lax.rem(target, per_half) == piece, chunk[piece], out)
        return out

    def send(chunk, cross):
        got = []
        for step in range(1, columns):
            pairs = []
            for t in range(columns):
                for c in range(cores):
                    target = (t + step) % columns
                    if target // per_half == c:
                        pairs.append((t * cores + c, target * cores + (c + cross) % cores))
            operand = piece_for(chunk, lax.rem(x + step, columns))
            got.append(lax.ppermute(operand, ("tensor", "sub"), pairs))
        return got

    def send_local(chunk):
        pairs = []
        for t in range(columns):
            c = t // per_half
            pairs.append((t * cores + c, t * cores + (c + 1) % cores))
        return lax.ppermute(piece_for(chunk, x), ("tensor", "sub"), pairs)

    def exchange(part):
        return [part] + [rotate(part, "tensor", step) for step in range(1, columns)]

    half_rows = row_count // 2
    one_half = [(0, half_rows)]
    both = one_half * 2
    up_other = rotate(up_adapters, "sub", 1)
    other_tokens = rotate(tokens, "sub", 1)
    down_packed = pack(down_adapters)
    down_arrived = by_owner(spread_out(down_packed))
    own_a, = shares(tokens, 0, half_rows, one_half, [down_packed])
    got_a = send(own_a, 0)
    up_packed = pack_wide(up_adapters, up_other, [own_a[-1]])
    own_b, = shares(tokens, half_rows, half_rows, one_half, [up_packed[0]])
    up_packed = tie(up_packed, [down_arrived, own_b[-1]])
    up_parts = along(up_packed, 1)

    down_part = adapter_product(owner_of, down_arrived, tokens, [up_packed[0], other_tokens])
    down_sums = exchange(down_part)
    own_b = tie(own_b, [down_part] + got_a)
    got_b = send(own_b, 0)
    cross_a, cross_a_near = shares(other_tokens, 0, half_rows, both, [own_b[-1]])
    *up_messages, down_wide = steps_gradients(
        place, owner_of, down_sums, cotangent, owners, half, 1.0, ADAPTER_SCALE, [cross_a[-1]]
    )
    up_messages = tie(up_messages, up_parts[1:])
    up_returned = along(up_messages, -1)
    back_part, up_cat = steps_product(place, owner_of, up_parts, cotangent, [up_messages[0]])
    back_sums = exchange(back_part)
    cross_a = tie(cross_a, [back_part] + got_b)
    late_a = send(cross_a, 1)
    down_messages, back_wide = gradients(
        owner_of, back_sums, tokens, owners, half, ADAPTER_SCALE, 1.0, jnp.int16, [cross_a[-1]]
    )
    down_returned = spread_out(down_messages)
    cross_b, cross_b_near = shares(other_tokens, half_rows, half_rows, both, [down_messages])
    late_b = send(cross_b, 1)
    collected = collect(up_returned, late_a + [cross_b[-1]])
    up_far = rotate(collected, "sub", 1)
    cross_a_near = tie(cross_a_near, [collected])
    local_a = send_local(cross_a_near)
    cross_b_near = tie(cross_b_near, [local_a])
    local_b = send_local(cross_b_near)

    tables_in = [place, pick, used, corr]
    fresh_up, fresh_up_first, fresh_up_second = steps_adam(
        tables_in, [up_adapters, up_first_moment, up_second_moment], up_returned, up_far,
        [cross_a_near[-1]],
    )
    mine_is_own = (lax.div(x, per_half) == s).astype(jnp.int32).reshape(1)
    terms_a = [(piece_for(own_a, x), 0, 1), (local_a, 0, 0)]
    terms_a += [(g, 0, 1) for g in got_a] + [(g, 0, 0) for g in late_a]
    terms_b = [(piece_for(own_b, x), half_rows, 1), (local_b, half_rows, 0)]
    terms_b += [(g, half_rows, 1) for g in got_b] + [(g, half_rows, 0) for g in late_b]
    projected = finish(
        mine_is_own, down_wide, up_cat, row_count, 0, half_rows, terms_a, None, [fresh_up]
    )
    fresh_down, fresh_down_first, fresh_down_second = coded_adam(
        tables_in, [down_adapters, down_first_moment, down_second_moment], down_returned,
        [projected],
    )
    projected = finish(
        mine_is_own, down_wide, up_cat, row_count, half_rows, half_rows, terms_b, projected,
        [fresh_down],
    )
    return (
        projected,
        flip(fresh_down),
        flip(fresh_up),
        flip(fresh_down_first),
        flip(fresh_up_first),
        flip(fresh_down_second),
        flip(fresh_up_second),
    )


def solution(mesh):
    placed = (
        P(("groups", "dp", "sub"), "tensor"),
        P("tensor", "sub"),
        P(("groups", "dp", "sub"), "tensor"),
        P(("groups", "dp"), ("tensor", "sub"), None),
        P(("groups", "dp"), ("tensor", "sub"), None),
        P(("groups", "dp"), ("tensor", "sub"), None),
        P(("groups", "dp"), ("tensor", "sub"), None),
        P(("groups", "dp"), ("tensor", "sub"), None),
        P(("groups", "dp"), ("tensor", "sub"), None),
        P(("groups", "dp")),
        P("groups"),
        P("groups"),
    )
    return jax.shard_map(
        on_device,
        mesh=mesh,
        in_specs=placed,
        out_specs=(
            P(("groups", "dp", "sub"), "tensor"),
            P(("groups", "dp"), ("tensor", "sub"), None),
            P(("groups", "dp"), ("tensor", "sub"), None),
            P(("groups", "dp"), ("tensor", "sub"), None),
            P(("groups", "dp"), ("tensor", "sub"), None),
            P(("groups", "dp"), ("tensor", "sub"), None),
            P(("groups", "dp"), ("tensor", "sub"), None),
        ),
        check_vma=False,
    )
```

```python
import functools

import jax
import jax.numpy as jnp
from jax import lax
from jax.experimental import pallas as pl
from jax.experimental.pallas import tpu as pltpu
from jax.sharding import PartitionSpec as P

BLK_ROWS = 128


ADAPTER_SCALE = 2.0
BETA_ONE = 0.9
BETA_TWO = 0.999
LEARN_RATE = 0.01
ADAM_EPS = 1e-08

SMEM = pl.BlockSpec(memory_space=pltpu.SMEM)
VMEM_BYTES = 65_500_000
TOP_CODE = 32767.0
LEVELS = 64.0
LEVEL_LANES = 128
COST = 20.0


def params():
    return pltpu.CompilerParams(vmem_limit_bytes=VMEM_BYTES)


def cost(micros):
    flops = int(micros * 1_000_000_000 * COST)
    return pl.CostEstimate(flops=flops, bytes_accessed=1000, transcendentals=0)


def rotate(value, axis, shift):
    size = lax.axis_size(axis)
    return lax.ppermute(value, axis, [(i, (i + shift) % size) for i in range(size)])


ANY = pl.BlockSpec(memory_space=pl.ANY)


def behind(kernel, deps, scalars=0):
    return lambda *refs: kernel(*refs[:scalars], *refs[scalars + len(deps) :])


def tie_kernel(*refs):
    pass


def tie(values, deps):
    return pl.pallas_call(
        tie_kernel,
        in_specs=[ANY] * (len(values) + len(deps)),
        out_specs=[ANY] * len(values),
        out_shape=[dims(v) for v in values],
        input_output_aliases={k: k for k in range(len(values))},
        compiler_params=params(),
        cost_estimate=cost(100),
        name="tie",
    )(*values, *deps)


def dims(value):
    return jax.ShapeDtypeStruct(value.shape, value.dtype)


def tables_kernel(devices, cores, slots, block_count, slot_of, tenant_of, pick, owner_of, used, place):
    z, s = lax.axis_index("dp"), lax.axis_index("sub")
    place[0] = z
    place[1] = s
    for k in range(slots):
        used[k] = 0

    def slot_at(device, b):
        return slot_of[tenant_of[device * block_count + b]]

    def per_device(device, carry):
        def per_block(b, found):
            local = slot_at(device, b) - z * slots
            mine = jnp.logical_and(local >= 0, local < slots)

            @pl.when(mine)
            def _():
                used[local] = 1

            return jnp.where(mine, local, found)

        pick[device] = lax.fori_loop(0, block_count, per_block, 0)
        return carry

    lax.fori_loop(0, devices, per_device, 0)
    for b in range(block_count):
        owner_of[b] = lax.div(slot_at(z * cores + s, b), slots)


def pack_kernel(devices, pick, own, out):
    for device in range(devices):
        out[device] = own[pick[device]].astype(jnp.bfloat16)


def pack_wide_kernel(owners, cores, place, pick, own, other, *outs):
    z, s = place[0], place[1]
    half = own.shape[2]
    for d in range(owners):
        k = pick[lax.rem(z + d, owners) * cores + s]
        near, far = own[k].astype(jnp.bfloat16), other[k].astype(jnp.bfloat16)
        outs[d][:, :half] = jnp.where(s == 0, near, far)
        outs[d][:, half:] = jnp.where(s == 0, far, near)


def product_kernel(owners, cores, rank, tile_rows, owner_of, *refs):
    halves, (rows, out) = refs[:cores], refs[cores:]
    step = pl.program_id(0)
    half = halves[0].shape[-1]
    full = 0.0
    for h in range(cores):
        full = full + lax.dot_general(
            halves[h][...].reshape(owners * rank, half),
            rows[:, h * half : (h + 1) * half],
            (((1,), (1,)), ((), ())),
            preferred_element_type=jnp.float32,
        )
    for b in range(tile_rows // BLK_ROWS):
        owner = owner_of[step * (tile_rows // BLK_ROWS) + b]
        span = slice(b * BLK_ROWS, (b + 1) * BLK_ROWS)
        value = full[:rank, span]
        for d in range(1, owners):
            value = jnp.where(owner == d, full[d * rank : (d + 1) * rank, span], value)
        out[:, span] = value


def steps_product_kernel(owners, rank, tile_rows, place, owner_of, *refs):
    parts, (rows, out, cat) = refs[:owners], refs[owners:]
    step = pl.program_id(0)

    @pl.when(step == 0)
    def _():
        for d in range(owners):
            owner = lax.rem(place[0] - d + owners, owners)
            cat[pl.ds(pl.multiple_of(owner * rank, rank), rank), :] = parts[d][...]

    full = lax.dot_general(
        cat[...], rows[...], (((1,), (1,)), ((), ())), preferred_element_type=jnp.float32
    )
    for b in range(tile_rows // BLK_ROWS):
        owner = owner_of[step * (tile_rows // BLK_ROWS) + b]
        span = slice(b * BLK_ROWS, (b + 1) * BLK_ROWS)
        value = full[:rank, span]
        for d in range(1, owners):
            value = jnp.where(owner == d, full[d * rank : (d + 1) * rank, span], value)
        out[:, span] = value


def steps_product(place, owner_of, parts, rows, deps):
    owners, (rank, features), row_count = len(parts), parts[0].shape, rows.shape[0]
    tile = min(256, row_count)
    return pl.pallas_call(
        behind(functools.partial(steps_product_kernel, owners, rank, tile), deps),
        grid=(row_count // tile,),
        in_specs=[ANY] * len(deps)
        + [SMEM] * 2
        + [pl.BlockSpec((rank, features), lambda i: (0, 0))] * owners
        + [pl.BlockSpec((tile, features), lambda i: (i, 0))],
        out_specs=[
            pl.BlockSpec((rank, tile), lambda i: (0, i)),
            pl.BlockSpec((owners * rank, features), lambda i: (0, 0)),
        ],
        out_shape=[
            jax.ShapeDtypeStruct((rank, row_count), jnp.float32),
            jax.ShapeDtypeStruct((owners * rank, features), jnp.bfloat16),
        ],
        compiler_params=params(),
        cost_estimate=cost(5),
        name="steps_product",
    )(*deps, place, owner_of, *parts, rows)


def halves_specs(owners, cores, rank, half):
    return [
        pl.BlockSpec((owners, None, rank, half), lambda *ids, h=h: (0, h, 0, 0))
        for h in range(cores)
    ]


def adapter_product(owner_of, adapters, rows, deps):
    (owners, cores, rank, half), (row_count, features) = adapters.shape, rows.shape
    tile = min(256, row_count)
    return pl.pallas_call(
        behind(functools.partial(product_kernel, owners, cores, rank, tile), deps),
        grid=(row_count // tile,),
        in_specs=[ANY] * len(deps)
        + [SMEM]
        + halves_specs(owners, cores, rank, half)
        + [pl.BlockSpec((tile, features), lambda i: (i, 0))],
        out_specs=pl.BlockSpec((rank, tile), lambda i: (0, i)),
        out_shape=jax.ShapeDtypeStruct((rank, row_count), jnp.float32),
        compiler_params=params(),
        cost_estimate=cost(5),
        name="adapter_product",
    )(*deps, owner_of, *[adapters] * cores, rows)


def encode(product, kind):
    if kind != jnp.int16:
        return product.astype(kind)
    top = jnp.maximum(jnp.max(jnp.abs(product), axis=1, keepdims=True), 1e-30)
    level = jnp.floor(jnp.log2(top) * LEVELS) + 2.0
    coded = jnp.round(product * (TOP_CODE * jnp.exp2(level * (-1.0 / LEVELS))))
    coded = jnp.clip(coded, -TOP_CODE, TOP_CODE).astype(jnp.int32).astype(jnp.int16)
    lanes = jnp.broadcast_to(level, (product.shape[0], LEVEL_LANES))
    return jnp.concatenate([coded, lanes.astype(jnp.int32).astype(jnp.int16)], axis=1)


def spread_rows(owners, rank, scale_in, owner_of, sums, wide):
    @pl.when(pl.program_id(0) == 0)
    def _():
        total = sums[0][...]
        for term in sums[1:]:
            total = total + term[...]
        value = (scale_in * total).astype(jnp.bfloat16)
        for b in range(value.shape[1] // BLK_ROWS):
            span = slice(b * BLK_ROWS, (b + 1) * BLK_ROWS)
            for d in range(owners):
                kept = jnp.where(owner_of[b] == d, value[:, span], jnp.zeros_like(value[:, span]))
                wide[d * rank : (d + 1) * rank, span] = kept


def steps_gradient_kernel(owners, rank, terms, scale_in, scale_out, place, owner_of, *refs):
    sums, rows, outs = refs[:terms], refs[terms], refs[terms + 1 : terms + 1 + owners]
    wide, coded = refs[-2:]
    spread_rows(owners, rank, scale_in, owner_of, sums, wide)
    product = scale_out * jnp.dot(wide[...], rows[...], preferred_element_type=jnp.float32)
    coded[...] = product.astype(coded.dtype)
    for d in range(owners):
        owner = lax.rem(place[0] - d + owners, owners)
        outs[d][...] = coded[pl.ds(pl.multiple_of(owner * rank, rank), rank), :]


def steps_gradients(place, owner_of, sums, rows, owners, half, scale_in, scale_out, deps):
    rank, row_count = sums[0].shape
    whole = pl.BlockSpec((rank, row_count), lambda h, place, owner_of: (0, 0))
    return pl.pallas_call(
        behind(
            functools.partial(
                steps_gradient_kernel, owners, rank, len(sums), scale_in, scale_out
            ),
            deps,
            2,
        ),
        grid_spec=pltpu.PrefetchScalarGridSpec(
            num_scalar_prefetch=2,
            grid=(2,),
            in_specs=[ANY] * len(deps)
            + [whole] * len(sums)
            + [
                pl.BlockSpec(
                    (row_count, half),
                    lambda h, place, owner_of: (0, jnp.where(h == 0, place[1], 1 - place[1])),
                )
            ],
            out_specs=[pl.BlockSpec((None, rank, half), lambda h, place, owner_of: (h, 0, 0))]
            * owners
            + [pl.BlockSpec((owners * rank, row_count), lambda h, place, owner_of: (0, 0))],
            scratch_shapes=[pltpu.VMEM((owners * rank, half), jnp.bfloat16)],
        ),
        out_shape=[jax.ShapeDtypeStruct((2, rank, half), jnp.bfloat16)] * owners
        + [jax.ShapeDtypeStruct((owners * rank, row_count), jnp.bfloat16)],
        compiler_params=params(),
        cost_estimate=cost(4),
        name="steps_gradients",
    )(place, owner_of, *deps, *sums, rows)


def collect_kernel(owners, *refs):
    for d in range(owners):
        refs[-1][d] = refs[d][...]


def collect(messages, deps):
    owners, (_, rank, half) = len(messages), messages[0].shape
    return pl.pallas_call(
        behind(functools.partial(collect_kernel, owners), deps),
        grid=(1,),
        in_specs=[ANY] * len(deps) + [pl.BlockSpec((None, rank, half), lambda i: (1, 0, 0))] * owners,
        out_specs=pl.BlockSpec((owners, rank, half), lambda i: (0, 0, 0)),
        out_shape=jax.ShapeDtypeStruct((owners, rank, half), messages[0].dtype),
        compiler_params=params(),
        cost_estimate=cost(1),
        name="collect",
    )(*deps, *messages)


def gradient_kernel(owners, rank, terms, scale_in, scale_out, owner_of, *refs):
    sums, (rows, out, wide) = refs[:terms], refs[terms:]
    spread_rows(owners, rank, scale_in, owner_of, sums, wide)
    product = scale_out * jnp.dot(wide[...], rows[...], preferred_element_type=jnp.float32)
    out[...] = encode(product, out.dtype).reshape(out.shape)


def gradients(owner_of, sums, rows, owners, half, scale_in, scale_out, kind, deps):
    rank, row_count = sums[0].shape
    cores = rows.shape[1] // half
    lanes = half + (LEVEL_LANES if kind == jnp.int16 else 0)
    whole = pl.BlockSpec((rank, row_count), lambda h: (0, 0))
    return pl.pallas_call(
        behind(
            functools.partial(gradient_kernel, owners, rank, len(sums), scale_in, scale_out), deps
        ),
        grid=(cores,),
        in_specs=[ANY] * len(deps)
        + [SMEM]
        + [whole] * len(sums)
        + [pl.BlockSpec((row_count, half), lambda h: (0, h))],
        out_specs=[
            pl.BlockSpec((owners, None, rank, lanes), lambda h: (0, h, 0, 0)),
            pl.BlockSpec((owners * rank, row_count), lambda h: (0, 0)),
        ],
        out_shape=[
            jax.ShapeDtypeStruct((owners, cores, rank, lanes), kind),
            jax.ShapeDtypeStruct((owners * rank, row_count), jnp.bfloat16),
        ],
        compiler_params=params(),
        cost_estimate=cost(4),
        name="gradients",
    )(*deps, owner_of, *sums, rows)


def share_kernel(spans, rows, weight, *outs):
    product = jnp.dot(rows[...], weight[...], preferred_element_type=jnp.float32)
    for out, (start, count) in zip(outs, spans):
        out[...] = product[start : start + count, :].astype(out.dtype)


def share(tokens, weight, piece, start, total, spans, width, deps):
    features = tokens.shape[1]
    tile = min(512, width)
    tiles = width // tile
    return pl.pallas_call(
        behind(functools.partial(share_kernel, spans), deps),
        grid=(tiles,),
        in_specs=[ANY] * len(deps)
        + [
            pl.BlockSpec((total, features), lambda j: (start // total, 0)),
            pl.BlockSpec((features, tile), lambda j: (0, piece * tiles + j)),
        ],
        out_specs=[pl.BlockSpec((count, tile), lambda j: (0, j)) for _, count in spans],
        out_shape=[jax.ShapeDtypeStruct((count, width), jnp.bfloat16) for _, count in spans],
        compiler_params=params(),
        cost_estimate=cost(4.0 * total / 256),
        name="share",
    )(*deps, tokens, weight)


def finish_kernel(steps, flags, spans, mine_is_own, wide, adapters, *refs):
    arrays, out = refs[: len(flags)], refs[-1]
    step = pl.program_id(0)
    turned = wide[...].T
    half = adapters.shape[1] // 2

    def run(kind):
        for h in range(2):
            span = slice(h * half, (h + 1) * half)
            total = ADAPTER_SCALE * jnp.dot(
                turned, adapters[:, span], preferred_element_type=jnp.float32
            )
            for array, flag, (first, last) in zip(arrays, flags, spans):
                if flag == kind:
                    value = array[:, span].astype(jnp.float32)
                    if last - first < steps:
                        active = jnp.logical_and(step >= first, step < last)
                        value = jnp.where(active, value, 0.0)
                    total = total + value
            out[:, span] = total.astype(out.dtype)

    for kind in (0, 1):
        pl.when(mine_is_own[0] == kind)(functools.partial(run, kind))


def finish(mine_is_own, wide, adapters, row_count, start, count, terms, previous, deps):
    stacked, width = adapters.shape
    tile = min(256, count)
    first = start // tile
    specs, spans = [], []
    for array, row, flag in terms:
        low, many = (row - start) // tile, array.shape[0] // tile

        def block_of(i, mine, low=low, many=many, flag=flag):
            return (jnp.where(mine[0] == flag, jnp.clip(i - low, 0, many - 1), 0), 0)

        specs.append(pl.BlockSpec((tile, width), block_of))
        spans.append((low, low + many))
    operands = [mine_is_own, *deps, wide, adapters]
    operands += [t[0] for t in terms]
    in_specs = (
        [ANY] * len(deps)
        + [
            pl.BlockSpec((stacked, tile), lambda i, mine: (0, first + i)),
            pl.BlockSpec((stacked, width), lambda i, mine: (0, 0)),
        ]
        + specs
    )
    aliases = {}
    if previous is not None:
        aliases = {len(operands): 0}
        operands.append(previous)
        in_specs.append(ANY)
    return pl.pallas_call(
        behind(functools.partial(finish_kernel, count // tile, [t[2] for t in terms], spans), deps, 1),
        grid_spec=pltpu.PrefetchScalarGridSpec(
            num_scalar_prefetch=1,
            grid=(count // tile,),
            in_specs=in_specs,
            out_specs=pl.BlockSpec((tile, width), lambda i, mine: (first + i, 0)),
        ),
        out_shape=jax.ShapeDtypeStruct((row_count, width), jnp.bfloat16),
        input_output_aliases=aliases,
        compiler_params=params(),
        cost_estimate=cost(4),
        name="finish",
    )(*operands)


def adam_step(slots, used, corr, param, first, second, new_param, new_first, new_second, grads):
    for k in range(slots):
        grad = grads[k]
        one = BETA_ONE * first[k] + (1.0 - BETA_ONE) * grad
        two = BETA_TWO * second[k] + (1.0 - BETA_TWO) * grad * grad
        update = LEARN_RATE * (one / corr[k]) / (jnp.sqrt(two / corr[slots + k]) + ADAM_EPS)
        keep = used[k] == 1
        new_param[k] = jnp.where(keep, param[k] - update, param[k])
        new_first[k] = jnp.where(keep, one, first[k])
        new_second[k] = jnp.where(keep, two, second[k])


def coded_adam_kernel(devices, slots, place, pick, used, corr, param, first, second, *refs):
    messages, levels = refs[:2]
    grads = refs[-1]
    grads[...] = jnp.zeros_like(grads)
    for device in range(devices):
        k = pick[device]
        level = levels[device].astype(jnp.float32)[:, :1]
        scale = jnp.exp2(level * (1.0 / LEVELS)) * (1.0 / TOP_CODE)
        grads[k] = grads[k] + messages[device].astype(jnp.float32) * scale
    adam_step(slots, used, corr, param, first, second, *refs[-4:])


def steps_adam_kernel(owners, slots, place, pick, used, corr, param, first, second, *refs):
    near, far, grads = refs[:owners], refs[owners], refs[-1]
    grads[...] = jnp.zeros_like(grads)
    for d in range(owners):
        device = lax.rem(place[0] + d, owners) * 2
        k = pick[device + place[1]]
        grads[k] = grads[k] + near[d][...].astype(jnp.float32)
        k = pick[device + 1 - place[1]]
        grads[k] = grads[k] + far[d].astype(jnp.float32)
    adam_step(slots, used, corr, param, first, second, *refs[-4:])


def adam(kernel, tables, states, messages, message_specs, deps):
    slots, rank, half = states[0].shape
    tile = feature_tile(half)
    state = pl.BlockSpec((slots, rank, tile), lambda i: (0, 0, i))
    return pl.pallas_call(
        behind(kernel, deps),
        grid=(half // tile,),
        in_specs=[ANY] * len(deps) + [SMEM] * len(tables) + [state] * 3 + message_specs,
        out_specs=[state] * 3,
        out_shape=[dims(states[0])] * 3,
        scratch_shapes=[pltpu.VMEM((slots, rank, tile), jnp.float32)],
        compiler_params=params(),
        cost_estimate=cost(4),
        name="adam",
    )(*deps, *tables, *states, *messages)


def feature_tile(half):
    return min(512, half)


def coded_adam(tables, states, messages, deps):
    devices, rank, _ = messages.shape
    slots, _, half = states[0].shape
    specs = [
        pl.BlockSpec((devices, rank, feature_tile(half)), lambda i: (0, 0, i)),
        pl.BlockSpec((devices, rank, LEVEL_LANES), lambda i: (0, 0, half // LEVEL_LANES)),
    ]
    kernel = functools.partial(coded_adam_kernel, devices, slots)
    return adam(kernel, tables, states, [messages] * 2, specs, deps)


def steps_adam(tables, states, near, far, deps):
    owners, rank, half = far.shape
    tile = feature_tile(half)
    specs = [pl.BlockSpec((None, rank, tile), lambda i: (0, 0, i))] * owners
    specs.append(pl.BlockSpec((owners, rank, tile), lambda i: (0, 0, i)))
    kernel = functools.partial(steps_adam_kernel, owners, states[0].shape[0])
    return adam(kernel, tables, states, [*near, far], specs, deps)


def on_device(
    tokens,
    frozen_weight,
    cotangent,
    down_adapters,
    up_adapters,
    down_first_moment,
    up_first_moment,
    down_second_moment,
    up_second_moment,
    optimizer_steps,
    slot_of_tenant,
    tenant_of_block,
):
    row_count, din_local = tokens.shape
    width = cotangent.shape[1]
    block_count = row_count // BLK_ROWS
    owners = lax.axis_size("dp")
    cores = lax.axis_size("sub")
    columns = lax.axis_size("tensor")
    s = lax.axis_index("sub")
    x = lax.axis_index("tensor")
    slots, half, rank = down_adapters.shape
    flip = lambda v: jnp.swapaxes(v, 1, 2)
    down_adapters, up_adapters = flip(down_adapters), flip(up_adapters)
    down_first_moment, up_first_moment = flip(down_first_moment), flip(up_first_moment)
    down_second_moment, up_second_moment = flip(down_second_moment), flip(up_second_moment)
    per_half = columns // cores

    devices = owners * cores

    pick, owner_of, used, place = pl.pallas_call(
        functools.partial(tables_kernel, devices, cores, slots, block_count),
        in_specs=[SMEM] * 2,
        out_specs=[SMEM] * 4,
        out_shape=[
            jax.ShapeDtypeStruct((devices,), jnp.int32),
            jax.ShapeDtypeStruct((block_count,), jnp.int32),
            jax.ShapeDtypeStruct((slots,), jnp.int32),
            jax.ShapeDtypeStruct((2,), jnp.int32),
        ],
        compiler_params=params(),
        cost_estimate=cost(2),
        name="tables",
    )(slot_of_tenant, tenant_of_block)
    steps = (optimizer_steps + 1).astype(jnp.float32)
    corr = jnp.concatenate(
        [
            1.0 - jnp.power(jnp.float32(BETA_ONE), steps),
            1.0 - jnp.power(jnp.float32(BETA_TWO), steps),
        ]
    )

    def pack(own):
        return pl.pallas_call(
            functools.partial(pack_kernel, devices),
            in_specs=[SMEM, pl.BlockSpec(memory_space=pltpu.VMEM)],
            out_specs=pl.BlockSpec(memory_space=pltpu.VMEM),
            out_shape=jax.ShapeDtypeStruct((devices, rank, half), jnp.bfloat16),
            compiler_params=params(),
            cost_estimate=cost(1),
            name="pack",
        )(pick, own)

    def spread_out(messages):
        flat = messages.reshape((devices,) + messages.shape[-2:])
        return lax.all_to_all(flat, ("dp", "sub"), split_axis=0, concat_axis=0, tiled=True)

    def by_owner(arrived):
        return arrived.reshape(owners, cores, rank, half)

    def pack_wide(own, other, deps):
        return pl.pallas_call(
            behind(functools.partial(pack_wide_kernel, owners, cores), deps),
            in_specs=[ANY] * len(deps)
            + [SMEM] * 2
            + [pl.BlockSpec(memory_space=pltpu.VMEM)] * 2,
            out_specs=[pl.BlockSpec(memory_space=pltpu.VMEM)] * owners,
            out_shape=[jax.ShapeDtypeStruct((rank, cores * half), jnp.bfloat16)] * owners,
            compiler_params=params(),
            cost_estimate=cost(1),
            name="pack_wide",
        )(*deps, place, pick, own, other)

    def along(messages, sign):
        return [m if d == 0 else rotate(m, "dp", sign * d) for d, m in enumerate(messages)]

    def shares(rows, start, total, spans, deps):
        pieces = []
        for piece in range(per_half):
            pieces.append(share(rows, frozen_weight, piece, start, total, spans, width, deps))
            deps = [pieces[-1][0]]
        return [list(chunk) for chunk in zip(*pieces)]

    def piece_for(chunk, target):
        if per_half == 1:
            return chunk[0]
        out = chunk[0]
        for piece in range(1, per_half):
            out = jnp.where(lax.rem(target, per_half) == piece, chunk[piece], out)
        return out

    def send(chunk, cross):
        got = []
        for step in range(1, columns):
            pairs = []
            for t in range(columns):
                for c in range(cores):
                    target = (t + step) % columns
                    if target // per_half == c:
                        pairs.append((t * cores + c, target * cores + (c + cross) % cores))
            operand = piece_for(chunk, lax.rem(x + step, columns))
            got.append(lax.ppermute(operand, ("tensor", "sub"), pairs))
        return got

    def send_local(chunk):
        pairs = []
        for t in range(columns):
            c = t // per_half
            pairs.append((t * cores + c, t * cores + (c + 1) % cores))
        return lax.ppermute(piece_for(chunk, x), ("tensor", "sub"), pairs)

    def exchange(part):
        return [part] + [rotate(part, "tensor", step) for step in range(1, columns)]

    half_rows = row_count // 2
    one_half = [(0, half_rows)]
    both = one_half * 2
    up_other = rotate(up_adapters, "sub", 1)
    other_tokens = rotate(tokens, "sub", 1)
    down_packed = pack(down_adapters)
    down_arrived = by_owner(spread_out(down_packed))
    own_a, = shares(tokens, 0, half_rows, one_half, [down_packed])
    got_a = send(own_a, 0)
    up_packed = pack_wide(up_adapters, up_other, [own_a[-1]])
    own_b, = shares(tokens, half_rows, half_rows, one_half, [up_packed[0]])
    up_packed = tie(up_packed, [down_arrived, own_b[-1]])
    up_parts = along(up_packed, 1)

    down_part = adapter_product(owner_of, down_arrived, tokens, [up_packed[0], other_tokens])
    down_sums = exchange(down_part)
    own_b = tie(own_b, [down_part] + got_a)
    got_b = send(own_b, 0)
    cross_a, cross_a_near = shares(other_tokens, 0, half_rows, both, [own_b[-1]])
    *up_messages, down_wide = steps_gradients(
        place, owner_of, down_sums, cotangent, owners, half, 1.0, ADAPTER_SCALE, [cross_a[-1]]
    )
    up_messages = tie(up_messages, up_parts[1:])
    up_returned = along(up_messages, -1)
    back_part, up_cat = steps_product(place, owner_of, up_parts, cotangent, [up_messages[0]])
    back_sums = exchange(back_part)
    cross_a = tie(cross_a, [back_part] + got_b)
    late_a = send(cross_a, 1)
    down_messages, back_wide = gradients(
        owner_of, back_sums, tokens, owners, half, ADAPTER_SCALE, 1.0, jnp.int16, [cross_a[-1]]
    )
    down_returned = spread_out(down_messages)
    cross_b, cross_b_near = shares(other_tokens, half_rows, half_rows, both, [down_messages])
    late_b = send(cross_b, 1)
    collected = collect(up_returned, late_a + [cross_b[-1]])
    up_far = rotate(collected, "sub", 1)
    cross_a_near = tie(cross_a_near, [collected])
    local_a = send_local(cross_a_near)
    cross_b_near = tie(cross_b_near, [local_a])
    local_b = send_local(cross_b_near)

    tables_in = [place, pick, used, corr]
    fresh_up, fresh_up_first, fresh_up_second = steps_adam(
        tables_in, [up_adapters, up_first_moment, up_second_moment], up_returned, up_far,
        [cross_a_near[-1]],
    )
    mine_is_own = (lax.div(x, per_half) == s).astype(jnp.int32).reshape(1)
    terms_a = [(piece_for(own_a, x), 0, 1), (local_a, 0, 0)]
    terms_a += [(g, 0, 1) for g in got_a] + [(g, 0, 0) for g in late_a]
    terms_b = [(piece_for(own_b, x), half_rows, 1), (local_b, half_rows, 0)]
    terms_b += [(g, half_rows, 1) for g in got_b] + [(g, half_rows, 0) for g in late_b]
    projected = finish(
        mine_is_own, down_wide, up_cat, row_count, 0, half_rows, terms_a, None, [fresh_up]
    )
    fresh_down, fresh_down_first, fresh_down_second = coded_adam(
        tables_in, [down_adapters, down_first_moment, down_second_moment], down_returned,
        [projected],
    )
    projected = finish(
        mine_is_own, down_wide, up_cat, row_count, half_rows, half_rows, terms_b, projected,
        [fresh_down],
    )
    return (
        projected,
        flip(fresh_down),
        flip(fresh_up),
        flip(fresh_down_first),
        flip(fresh_up_first),
        flip(fresh_down_second),
        flip(fresh_up_second),
    )


def solution(mesh):
    placed = (
        P(("groups", "dp", "sub"), "tensor"),
        P("tensor", "sub"),
        P(("groups", "dp", "sub"), "tensor"),
        P(("groups", "dp"), ("tensor", "sub"), None),
        P(("groups", "dp"), ("tensor", "sub"), None),
        P(("groups", "dp"), ("tensor", "sub"), None),
        P(("groups", "dp"), ("tensor", "sub"), None),
        P(("groups", "dp"), ("tensor", "sub"), None),
        P(("groups", "dp"), ("tensor", "sub"), None),
        P(("groups", "dp")),
        P("groups"),
        P("groups"),
    )
    return jax.shard_map(
        on_device,
        mesh=mesh,
        in_specs=placed,
        out_specs=(
            P(("groups", "dp", "sub"), "tensor"),
            P(("groups", "dp"), ("tensor", "sub"), None),
            P(("groups", "dp"), ("tensor", "sub"), None),
            P(("groups", "dp"), ("tensor", "sub"), None),
            P(("groups", "dp"), ("tensor", "sub"), None),
            P(("groups", "dp"), ("tensor", "sub"), None),
            P(("groups", "dp"), ("tensor", "sub"), None),
        ),
        check_vma=False,
    )
```

```python
import functools

import jax
import jax.numpy as jnp
from jax import lax
from jax.experimental import pallas as pl
from jax.experimental.pallas import tpu as pltpu
from jax.sharding import PartitionSpec as P

BLK_ROWS = 128


ADAPTER_SCALE = 2.0
BETA_ONE = 0.9
BETA_TWO = 0.999
LEARN_RATE = 0.01
ADAM_EPS = 1e-08

SMEM = pl.BlockSpec(memory_space=pltpu.SMEM)
VMEM_BYTES = 65_500_000
TOP_CODE = 32767.0
LEVELS = 64.0
LEVEL_LANES = 128
COST = 20.0


def params():
    return pltpu.CompilerParams(vmem_limit_bytes=VMEM_BYTES)


def cost(micros):
    flops = int(micros * 1_000_000_000 * COST)
    return pl.CostEstimate(flops=flops, bytes_accessed=1000, transcendentals=0)


def rotate(value, axis, shift):
    size = lax.axis_size(axis)
    return lax.ppermute(value, axis, [(i, (i + shift) % size) for i in range(size)])


ANY = pl.BlockSpec(memory_space=pl.ANY)


def behind(kernel, deps, scalars=0):
    return lambda *refs: kernel(*refs[:scalars], *refs[scalars + len(deps) :])


def tie_kernel(*refs):
    pass


def tie(values, deps):
    return pl.pallas_call(
        tie_kernel,
        in_specs=[ANY] * (len(values) + len(deps)),
        out_specs=[ANY] * len(values),
        out_shape=[dims(v) for v in values],
        input_output_aliases={k: k for k in range(len(values))},
        compiler_params=params(),
        cost_estimate=cost(100),
        name="tie",
    )(*values, *deps)


def dims(value):
    return jax.ShapeDtypeStruct(value.shape, value.dtype)


def tables_kernel(devices, cores, slots, block_count, slot_of, tenant_of, pick, owner_of, used, place):
    z, s = lax.axis_index("dp"), lax.axis_index("sub")
    place[0] = z
    place[1] = s
    for k in range(slots):
        used[k] = 0

    def slot_at(device, b):
        return slot_of[tenant_of[device * block_count + b]]

    def per_device(device, carry):
        def per_block(b, found):
            local = slot_at(device, b) - z * slots
            mine = jnp.logical_and(local >= 0, local < slots)

            @pl.when(mine)
            def _():
                used[local] = 1

            return jnp.where(mine, local, found)

        pick[device] = lax.fori_loop(0, block_count, per_block, 0)
        return carry

    lax.fori_loop(0, devices, per_device, 0)
    for b in range(block_count):
        owner_of[b] = lax.div(slot_at(z * cores + s, b), slots)


def pack_kernel(devices, pick, own, out):
    for device in range(devices):
        out[device] = own[pick[device]].astype(jnp.bfloat16)


def pack_wide_kernel(owners, cores, place, pick, own, other, *outs):
    z, s = place[0], place[1]
    half = own.shape[2]
    for d in range(owners):
        k = pick[lax.rem(z + d, owners) * cores + s]
        near, far = own[k].astype(jnp.bfloat16), other[k].astype(jnp.bfloat16)
        outs[d][:, :half] = jnp.where(s == 0, near, far)
        outs[d][:, half:] = jnp.where(s == 0, far, near)


def product_kernel(owners, cores, rank, tile_rows, owner_of, *refs):
    halves, (rows, out) = refs[:cores], refs[cores:]
    step = pl.program_id(0)
    half = halves[0].shape[-1]
    full = 0.0
    for h in range(cores):
        full = full + lax.dot_general(
            halves[h][...].reshape(owners * rank, half),
            rows[:, h * half : (h + 1) * half],
            (((1,), (1,)), ((), ())),
            preferred_element_type=jnp.float32,
        )
    for b in range(tile_rows // BLK_ROWS):
        owner = owner_of[step * (tile_rows // BLK_ROWS) + b]
        span = slice(b * BLK_ROWS, (b + 1) * BLK_ROWS)
        value = full[:rank, span]
        for d in range(1, owners):
            value = jnp.where(owner == d, full[d * rank : (d + 1) * rank, span], value)
        out[:, span] = value


def steps_product_kernel(owners, rank, tile_rows, place, owner_of, *refs):
    parts, (rows, out, cat) = refs[:owners], refs[owners:]
    step = pl.program_id(0)

    @pl.when(step == 0)
    def _():
        for d in range(owners):
            owner = lax.rem(place[0] - d + owners, owners)
            cat[pl.ds(pl.multiple_of(owner * rank, rank), rank), :] = parts[d][...]

    full = lax.dot_general(
        cat[...], rows[...], (((1,), (1,)), ((), ())), preferred_element_type=jnp.float32
    )
    for b in range(tile_rows // BLK_ROWS):
        owner = owner_of[step * (tile_rows // BLK_ROWS) + b]
        span = slice(b * BLK_ROWS, (b + 1) * BLK_ROWS)
        value = full[:rank, span]
        for d in range(1, owners):
            value = jnp.where(owner == d, full[d * rank : (d + 1) * rank, span], value)
        out[:, span] = value


def steps_product(place, owner_of, parts, rows, deps):
    owners, (rank, features), row_count = len(parts), parts[0].shape, rows.shape[0]
    tile = min(256, row_count)
    return pl.pallas_call(
        behind(functools.partial(steps_product_kernel, owners, rank, tile), deps),
        grid=(row_count // tile,),
        in_specs=[ANY] * len(deps)
        + [SMEM] * 2
        + [pl.BlockSpec((rank, features), lambda i: (0, 0))] * owners
        + [pl.BlockSpec((tile, features), lambda i: (i, 0))],
        out_specs=[
            pl.BlockSpec((rank, tile), lambda i: (0, i)),
            pl.BlockSpec((owners * rank, features), lambda i: (0, 0)),
        ],
        out_shape=[
            jax.ShapeDtypeStruct((rank, row_count), jnp.float32),
            jax.ShapeDtypeStruct((owners * rank, features), jnp.bfloat16),
        ],
        compiler_params=params(),
        cost_estimate=cost(5),
        name="steps_product",
    )(*deps, place, owner_of, *parts, rows)


def halves_specs(owners, cores, rank, half):
    return [
        pl.BlockSpec((owners, None, rank, half), lambda *ids, h=h: (0, h, 0, 0))
        for h in range(cores)
    ]


def adapter_product(owner_of, adapters, rows, deps):
    (owners, cores, rank, half), (row_count, features) = adapters.shape, rows.shape
    tile = min(256, row_count)
    return pl.pallas_call(
        behind(functools.partial(product_kernel, owners, cores, rank, tile), deps),
        grid=(row_count // tile,),
        in_specs=[ANY] * len(deps)
        + [SMEM]
        + halves_specs(owners, cores, rank, half)
        + [pl.BlockSpec((tile, features), lambda i: (i, 0))],
        out_specs=pl.BlockSpec((rank, tile), lambda i: (0, i)),
        out_shape=jax.ShapeDtypeStruct((rank, row_count), jnp.float32),
        compiler_params=params(),
        cost_estimate=cost(5),
        name="adapter_product",
    )(*deps, owner_of, *[adapters] * cores, rows)


def encode(product, kind):
    if kind != jnp.int16:
        return product.astype(kind)
    top = jnp.maximum(jnp.max(jnp.abs(product), axis=1, keepdims=True), 1e-30)
    level = jnp.floor(jnp.log2(top) * LEVELS) + 2.0
    coded = jnp.round(product * (TOP_CODE * jnp.exp2(level * (-1.0 / LEVELS))))
    coded = jnp.clip(coded, -TOP_CODE, TOP_CODE).astype(jnp.int32).astype(jnp.int16)
    lanes = jnp.broadcast_to(level, (product.shape[0], LEVEL_LANES))
    return jnp.concatenate([coded, lanes.astype(jnp.int32).astype(jnp.int16)], axis=1)


def spread_rows(owners, rank, scale_in, owner_of, sums, wide):
    @pl.when(pl.program_id(0) == 0)
    def _():
        total = sums[0][...]
        for term in sums[1:]:
            total = total + term[...]
        value = (scale_in * total).astype(jnp.bfloat16)
        for b in range(value.shape[1] // BLK_ROWS):
            span = slice(b * BLK_ROWS, (b + 1) * BLK_ROWS)
            for d in range(owners):
                kept = jnp.where(owner_of[b] == d, value[:, span], jnp.zeros_like(value[:, span]))
                wide[d * rank : (d + 1) * rank, span] = kept


def steps_gradient_kernel(owners, rank, terms, scale_in, scale_out, place, owner_of, *refs):
    sums, rows, outs = refs[:terms], refs[terms], refs[terms + 1 : terms + 1 + owners]
    wide, coded = refs[-2:]
    spread_rows(owners, rank, scale_in, owner_of, sums, wide)
    product = scale_out * jnp.dot(wide[...], rows[...], preferred_element_type=jnp.float32)
    coded[...] = product.astype(coded.dtype)
    for d in range(owners):
        owner = lax.rem(place[0] - d + owners, owners)
        outs[d][...] = coded[pl.ds(pl.multiple_of(owner * rank, rank), rank), :]


def steps_gradients(place, owner_of, sums, rows, owners, half, scale_in, scale_out, deps):
    rank, row_count = sums[0].shape
    whole = pl.BlockSpec((rank, row_count), lambda h, place, owner_of: (0, 0))
    return pl.pallas_call(
        behind(
            functools.partial(
                steps_gradient_kernel, owners, rank, len(sums), scale_in, scale_out
            ),
            deps,
            2,
        ),
        grid_spec=pltpu.PrefetchScalarGridSpec(
            num_scalar_prefetch=2,
            grid=(2,),
            in_specs=[ANY] * len(deps)
            + [whole] * len(sums)
            + [
                pl.BlockSpec(
                    (row_count, half),
                    lambda h, place, owner_of: (0, jnp.where(h == 0, place[1], 1 - place[1])),
                )
            ],
            out_specs=[pl.BlockSpec((None, rank, half), lambda h, place, owner_of: (h, 0, 0))]
            * owners
            + [pl.BlockSpec((owners * rank, row_count), lambda h, place, owner_of: (0, 0))],
            scratch_shapes=[pltpu.VMEM((owners * rank, half), jnp.bfloat16)],
        ),
        out_shape=[jax.ShapeDtypeStruct((2, rank, half), jnp.bfloat16)] * owners
        + [jax.ShapeDtypeStruct((owners * rank, row_count), jnp.bfloat16)],
        compiler_params=params(),
        cost_estimate=cost(4),
        name="steps_gradients",
    )(place, owner_of, *deps, *sums, rows)


def collect_kernel(owners, *refs):
    for d in range(owners):
        refs[-1][d] = refs[d][...]


def collect(messages, deps):
    owners, (_, rank, half) = len(messages), messages[0].shape
    return pl.pallas_call(
        behind(functools.partial(collect_kernel, owners), deps),
        grid=(1,),
        in_specs=[ANY] * len(deps) + [pl.BlockSpec((None, rank, half), lambda i: (1, 0, 0))] * owners,
        out_specs=pl.BlockSpec((owners, rank, half), lambda i: (0, 0, 0)),
        out_shape=jax.ShapeDtypeStruct((owners, rank, half), messages[0].dtype),
        compiler_params=params(),
        cost_estimate=cost(1),
        name="collect",
    )(*deps, *messages)


def gradient_kernel(owners, rank, terms, scale_in, scale_out, owner_of, *refs):
    sums, (rows, out, wide) = refs[:terms], refs[terms:]
    spread_rows(owners, rank, scale_in, owner_of, sums, wide)
    product = scale_out * jnp.dot(wide[...], rows[...], preferred_element_type=jnp.float32)
    out[...] = encode(product, out.dtype).reshape(out.shape)


def gradients(owner_of, sums, rows, owners, half, scale_in, scale_out, kind, deps):
    rank, row_count = sums[0].shape
    cores = rows.shape[1] // half
    lanes = half + (LEVEL_LANES if kind == jnp.int16 else 0)
    whole = pl.BlockSpec((rank, row_count), lambda h: (0, 0))
    return pl.pallas_call(
        behind(
            functools.partial(gradient_kernel, owners, rank, len(sums), scale_in, scale_out), deps
        ),
        grid=(cores,),
        in_specs=[ANY] * len(deps)
        + [SMEM]
        + [whole] * len(sums)
        + [pl.BlockSpec((row_count, half), lambda h: (0, h))],
        out_specs=[
            pl.BlockSpec((owners, None, rank, lanes), lambda h: (0, h, 0, 0)),
            pl.BlockSpec((owners * rank, row_count), lambda h: (0, 0)),
        ],
        out_shape=[
            jax.ShapeDtypeStruct((owners, cores, rank, lanes), kind),
            jax.ShapeDtypeStruct((owners * rank, row_count), jnp.bfloat16),
        ],
        compiler_params=params(),
        cost_estimate=cost(4),
        name="gradients",
    )(*deps, owner_of, *sums, rows)


def share_kernel(spans, rows, weight, *outs):
    product = jnp.dot(rows[...], weight[...], preferred_element_type=jnp.float32)
    for out, (start, count) in zip(outs, spans):
        out[...] = product[start : start + count, :].astype(out.dtype)


def share(tokens, weight, piece, start, total, spans, width, deps):
    features = tokens.shape[1]
    tile = min(512, width)
    tiles = width // tile
    return pl.pallas_call(
        behind(functools.partial(share_kernel, spans), deps),
        grid=(tiles,),
        in_specs=[ANY] * len(deps)
        + [
            pl.BlockSpec((total, features), lambda j: (start // total, 0)),
            pl.BlockSpec((features, tile), lambda j: (0, piece * tiles + j)),
        ],
        out_specs=[pl.BlockSpec((count, tile), lambda j: (0, j)) for _, count in spans],
        out_shape=[jax.ShapeDtypeStruct((count, width), jnp.bfloat16) for _, count in spans],
        compiler_params=params(),
        cost_estimate=cost(4.0 * total / 256),
        name="share",
    )(*deps, tokens, weight)


def finish_kernel(steps, flags, spans, mine_is_own, wide, adapters, *refs):
    arrays, out = refs[: len(flags)], refs[-1]
    step = pl.program_id(0)
    turned = wide[...].T
    half = adapters.shape[1] // 2

    def run(kind):
        for h in range(2):
            span = slice(h * half, (h + 1) * half)
            total = ADAPTER_SCALE * jnp.dot(
                turned, adapters[:, span], preferred_element_type=jnp.float32
            )
            for array, flag, (first, last) in zip(arrays, flags, spans):
                if flag == kind:
                    value = array[:, span].astype(jnp.float32)
                    if last - first < steps:
                        active = jnp.logical_and(step >= first, step < last)
                        value = jnp.where(active, value, 0.0)
                    total = total + value
            out[:, span] = total.astype(out.dtype)

    for kind in (0, 1):
        pl.when(mine_is_own[0] == kind)(functools.partial(run, kind))


def finish(mine_is_own, wide, adapters, row_count, start, count, terms, previous, deps):
    stacked, width = adapters.shape
    tile = min(256, count)
    first = start // tile
    specs, spans = [], []
    for array, row, flag in terms:
        low, many = (row - start) // tile, array.shape[0] // tile

        def block_of(i, mine, low=low, many=many, flag=flag):
            return (jnp.where(mine[0] == flag, jnp.clip(i - low, 0, many - 1), 0), 0)

        specs.append(pl.BlockSpec((tile, width), block_of))
        spans.append((low, low + many))
    operands = [mine_is_own, *deps, wide, adapters]
    operands += [t[0] for t in terms]
    in_specs = (
        [ANY] * len(deps)
        + [
            pl.BlockSpec((stacked, tile), lambda i, mine: (0, first + i)),
            pl.BlockSpec((stacked, width), lambda i, mine: (0, 0)),
        ]
        + specs
    )
    aliases = {}
    if previous is not None:
        aliases = {len(operands): 0}
        operands.append(previous)
        in_specs.append(ANY)
    return pl.pallas_call(
        behind(functools.partial(finish_kernel, count // tile, [t[2] for t in terms], spans), deps, 1),
        grid_spec=pltpu.PrefetchScalarGridSpec(
            num_scalar_prefetch=1,
            grid=(count // tile,),
            in_specs=in_specs,
            out_specs=pl.BlockSpec((tile, width), lambda i, mine: (first + i, 0)),
        ),
        out_shape=jax.ShapeDtypeStruct((row_count, width), jnp.bfloat16),
        input_output_aliases=aliases,
        compiler_params=params(),
        cost_estimate=cost(4),
        name="finish",
    )(*operands)


def adam_step(slots, used, corr, param, first, second, new_param, new_first, new_second, grads):
    for k in range(slots):
        grad = grads[k]
        one = BETA_ONE * first[k] + (1.0 - BETA_ONE) * grad
        two = BETA_TWO * second[k] + (1.0 - BETA_TWO) * grad * grad
        update = LEARN_RATE * (one / corr[k]) / (jnp.sqrt(two / corr[slots + k]) + ADAM_EPS)
        keep = used[k] == 1
        new_param[k] = jnp.where(keep, param[k] - update, param[k])
        new_first[k] = jnp.where(keep, one, first[k])
        new_second[k] = jnp.where(keep, two, second[k])


def coded_adam_kernel(devices, slots, place, pick, used, corr, param, first, second, *refs):
    messages, levels = refs[:2]
    grads = refs[-1]
    grads[...] = jnp.zeros_like(grads)
    for device in range(devices):
        k = pick[device]
        level = levels[device].astype(jnp.float32)[:, :1]
        scale = jnp.exp2(level * (1.0 / LEVELS)) * (1.0 / TOP_CODE)
        grads[k] = grads[k] + messages[device].astype(jnp.float32) * scale
    adam_step(slots, used, corr, param, first, second, *refs[-4:])


def steps_adam_kernel(owners, slots, place, pick, used, corr, param, first, second, *refs):
    near, far, grads = refs[:owners], refs[owners], refs[-1]
    grads[...] = jnp.zeros_like(grads)
    for d in range(owners):
        device = lax.rem(place[0] + d, owners) * 2
        k = pick[device + place[1]]
        grads[k] = grads[k] + near[d][...].astype(jnp.float32)
        k = pick[device + 1 - place[1]]
        grads[k] = grads[k] + far[d].astype(jnp.float32)
    adam_step(slots, used, corr, param, first, second, *refs[-4:])


def adam(kernel, tables, states, messages, message_specs, deps):
    slots, rank, half = states[0].shape
    tile = feature_tile(half)
    state = pl.BlockSpec((slots, rank, tile), lambda i: (0, 0, i))
    return pl.pallas_call(
        behind(kernel, deps),
        grid=(half // tile,),
        in_specs=[ANY] * len(deps) + [SMEM] * len(tables) + [state] * 3 + message_specs,
        out_specs=[state] * 3,
        out_shape=[dims(states[0])] * 3,
        scratch_shapes=[pltpu.VMEM((slots, rank, tile), jnp.float32)],
        compiler_params=params(),
        cost_estimate=cost(4),
        name="adam",
    )(*deps, *tables, *states, *messages)


def feature_tile(half):
    return min(512, half)


def coded_adam(tables, states, messages, deps):
    devices, rank, _ = messages.shape
    slots, _, half = states[0].shape
    specs = [
        pl.BlockSpec((devices, rank, feature_tile(half)), lambda i: (0, 0, i)),
        pl.BlockSpec((devices, rank, LEVEL_LANES), lambda i: (0, 0, half // LEVEL_LANES)),
    ]
    kernel = functools.partial(coded_adam_kernel, devices, slots)
    return adam(kernel, tables, states, [messages] * 2, specs, deps)


def steps_adam(tables, states, near, far, deps):
    owners, rank, half = far.shape
    tile = feature_tile(half)
    specs = [pl.BlockSpec((None, rank, tile), lambda i: (0, 0, i))] * owners
    specs.append(pl.BlockSpec((owners, rank, tile), lambda i: (0, 0, i)))
    kernel = functools.partial(steps_adam_kernel, owners, states[0].shape[0])
    return adam(kernel, tables, states, [*near, far], specs, deps)


def on_device(
    tokens,
    frozen_weight,
    cotangent,
    down_adapters,
    up_adapters,
    down_first_moment,
    up_first_moment,
    down_second_moment,
    up_second_moment,
    optimizer_steps,
    slot_of_tenant,
    tenant_of_block,
):
    row_count, din_local = tokens.shape
    width = cotangent.shape[1]
    block_count = row_count // BLK_ROWS
    owners = lax.axis_size("dp")
    cores = lax.axis_size("sub")
    columns = lax.axis_size("tensor")
    s = lax.axis_index("sub")
    x = lax.axis_index("tensor")
    slots, half, rank = down_adapters.shape
    flip = lambda v: jnp.swapaxes(v, 1, 2)
    down_adapters, up_adapters = flip(down_adapters), flip(up_adapters)
    down_first_moment, up_first_moment = flip(down_first_moment), flip(up_first_moment)
    down_second_moment, up_second_moment = flip(down_second_moment), flip(up_second_moment)
    per_half = columns // cores

    devices = owners * cores

    pick, owner_of, used, place = pl.pallas_call(
        functools.partial(tables_kernel, devices, cores, slots, block_count),
        in_specs=[SMEM] * 2,
        out_specs=[SMEM] * 4,
        out_shape=[
            jax.ShapeDtypeStruct((devices,), jnp.int32),
            jax.ShapeDtypeStruct((block_count,), jnp.int32),
            jax.ShapeDtypeStruct((slots,), jnp.int32),
            jax.ShapeDtypeStruct((2,), jnp.int32),
        ],
        compiler_params=params(),
        cost_estimate=cost(2),
        name="tables",
    )(slot_of_tenant, tenant_of_block)
    steps = (optimizer_steps + 1).astype(jnp.float32)
    corr = jnp.concatenate(
        [
            1.0 - jnp.power(jnp.float32(BETA_ONE), steps),
            1.0 - jnp.power(jnp.float32(BETA_TWO), steps),
        ]
    )

    def pack(own):
        return pl.pallas_call(
            functools.partial(pack_kernel, devices),
            in_specs=[SMEM, pl.BlockSpec(memory_space=pltpu.VMEM)],
            out_specs=pl.BlockSpec(memory_space=pltpu.VMEM),
            out_shape=jax.ShapeDtypeStruct((devices, rank, half), jnp.bfloat16),
            compiler_params=params(),
            cost_estimate=cost(1),
            name="pack",
        )(pick, own)

    def spread_out(messages):
        flat = messages.reshape((devices,) + messages.shape[-2:])
        return lax.all_to_all(flat, ("dp", "sub"), split_axis=0, concat_axis=0, tiled=True)

    def by_owner(arrived):
        return arrived.reshape(owners, cores, rank, half)

    def pack_wide(own, other, deps):
        return pl.pallas_call(
            behind(functools.partial(pack_wide_kernel, owners, cores), deps),
            in_specs=[ANY] * len(deps)
            + [SMEM] * 2
            + [pl.BlockSpec(memory_space=pltpu.VMEM)] * 2,
            out_specs=[pl.BlockSpec(memory_space=pltpu.VMEM)] * owners,
            out_shape=[jax.ShapeDtypeStruct((rank, cores * half), jnp.bfloat16)] * owners,
            compiler_params=params(),
            cost_estimate=cost(1),
            name="pack_wide",
        )(*deps, place, pick, own, other)

    def along(messages, sign):
        return [m if d == 0 else rotate(m, "dp", sign * d) for d, m in enumerate(messages)]

    def shares(rows, start, total, spans, deps):
        pieces = []
        for piece in range(per_half):
            pieces.append(share(rows, frozen_weight, piece, start, total, spans, width, deps))
            deps = [pieces[-1][0]]
        return [list(chunk) for chunk in zip(*pieces)]

    def piece_for(chunk, target):
        if per_half == 1:
            return chunk[0]
        out = chunk[0]
        for piece in range(1, per_half):
            out = jnp.where(lax.rem(target, per_half) == piece, chunk[piece], out)
        return out

    def send(chunk, cross):
        got = []
        for step in range(1, columns):
            pairs = []
            for t in range(columns):
                for c in range(cores):
                    target = (t + step) % columns
                    if target // per_half == c:
                        pairs.append((t * cores + c, target * cores + (c + cross) % cores))
            operand = piece_for(chunk, lax.rem(x + step, columns))
            got.append(lax.ppermute(operand, ("tensor", "sub"), pairs))
        return got

    def send_local(chunk):
        pairs = []
        for t in range(columns):
            c = t // per_half
            pairs.append((t * cores + c, t * cores + (c + 1) % cores))
        return lax.ppermute(piece_for(chunk, x), ("tensor", "sub"), pairs)

    def exchange(part):
        return [part] + [rotate(part, "tensor", step) for step in range(1, columns)]

    half_rows = row_count // 2
    one_half = [(0, half_rows)]
    both = one_half * 2
    up_other = rotate(up_adapters, "sub", 1)
    other_tokens = rotate(tokens, "sub", 1)
    down_packed = pack(down_adapters)
    down_arrived = by_owner(spread_out(down_packed))
    own_a, = shares(tokens, 0, half_rows, one_half, [down_packed])
    got_a = send(own_a, 0)
    up_packed = pack_wide(up_adapters, up_other, [own_a[-1]])
    own_b, = shares(tokens, half_rows, half_rows, one_half, [up_packed[0]])
    down_part = adapter_product(owner_of, down_arrived, tokens, [own_b[-1], other_tokens])
    down_sums = exchange(down_part)
    up_packed = tie(up_packed, [down_part])
    up_parts = along(up_packed, 1)
    own_b = tie(own_b, [up_packed[0]] + got_a)
    got_b = send(own_b, 0)
    cross_a, cross_a_near = shares(other_tokens, 0, half_rows, both, [own_b[-1]])
    *up_messages, down_wide = steps_gradients(
        place, owner_of, down_sums, cotangent, owners, half, 1.0, ADAPTER_SCALE, [cross_a[-1]]
    )
    up_messages = tie(up_messages, up_parts[1:])
    up_returned = along(up_messages, -1)
    back_part, up_cat = steps_product(place, owner_of, up_parts, cotangent, [up_messages[0]])
    back_sums = exchange(back_part)
    cross_a = tie(cross_a, [back_part] + got_b)
    late_a = send(cross_a, 1)
    down_messages, back_wide = gradients(
        owner_of, back_sums, tokens, owners, half, ADAPTER_SCALE, 1.0, jnp.int16, [cross_a[-1]]
    )
    down_returned = spread_out(down_messages)
    cross_b, cross_b_near = shares(other_tokens, half_rows, half_rows, both, [down_messages])
    late_b = send(cross_b, 1)
    collected = collect(up_returned, late_a + [cross_b[-1]])
    up_far = rotate(collected, "sub", 1)
    cross_a_near = tie(cross_a_near, [collected])
    local_a = send_local(cross_a_near)
    cross_b_near = tie(cross_b_near, [local_a])
    local_b = send_local(cross_b_near)

    tables_in = [place, pick, used, corr]
    fresh_up, fresh_up_first, fresh_up_second = steps_adam(
        tables_in, [up_adapters, up_first_moment, up_second_moment], up_returned, up_far,
        [cross_a_near[-1]],
    )
    mine_is_own = (lax.div(x, per_half) == s).astype(jnp.int32).reshape(1)
    terms_a = [(piece_for(own_a, x), 0, 1), (local_a, 0, 0)]
    terms_a += [(g, 0, 1) for g in got_a] + [(g, 0, 0) for g in late_a]
    terms_b = [(piece_for(own_b, x), half_rows, 1), (local_b, half_rows, 0)]
    terms_b += [(g, half_rows, 1) for g in got_b] + [(g, half_rows, 0) for g in late_b]
    projected = finish(
        mine_is_own, down_wide, up_cat, row_count, 0, half_rows, terms_a, None, [fresh_up]
    )
    fresh_down, fresh_down_first, fresh_down_second = coded_adam(
        tables_in, [down_adapters, down_first_moment, down_second_moment], down_returned,
        [projected],
    )
    projected = finish(
        mine_is_own, down_wide, up_cat, row_count, half_rows, half_rows, terms_b, projected,
        [fresh_down],
    )
    return (
        projected,
        flip(fresh_down),
        flip(fresh_up),
        flip(fresh_down_first),
        flip(fresh_up_first),
        flip(fresh_down_second),
        flip(fresh_up_second),
    )


def solution(mesh):
    placed = (
        P(("groups", "dp", "sub"), "tensor"),
        P("tensor", "sub"),
        P(("groups", "dp", "sub"), "tensor"),
        P(("groups", "dp"), ("tensor", "sub"), None),
        P(("groups", "dp"), ("tensor", "sub"), None),
        P(("groups", "dp"), ("tensor", "sub"), None),
        P(("groups", "dp"), ("tensor", "sub"), None),
        P(("groups", "dp"), ("tensor", "sub"), None),
        P(("groups", "dp"), ("tensor", "sub"), None),
        P(("groups", "dp")),
        P("groups"),
        P("groups"),
    )
    return jax.shard_map(
        on_device,
        mesh=mesh,
        in_specs=placed,
        out_specs=(
            P(("groups", "dp", "sub"), "tensor"),
            P(("groups", "dp"), ("tensor", "sub"), None),
            P(("groups", "dp"), ("tensor", "sub"), None),
            P(("groups", "dp"), ("tensor", "sub"), None),
            P(("groups", "dp"), ("tensor", "sub"), None),
            P(("groups", "dp"), ("tensor", "sub"), None),
            P(("groups", "dp"), ("tensor", "sub"), None),
        ),
        check_vma=False,
    )
```
